512 devices in a mesh: sub: 64 (over z, x, core), coarse: 8 (over y).
Axes of the slice: x: 4, y: 8, z: 8, core: 2. Of those that a mesh axis runs over, the one named last changes fastest.
Arguments:
- load: bfloat16 [512, 512, 128], P(('sub', 'coarse')), may hold values from -18 to 18
- schur: bfloat16 [512, 512, 512], P(('sub', 'coarse')), as said below
- coupling: bfloat16 [512, 24, 512], P(('sub', 'coarse')), may hold values from -0.5 to 0.5
- coarse_inverse: bfloat16 [16384, 16384], P('coarse', 'sub'), as said below
- neighbour_sub: int32 [512, 8], P(('sub', 'coarse')), may hold values from 0 to 511, as said below
- neighbour_edge: int32 [512, 8], P(('sub', 'coarse')), may hold values from 0 to 7, as said below
- primal_owner: int32 [512, 24, 1], P(('sub', 'coarse')), may hold values from 0 to 63; in each aligned block of 24 rows (0 to 23, 24 to 47, ..., all dimensions but the last counted through in order) at most 2 rows name the same one
- primal_offset: int32 [512, 24], P(('sub', 'coarse')), may hold values from 0 to 255
Outputs:
- multipliers: float32 [512, 512, 128], P(('sub', 'coarse'))
The draws below stay inside these ranges and needn't reach their ends.
Inputs may be any that keep to these rules, and one draw needn't show every extreme that they name: `neighbour_sub`: each edge faces exactly one edge of a subdomain, and that edge faces it back. The subdomain across lies on the same index of coarse and on the same index of sub or the one before or after it, cyclically. On every device exactly 8 edges face a subdomain of another device, half of them on each side. `neighbour_edge`: the number of the facing edge at the subdomain across. `primal_owner`: among the primal dofs of the subdomains of one device, no owner is named more than 2 times; in every draw some owner is named exactly 2 times by some device. `schur`: each matrix is symmetric positive definite. `coarse_inverse`: symmetric positive definite once its rows are put in the order of its columns as the steps state.
All inputs are finite; a program needn't handle non-finite values.
Results may differ from the reference program's by a relative error of at most 0.0003.
The reference program's roundings to bfloat16 on the way count: a program that leaves them out, or rounds other values in their place, can miss the bound.
Values may be sent and summed in bfloat16 or wider, within the bound.
No kernel may reach another device: no remote copies, remote signals or barrier semaphores. Data moves between devices by JAX's collectives and lax.ppermute only.
A program may use at most 64 MiB of HBM per device.

```python
import math
import jax
import jax.numpy as jnp
import numpy as np
from jax import lax

SUB_DEV = 1
ND = 512
E = 8
NP = 24
NRHS = 128
CB = 256
ITERS = 2
CAPR = 8
EW = 64
NSUB = 512
NC = 16384
RB = 32
CAPC = 2
N_SUB = 64
N_COARSE = 8


def edge_pairs(key):
    devices_all = NSUB // SUB_DEV
    slots = SUB_DEV * E
    half = CAPR // 2
    keys = jax.random.split(key, devices_all)
    orders = jax.vmap(lambda k: jax.random.permutation(k, slots))(keys).astype(jnp.int32)
    places = jnp.arange(slots, dtype=jnp.int32)[None, :]
    device_ids = jnp.arange(devices_all, dtype=jnp.int32)
    sub_place = device_ids // N_COARSE
    coarse_place = device_ids % N_COARSE
    after = (sub_place + 1) % N_SUB * N_COARSE + coarse_place
    before = (sub_place + N_SUB - 1) % N_SUB * N_COARSE + coarse_place
    partner_dev = jnp.where(places < half, after[:, None], jnp.where(places < 2 * half, before[:, None], device_ids[:, None]))
    partner_place = jnp.where(places < half, places + half, jnp.where(places < 2 * half, places - half, 2 * half + (places - 2 * half ^ 1)))
    partner_slot = orders[partner_dev, partner_place]
    global_ids = partner_dev * slots + partner_slot
    inverse = jnp.argsort(orders, axis=1, stable=True)
    by_slot = jnp.take_along_axis(global_ids, inverse, axis=1)
    return by_slot.reshape(NSUB, E).astype(jnp.int32)


def draw_neighbour_sub(key, part):
    paired = edge_pairs(key)
    return paired // E


def draw_neighbour_edge(key, part):
    paired = edge_pairs(key)
    return paired % E


def draw_load(key, part):
    key = jax.random.fold_in(key, 31)
    place = jnp.arange(NSUB, dtype=jnp.float32) / float(max(NSUB - 1, 1))
    amplitude = jnp.exp(place * math.log(3.0))
    values = jnp.clip(jax.random.normal(key, (NSUB, ND, NRHS), jnp.float32), -6.0, 6.0)
    return (values * amplitude[:, None, None]).astype(jnp.bfloat16)


def draw_schur(key, part):
    key = jax.random.fold_in(key, 11)
    keys = jax.random.split(key, NSUB)
    eye = jnp.eye(ND, dtype=jnp.float32)

    def single(k):
        k_off, k_diag = jax.random.split(k)
        noise = jax.random.normal(k_off, (ND, ND), jnp.float32)
        sym = (noise + noise.T) * (0.25 / math.sqrt(ND))
        diag = jnp.exp(jax.random.uniform(k_diag, (ND,), jnp.float32, 0.0, math.log(4.0)))
        return (sym * (1.0 - eye) + eye * diag[:, None]).astype(jnp.bfloat16)
    return jax.lax.map(single, keys)


def draw_coarse_inverse(key, part):
    key = jax.random.fold_in(key, 23)
    k_off, k_diag = jax.random.split(key)
    noise = jax.random.normal(k_off, (NC, NC), jnp.float32)
    sym = (noise + noise.T) * (0.25 / math.sqrt(NC))
    diag = jnp.exp(jax.random.uniform(k_diag, (NC,), jnp.float32, math.log(1.2), math.log(3.0)))
    rows = jnp.arange(NC)
    on_diag = rows[:, None] == rows[None, :]
    matrix = jnp.where(on_diag, diag[:, None], sym).astype(jnp.bfloat16)
    return matrix.reshape(NC // CB, CB // RB, RB, NC).transpose(1, 0, 2, 3).reshape(NC, NC)


def with_ends(drawn, own_key, low, high):
    index_at = [jax.random.randint(jax.random.fold_in(own_key, axis), (), 0, length) for axis, length in enumerate(drawn.shape)]
    main_axis = drawn.shape.index(max(drawn.shape))
    beside = index_at[:main_axis] + [(index_at[main_axis] + 1) % drawn.shape[main_axis]] + index_at[main_axis + 1:]
    return drawn.at[tuple(index_at)].set(low).at[tuple(beside)].set(high)


def steps_of(stream_key, extent, pieces, least, high):
    def one(dim, blocks):
        heights = jax.random.uniform(jax.random.fold_in(jax.random.fold_in(stream_key, 6), dim), (blocks,), jnp.float32, least / len(pieces), high / len(pieces))
        return jnp.repeat(jnp.exp(heights), extent[dim] // blocks).reshape((-1,) + (1,) * (len(extent) - dim - 1))

    gain = one(*pieces[0])
    for cut in pieces[1:]:
        gain = gain * one(*cut)
    return gain


def routed_block(rng, own, number, rows, count, top, most, skew):
    sequence = jax.random.permutation(rng, count)
    crowded, ordinary = portions_of(count, rows * top, most, skew, True), portions_of(count, rows * top, most, skew, False)
    places = jnp.arange(count)

    def named(sizes, offset_by):
        used = int((sizes > 0).sum())
        fixed = max(1, used // 4)
        shifted = fixed + (places - fixed + offset_by * (used - fixed)) % max(1, count - fixed)
        return jnp.zeros((count,), jnp.int32).at[sequence[jnp.where(places < fixed, places, shifted)]].set(jnp.asarray(sizes, jnp.int32))

    sizes = jnp.where(number % 4 == 0, named(crowded, number // 4), named(ordinary, number - number // 4 - 1))
    mixed = jax.random.permutation(jax.random.fold_in(own, 3), count)
    giver, taker = mixed[0:count // 2 * 2:2], mixed[1:count // 2 * 2:2]
    room = jnp.minimum(sizes[giver] - 1, most - sizes[taker]) // 2
    room = jnp.where((giver == sequence[0]) | (taker == sequence[0]) | (sizes[taker] == 0), 0, jnp.maximum(room, 0))
    shifted = jax.random.randint(jax.random.fold_in(own, 4), (count // 2,), 0, 1 << 20) % (room + 1)
    sizes = sizes.at[giver].add(-shifted).at[taker].add(shifted)
    items = jnp.searchsorted(jnp.cumsum(sizes), jnp.arange(rows * top), side="right").astype(jnp.int32)
    grid = items.reshape(top, rows).T
    grid = grid[jax.random.permutation(jax.random.fold_in(own, 1), rows)]
    offset_by = jax.random.randint(jax.random.fold_in(own, 2), (rows, 1), 0, top)
    return jnp.take_along_axis(grid, (jnp.arange(top)[None, :] + offset_by) % top, axis=1)


def portions_of(count, total, reach, lean, full):
    loads = [(1 << 20) // math.isqrt(grade ** lean) + 1 for grade in range(1, count + 1)]
    largest = reach if full else min(reach, max(-(-total // count), total * loads[0] // sum(loads)))
    least = 1 if total - largest >= count - 1 else 0
    given, spare = [largest] + [least] * (count - 1), total - largest - least * (count - 1)
    while spare > 0:
        candidates = [i for i in range(1, count) if given[i] < largest] or [i for i in range(1, count) if given[i] < reach]
        whole, budget = sum([loads[i] for i in candidates]), spare
        for i in candidates:
            addition = min(reach - given[i], max(1, budget * loads[i] // whole), spare)
            given[i] = given[i] + addition
            spare = spare - addition
    return np.array(given)


def scatter_about(stream_key, extent, deviation, reach, shards=(), kind=jnp.bfloat16):
    drawn = deviation * jax.random.normal(stream_key, extent, jnp.float32)
    if shards:
        drawn = drawn * steps_of(stream_key, extent, shards, -0.22, 0.18)
    return jnp.clip(drawn, -reach, reach).astype(kind)


def setup_inputs(seed: int = 0) -> dict:
    splits = jax.random.split(jax.random.key(seed), 9)
    load = draw_load(jax.random.fold_in(splits[8], 71), 0)
    schur = draw_schur(jax.random.fold_in(splits[8], 71), 0)
    coupling = scatter_about(splits[2], (NSUB, NP, ND), (ND // 4) ** -0.5, 0.5, ((0, 512),))
    coarse_inverse = draw_coarse_inverse(jax.random.fold_in(splits[8], 71), 0)
    neighbour_sub = draw_neighbour_sub(jax.random.fold_in(splits[8], 71), 0)
    neighbour_edge = draw_neighbour_edge(jax.random.fold_in(splits[8], 71), 0)
    primal_owner_keys = jax.random.split(jax.random.fold_in(splits[6], 1), NSUB * NP // (SUB_DEV * NP))
    primal_owner_turns = jax.random.permutation(jax.random.fold_in(splits[6], 3), NSUB * NP // (SUB_DEV * NP))
    primal_owner = jax.vmap(lambda own, number: routed_block(jax.random.fold_in(splits[6], 2), own, number, SUB_DEV * NP, N_SUB, 1, CAPC, 2))(primal_owner_keys, primal_owner_turns).reshape((NSUB, NP, 1))
    primal_offset = with_ends(jax.random.randint(splits[7], (NSUB, NP), 0, CB), jax.random.fold_in(splits[7], 1), 0, CB - 1).astype(jnp.int32)
    return dict(load=load, schur=schur, coupling=coupling, coarse_inverse=coarse_inverse, neighbour_sub=neighbour_sub, neighbour_edge=neighbour_edge, primal_owner=primal_owner, primal_offset=primal_offset)


def jump(field, neighbour_sub, neighbour_edge):
    edges = field.reshape(NSUB * E, EW, NRHS)
    facing = edges[(neighbour_sub * E + neighbour_edge).reshape(-1).astype(jnp.int32)]
    return (edges - facing).reshape(NSUB, ND, NRHS)


def apply_schur(schur, jumps):
    def single(pair):
        return jnp.dot(pair[0], pair[1], preferred_element_type=jnp.float32)
    return lax.map(single, (schur, jumps))


def operator(field, schur, coupling, coarse_inverse, neighbour_sub, neighbour_edge, primal_owner, primal_offset):
    jumps = jump(field, neighbour_sub, neighbour_edge).astype(jnp.bfloat16)
    local = apply_schur(schur, jumps)
    terms = jnp.einsum("spn,snr->spr", coupling.astype(jnp.float32), jumps.astype(jnp.float32))
    index = (primal_owner[:, :, 0] * CB + primal_offset).reshape(-1).astype(jnp.int32)
    coarse_rhs = jnp.zeros((NC, NRHS), jnp.float32).at[index].add(terms.reshape(NSUB * NP, NRHS))
    coarse_rhs = coarse_rhs.astype(jnp.bfloat16)
    solved = jnp.dot(coarse_inverse, coarse_rhs, preferred_element_type=jnp.float32).astype(jnp.bfloat16)
    ordered = solved.reshape(N_COARSE, N_SUB, RB, NRHS).transpose(1, 0, 2, 3).reshape(NC, NRHS)
    values = ordered[index].reshape(NSUB, NP, NRHS)
    back = jnp.einsum("spn,spr->snr", coupling.astype(jnp.float32), values.astype(jnp.float32))
    return jump(local + back, neighbour_sub, neighbour_edge)


def reference(load, schur, coupling, coarse_inverse, neighbour_sub, neighbour_edge, primal_owner, primal_offset):
    residual = jump(load.astype(jnp.float32), neighbour_sub, neighbour_edge)
    direction = residual
    solution = jnp.zeros_like(residual)
    norm_now = jnp.sum(residual * residual, axis=(0, 1))
    for step in range(ITERS):
        image = operator(direction, schur, coupling, coarse_inverse, neighbour_sub, neighbour_edge, primal_owner, primal_offset)
        alpha = norm_now / jnp.sum(direction * image, axis=(0, 1))
        solution = solution + alpha * direction
        if step + 1 < ITERS:
            residual = residual - alpha * image
            norm_next = jnp.sum(residual * residual, axis=(0, 1))
            direction = residual + (norm_next / norm_now) * direction
            norm_now = norm_next
    return solution
```

```python
import jax
import jax.numpy as jnp
from jax import lax
from jax.sharding import PartitionSpec as P

HIGHEST = lax.Precision.HIGHEST
F32, BF16 = jnp.float32, jnp.bfloat16


def exchange(blocks, axis):
    return lax.all_to_all(blocks, axis, split_axis=0, concat_axis=0, tiled=True)


def in_three(value):
    high = lax.reduce_precision(value, 8, 7)
    rest = value - high
    middle = lax.reduce_precision(rest, 8, 7)
    return [part.astype(BF16) for part in (high, middle, rest - middle)]


def body(
    load,
    schur,
    coupling,
    coarse_inverse,
    neighbour_sub,
    neighbour_edge,
    primal_owner,
    primal_offset,
):
    _, order, cases = load.shape
    edges = neighbour_sub.shape[1]
    width = order // edges
    half = edges // 2
    rows, block = coarse_inverse.shape
    n_sub, n_coarse = lax.axis_size("sub"), lax.axis_size("coarse")
    piece = block // n_coarse
    capacity = 2
    slots = n_sub * capacity
    sub_index = lax.axis_index("sub")

    faces_next = (neighbour_sub[0] // n_coarse - sub_index) % n_sub == 1
    edge_at = neighbour_edge[0]
    same_side = faces_next[:, None] == faces_next[None, :]
    ids = jnp.arange(edges, dtype=jnp.int32)
    from_place = jnp.sum((same_side & (edge_at[None, :] < edge_at[:, None])).astype(jnp.int32), axis=1)
    from_place = from_place + jnp.where(faces_next, half, 0)
    to_place = jnp.sum((same_side & (ids[None, :] < ids[:, None])).astype(jnp.int32), axis=1)
    to_place = to_place + jnp.where(faces_next, 0, half)
    send_order = jnp.sum(jnp.where(to_place[None, :] == ids[:, None], ids[None, :], 0), axis=1)

    def facing(field):
        ordered = field.reshape(edges, width, cases)[send_order]
        from_before = lax.ppermute(ordered[:half], "sub", [(i, (i + 1) % n_sub) for i in range(n_sub)])
        from_next = lax.ppermute(ordered[half:], "sub", [((i + 1) % n_sub, i) for i in range(n_sub)])
        both = jnp.concatenate([from_before, from_next], axis=0)
        return both[from_place].reshape(order, cases)

    owners = primal_owner.reshape(-1)
    offsets = primal_offset.reshape(-1)
    prims = owners.shape[0]
    row_ids = jnp.arange(prims, dtype=jnp.int32)
    earlier = (owners[:, None] == owners[None, :]) & (row_ids[None, :] < row_ids[:, None])
    slot_of = owners * capacity + jnp.sum(earlier.astype(jnp.int32), axis=1)
    placed = jnp.arange(slots, dtype=jnp.int32)[:, None] == slot_of[None, :]
    slotted = jnp.dot(placed.astype(BF16), coupling[0], preferred_element_type=F32).astype(BF16)
    slot_offset = jnp.sum(jnp.where(placed, offsets[None, :] + 1, 0), axis=1) - 1
    inverse_t = coarse_inverse.T

    def forward(field, scalars, marks):
        twice = 2.0 * field
        jumps = twice.astype(BF16)
        rest = (twice - jumps.astype(F32)).astype(BF16)
        local = jnp.dot(schur[0], jumps, preferred_element_type=F32)
        terms = jnp.dot(slotted, jnp.concatenate([jumps, rest], axis=1), preferred_element_type=F32)
        rounded, left = terms[:, :cases], terms[:, cases:]
        near = jnp.sum(twice * local, axis=0)
        tail = jnp.stack([near] + scalars)
        parts = [
            rounded.reshape(n_sub, capacity, cases),
            (rounded + left).reshape(n_sub, capacity, cases),
            jnp.broadcast_to(tail[None], (n_sub,) + tail.shape),
        ]
        if marks is None:
            parts.append(
                jnp.broadcast_to(slot_offset.astype(F32).reshape(n_sub, capacity, 1), (n_sub, capacity, cases))
            )
        incoming = exchange(jnp.concatenate(parts, axis=1), "sub")
        if marks is None:
            named = incoming[:, -capacity:].reshape(slots, cases)
            lanes = lax.broadcasted_iota(jnp.int32, (slots, block), 1).astype(F32)
            marks = (jnp.tile(named, (1, block // cases)) == lanes).astype(F32)
        given = jnp.concatenate(
            [incoming[:, :capacity].reshape(slots, cases), incoming[:, capacity : 2 * capacity].reshape(slots, cases)],
            axis=1,
        )
        partial = lax.dot_general(marks, given, (((0,), (0,)), ((), ())), precision=HIGHEST)
        count = tail.shape[0]
        sums = jnp.sum(incoming[:, 2 * capacity : 2 * capacity + count], axis=0)
        out = jnp.concatenate(
            [
                partial[:, :cases].reshape(n_coarse, piece, cases),
                partial[:, cases:].reshape(n_coarse, piece, cases),
                jnp.broadcast_to(sums[None], (n_coarse, count, cases)),
            ],
            axis=1,
        )
        total = jnp.sum(exchange(out, "coarse"), axis=0)
        return local, marks, total[:piece].astype(BF16), total[piece : 2 * piece], total[2 * piece :]

    def coarse(rhs):
        everyone = exchange(jnp.broadcast_to(rhs[None], (n_sub,) + rhs.shape), "sub")
        product = jnp.dot(inverse_t, everyone.reshape(rows, cases), preferred_element_type=F32)
        return jnp.sum(exchange(product.reshape(n_coarse, piece, cases), "coarse"), axis=0).astype(BF16)

    start = load[0]
    residual = start.astype(F32) - facing(start).astype(F32)
    local, marks, rhs, weights, sums = forward(residual, [jnp.sum(residual * residual, axis=0)], None)
    near, norm_now = sums[0], sums[1]
    solved = coarse(rhs)
    far = jnp.sum(weights * solved.astype(F32), axis=0)
    mine = jnp.concatenate([solved, jnp.stack(in_three(far))], axis=0)
    owned = exchange(jnp.broadcast_to(mine[None], (n_coarse,) + mine.shape), "coarse")
    far = jnp.sum(owned[:, piece:].astype(F32), axis=(0, 1))
    answers = lax.dot_general(
        marks.astype(BF16), owned[:, :piece].reshape(block, cases), (((1,), (0,)), ((), ())), preferred_element_type=F32
    ).astype(BF16)
    outgoing = jnp.concatenate(
        [
            answers.reshape(n_sub, capacity, cases),
            jnp.broadcast_to(jnp.stack(in_three(far))[None], (n_sub, 3, cases)),
        ],
        axis=1,
    )
    replies = exchange(outgoing, "sub")
    far = jnp.sum(replies[:, capacity:].astype(F32), axis=(0, 1))
    curvature = near + far
    alpha = norm_now / curvature
    values = replies[:, :capacity].reshape(slots, cases)
    image = local + lax.dot_general(slotted, values, (((0,), (0,)), ((), ())), preferred_element_type=F32)
    image = image - facing(image)
    remainder = residual - alpha * image

    scalars = [jnp.sum(remainder * remainder, axis=0), jnp.sum(remainder * image, axis=0)]
    _, _, rhs, weights, sums = forward(remainder, scalars, marks)
    near, norm_next, cross = sums[0], sums[1], sums[2]
    solved = coarse(rhs)
    far = jnp.sum(weights * solved.astype(F32), axis=0)
    far = jnp.sum(exchange(jnp.broadcast_to(far[None], (n_coarse, cases)), "coarse"), axis=0)
    far = jnp.sum(exchange(jnp.broadcast_to(far[None], (n_sub, cases)), "sub"), axis=0)
    beta = norm_next / norm_now
    step = norm_next / (near + far + 2.0 * beta * cross + beta * beta * curvature)
    return ((alpha + step * beta) * residual + step * remainder)[None]


def solution(mesh):
    return jax.shard_map(
        body,
        mesh=mesh,
        in_specs=(
            P(("sub", "coarse"), None, None),
            P(("sub", "coarse"), None, None),
            P(("sub", "coarse"), None, None),
            P("coarse", "sub"),
            P(("sub", "coarse"), None),
            P(("sub", "coarse"), None),
            P(("sub", "coarse"), None, None),
            P(("sub", "coarse"), None),
        ),
        out_specs=P(("sub", "coarse"), None, None),
        check_vma=False,
    )
```

```python
import jax
import jax.numpy as jnp
from jax import lax
from jax.sharding import PartitionSpec as P

HIGHEST = lax.Precision.HIGHEST
F32, BF16 = jnp.float32, jnp.bfloat16


def exchange(blocks, axis):
    return lax.all_to_all(blocks, axis, split_axis=0, concat_axis=0, tiled=True)


def in_two(value):
    high = lax.reduce_precision(value, 8, 7)
    return jnp.stack([high, value - high]).astype(BF16)


def body(
    load,
    schur,
    coupling,
    coarse_inverse,
    neighbour_sub,
    neighbour_edge,
    primal_owner,
    primal_offset,
):
    _, order, cases = load.shape
    edges = neighbour_sub.shape[1]
    width = order // edges
    half = edges // 2
    rows, block = coarse_inverse.shape
    n_sub, n_coarse = lax.axis_size("sub"), lax.axis_size("coarse")
    piece = block // n_coarse
    capacity = 2
    slots = n_sub * capacity
    sub_index, coarse_index = lax.axis_index("sub"), lax.axis_index("coarse")

    faces_next = (neighbour_sub[0] // n_coarse - sub_index) % n_sub == 1
    edge_at = neighbour_edge[0]
    same_side = faces_next[:, None] == faces_next[None, :]
    ids = jnp.arange(edges, dtype=jnp.int32)
    from_place = jnp.sum((same_side & (edge_at[None, :] < edge_at[:, None])).astype(jnp.int32), axis=1)
    from_place = from_place + jnp.where(faces_next, half, 0)
    to_place = jnp.sum((same_side & (ids[None, :] < ids[:, None])).astype(jnp.int32), axis=1)
    to_place = to_place + jnp.where(faces_next, 0, half)
    send_order = jnp.sum(jnp.where(to_place[None, :] == ids[:, None], ids[None, :], 0), axis=1)

    def facing(field):
        ordered = field.reshape(edges, width, cases)[send_order]
        from_before = lax.ppermute(ordered[:half], "sub", [(i, (i + 1) % n_sub) for i in range(n_sub)])
        from_next = lax.ppermute(ordered[half:], "sub", [((i + 1) % n_sub, i) for i in range(n_sub)])
        both = jnp.concatenate([from_before, from_next], axis=0)
        return both[from_place].reshape(order, cases)

    owners = primal_owner.reshape(-1)
    offsets = primal_offset.reshape(-1)
    prims = owners.shape[0]
    row_ids = jnp.arange(prims, dtype=jnp.int32)
    earlier = (owners[:, None] == owners[None, :]) & (row_ids[None, :] < row_ids[:, None])
    slot_of = owners * capacity + jnp.sum(earlier.astype(jnp.int32), axis=1)
    placed = jnp.arange(slots, dtype=jnp.int32)[:, None] == slot_of[None, :]
    slotted = jnp.dot(placed.astype(BF16), coupling[0], preferred_element_type=F32).astype(BF16)
    slot_offset = jnp.sum(jnp.where(placed, offsets[None, :] + 1, 0), axis=1) - 1

    def contributions(field):
        twice = 2.0 * field
        jumps = twice.astype(BF16)
        rest = (twice - jumps.astype(F32)).astype(BF16)
        local = jnp.dot(schur[0], jumps, preferred_element_type=F32)
        near = jnp.sum(twice * local, axis=0)
        terms = jnp.dot(slotted, jnp.concatenate([jumps, rest], axis=1), preferred_element_type=F32)
        rounded, whole = terms[:, :cases], terms[:, :cases] + terms[:, cases:]
        by_owner = (n_sub, capacity, cases)
        return local, near, rounded.reshape(by_owner), whole.reshape(by_owner)

    chips = n_sub // 2
    same_core = [[2 * chip + core for chip in range(chips)] for core in range(2)]
    other_core = [(i, i ^ 1) for i in range(n_sub)]

    def product(rhs):
        mine = lax.all_to_all(
            jnp.broadcast_to(rhs[None], (chips,) + rhs.shape), "sub", 0, 0, tiled=True, axis_index_groups=same_core
        )
        theirs = lax.ppermute(mine, "sub", other_core)
        both = jnp.where(
            sub_index % 2 == 0, jnp.concatenate([mine, theirs], axis=1), jnp.concatenate([theirs, mine], axis=1)
        )
        return lax.dot_general(
            coarse_inverse, both.reshape(rows, cases), (((0,), (0,)), ((), ())), preferred_element_type=F32
        )

    start = load[0]
    residual = start.astype(F32) - facing(start).astype(F32)
    local, near, rounded, whole = contributions(residual)
    marked = jnp.broadcast_to(slot_offset.astype(F32).reshape(n_sub, capacity, 1), (n_sub, capacity, cases))
    scalars = jnp.stack([near, jnp.sum(residual * residual, axis=0)])
    incoming = exchange(
        jnp.concatenate([rounded, whole, marked, jnp.broadcast_to(scalars[None], (n_sub, 2, cases))], axis=1), "sub"
    )
    named = incoming[:, 2 * capacity : 3 * capacity].reshape(slots, cases)
    lanes = lax.broadcasted_iota(jnp.int32, (slots, block), 1).astype(F32)
    marks = (jnp.tile(named, (1, block // cases)) == lanes).astype(F32)
    given = jnp.concatenate(
        [incoming[:, :capacity].reshape(slots, cases), incoming[:, capacity : 2 * capacity].reshape(slots, cases)], axis=1
    )
    partial = lax.dot_general(marks, given, (((0,), (0,)), ((), ())), precision=HIGHEST)
    sums = jnp.sum(incoming[:, 3 * capacity :], axis=0)
    total = exchange(
        jnp.concatenate(
            [
                partial[:, :cases].reshape(n_coarse, piece, cases),
                partial[:, cases:].reshape(n_coarse, piece, cases),
                jnp.broadcast_to(sums[None], (n_coarse, 2, cases)),
            ],
            axis=1,
        ),
        "coarse",
    )
    total = jnp.sum(total, axis=0)
    weights, near, norm_now = total[piece : 2 * piece], total[2 * piece], total[2 * piece + 1]
    share = product(total[:piece].astype(BF16))
    solved = jnp.sum(exchange(share.reshape(n_coarse, piece, cases), "coarse"), axis=0).astype(BF16)
    far = jnp.sum(weights * solved.astype(F32), axis=0)
    mine = jnp.concatenate([solved, in_two(far)], axis=0)
    owned = exchange(jnp.broadcast_to(mine[None], (n_coarse,) + mine.shape), "coarse")
    far = jnp.sum(owned[:, piece:].astype(F32), axis=(0, 1))
    answers = jnp.dot(
        marks.astype(BF16), owned[:, :piece].reshape(block, cases), preferred_element_type=F32
    ).astype(BF16)
    replies = exchange(
        jnp.concatenate(
            [answers.reshape(n_sub, capacity, cases), jnp.broadcast_to(in_two(far)[None], (n_sub, 2, cases))], axis=1
        ),
        "sub",
    )
    curvature = near + jnp.sum(replies[:, capacity:].astype(F32), axis=(0, 1))
    alpha = norm_now / curvature
    values = replies[:, :capacity].reshape(slots, cases)
    image = local + lax.dot_general(slotted, values, (((0,), (0,)), ((), ())), preferred_element_type=F32)
    image = image - facing(image)
    remainder = residual - alpha * image

    _, near, _, whole = contributions(remainder)
    incoming = exchange(whole, "sub").reshape(slots, cases)
    partial = lax.dot_general(marks, incoming, (((0,), (0,)), ((), ())), precision=HIGHEST).astype(BF16)
    partial = exchange(jnp.broadcast_to(partial[None], (n_coarse, block, cases)), "coarse")
    weights = jnp.sum(partial.astype(F32), axis=0)
    rhs = lax.dynamic_slice_in_dim(weights, coarse_index * piece, piece, axis=0).astype(BF16)
    scalars = jnp.stack([near + jnp.sum(weights * product(rhs), axis=0), jnp.sum(remainder * remainder, axis=0)])
    scalars = jnp.sum(exchange(jnp.broadcast_to(scalars[None], (n_coarse, 2, cases)), "coarse"), axis=0)
    scalars = jnp.sum(exchange(jnp.broadcast_to(scalars[None], (n_sub, 2, cases)), "sub"), axis=0)
    beta = scalars[1] / norm_now
    step = scalars[1] / (scalars[0] - beta * beta * curvature)
    return ((alpha + step * beta) * residual + step * remainder)[None]


def solution(mesh):
    return jax.shard_map(
        body,
        mesh=mesh,
        in_specs=(
            P(("sub", "coarse"), None, None),
            P(("sub", "coarse"), None, None),
            P(("sub", "coarse"), None, None),
            P("coarse", "sub"),
            P(("sub", "coarse"), None),
            P(("sub", "coarse"), None),
            P(("sub", "coarse"), None, None),
            P(("sub", "coarse"), None),
        ),
        out_specs=P(("sub", "coarse"), None, None),
        check_vma=False,
    )
```

```python
import jax
import jax.numpy as jnp
from jax import lax
from jax.sharding import PartitionSpec as P

F32, BF16 = jnp.float32, jnp.bfloat16


def exchange(blocks, axis):
    return lax.all_to_all(blocks, axis, split_axis=0, concat_axis=0, tiled=True)


def in_two(value):
    high = lax.reduce_precision(value, 8, 7)
    return high.astype(BF16), (value - high).astype(BF16)


def in_parts(marks, value, flip):
    high = lax.reduce_precision(value, 8, 7)
    middle = lax.reduce_precision(value - high, 8, 7)
    parts = jnp.concatenate([high, middle, value - high - middle], axis=1).astype(BF16)
    out = lax.dot_general(marks, parts, (((1 - flip,), (0,)), ((), ())), preferred_element_type=F32)
    wide = value.shape[1]
    return out[:, :wide] + out[:, wide : 2 * wide] + out[:, 2 * wide :]


def body(
    load,
    schur,
    coupling,
    coarse_inverse,
    neighbour_sub,
    neighbour_edge,
    primal_owner,
    primal_offset,
):
    _, order, cases = load.shape
    edges = neighbour_sub.shape[1]
    width = order // edges
    half = edges // 2
    rows, block = coarse_inverse.shape
    n_sub, n_coarse = lax.axis_size("sub"), lax.axis_size("coarse")
    piece = block // n_coarse
    capacity = 2
    slots = n_sub * capacity
    sub_index, coarse_index = lax.axis_index("sub"), lax.axis_index("coarse")

    faces_next = (neighbour_sub[0] // n_coarse - sub_index) % n_sub == 1
    edge_at = neighbour_edge[0]
    same_side = faces_next[:, None] == faces_next[None, :]
    ids = jnp.arange(edges, dtype=jnp.int32)
    from_place = jnp.sum((same_side & (edge_at[None, :] < edge_at[:, None])).astype(jnp.int32), axis=1)
    from_place = from_place + jnp.where(faces_next, half, 0)
    to_place = jnp.sum((same_side & (ids[None, :] < ids[:, None])).astype(jnp.int32), axis=1)
    to_place = to_place + jnp.where(faces_next, 0, half)
    send_order = jnp.sum(jnp.where(to_place[None, :] == ids[:, None], ids[None, :], 0), axis=1)

    def facing(field):
        ordered = field.reshape(edges, width, cases)[send_order]
        from_before = lax.ppermute(ordered[:half], "sub", [(i, (i + 1) % n_sub) for i in range(n_sub)])
        from_next = lax.ppermute(ordered[half:], "sub", [((i + 1) % n_sub, i) for i in range(n_sub)])
        both = jnp.concatenate([from_before, from_next], axis=0)
        return both[from_place].reshape(order, cases)

    owners = primal_owner.reshape(-1)
    offsets = primal_offset.reshape(-1)
    prims = owners.shape[0]
    row_ids = jnp.arange(prims, dtype=jnp.int32)
    earlier = (owners[:, None] == owners[None, :]) & (row_ids[None, :] < row_ids[:, None])
    slot_of = owners * capacity + jnp.sum(earlier.astype(jnp.int32), axis=1)
    placed = jnp.arange(slots, dtype=jnp.int32)[:, None] == slot_of[None, :]
    slotted = jnp.dot(placed.astype(BF16), coupling[0], preferred_element_type=F32).astype(BF16)
    slot_offset = jnp.sum(jnp.where(placed, offsets[None, :] + 1, 0), axis=1).reshape(n_sub, capacity, 1)
    lane = jnp.arange(slots, dtype=jnp.int32).reshape(1, capacity, n_sub)
    asked = jnp.where(lane == sub_index + n_sub * jnp.arange(capacity).reshape(1, capacity, 1), slot_offset, 0)
    asked = asked.astype(F32).reshape(n_sub, 1, slots)
    codes = jnp.pad(slot_of, (0, cases - prims), constant_values=-1).astype(F32)

    chips = n_sub // 2
    same_core = [[2 * chip + core for chip in range(chips)] for core in range(2)]
    other_core = [(i, i ^ 1) for i in range(n_sub)]
    devices = n_sub * n_coarse
    near_by = 2 * n_coarse
    columns = [[start + k for k in range(near_by)] for start in range(0, devices, near_by)]
    planes = [[start + k for k in range(0, devices, near_by)] for start in range(near_by)]

    def product(rhs):
        mine = lax.all_to_all(
            jnp.broadcast_to(rhs[None], (chips,) + rhs.shape), "sub", 0, 0, tiled=True, axis_index_groups=same_core
        )
        theirs = lax.ppermute(mine, "sub", other_core)
        both = jnp.where(
            sub_index % 2 == 0, jnp.concatenate([mine, theirs], axis=1), jnp.concatenate([theirs, mine], axis=1)
        )
        return lax.dot_general(
            coarse_inverse, both.reshape(rows, cases), (((0,), (0,)), ((), ())), preferred_element_type=F32
        )

    def added(scalars, groups):
        wide = jnp.broadcast_to(scalars[None], (len(groups[0]),) + scalars.shape)
        wide = lax.all_to_all(wide, ("sub", "coarse"), 0, 0, tiled=True, axis_index_groups=groups)
        return jnp.sum(wide, axis=0)

    start = load[0]
    residual = start.astype(F32) - facing(start).astype(F32)
    jumps, rest = in_two(2.0 * residual)
    local = jnp.dot(schur[0], jumps, preferred_element_type=F32)
    near = jnp.sum(2.0 * residual * local, axis=0)
    terms = jnp.dot(slotted, jumps, preferred_element_type=F32).reshape(n_sub, capacity, cases)
    squares = jnp.broadcast_to(jnp.sum(residual * residual, axis=0), (n_sub, 1, cases))
    incoming = exchange(jnp.concatenate([terms, asked, squares], axis=1), "sub")
    given = jnp.concatenate([incoming[:, k] for k in range(capacity)], axis=0)
    asked = jnp.sum(incoming[:, capacity], axis=0)
    norm_now = jnp.sum(incoming[:, capacity + 1], axis=0)
    ids = lax.broadcasted_iota(jnp.int32, (block, slots), 0).astype(F32) + 1.0
    partial = in_parts((ids == asked[None]).astype(BF16), given, 0)
    sides = jnp.broadcast_to(jnp.stack([asked, codes])[None], (n_coarse, 2, cases))
    incoming = exchange(jnp.concatenate([partial.reshape(n_coarse, piece, cases), sides], axis=1), "coarse")
    asked_all = incoming[:, piece].reshape(1, n_coarse * slots)
    codes_all = incoming[:, piece + 1]
    ids = lax.broadcasted_iota(jnp.int32, (block, n_coarse * slots), 0).astype(F32) + 1.0
    marks = (ids == asked_all).astype(BF16)
    share = product(jnp.sum(incoming[:, :piece], axis=0).astype(BF16))
    answers = in_parts(marks, share, 1).reshape(n_coarse, slots, cases)
    solved = jnp.sum(exchange(answers, "coarse"), axis=0).astype(BF16)
    far = in_two(near + jnp.sum(given * solved.astype(F32), axis=0))
    out = [solved[k * n_sub : (k + 1) * n_sub, None] for k in range(capacity)]
    out = out + [jnp.broadcast_to(part, (n_sub, 1, cases)) for part in far]
    replies = exchange(jnp.concatenate(out, axis=1), "sub")
    curvature = jnp.sum(replies[:, capacity:].astype(F32), axis=(0, 1))
    values = replies[:, :capacity].reshape(slots, cases)
    image = local + lax.dot_general(slotted, values, (((0,), (0,)), ((), ())), preferred_element_type=F32)
    image = image - facing(image)

    old = jnp.dot(coupling[0], jnp.concatenate([jumps, rest], axis=1), preferred_element_type=F32)
    new = jnp.dot(coupling[0], jnp.concatenate(in_two(2.0 * image), axis=1), preferred_element_type=F32)
    sent = jnp.concatenate(
        [old[:, :cases] + old[:, cases:], new[:, :cases] + new[:, cases:], curvature[None], norm_now[None]], axis=0
    )
    incoming = exchange(jnp.broadcast_to(sent[None], (n_coarse,) + sent.shape), "coarse")
    curvature = jnp.sum(incoming[:, 2 * prims], axis=0)
    norm_now = jnp.sum(incoming[:, 2 * prims + 1], axis=0)
    alpha = norm_now / curvature
    coupled = (incoming[:, :prims] - alpha * incoming[:, prims : 2 * prims]).astype(BF16)
    room = 32
    coupled = jnp.pad(coupled, ((0, 0), (0, room - prims), (0, 0))).reshape(n_coarse * room, cases)
    codes_all = codes_all[:, :room].reshape(1, n_coarse * room)
    place = lax.broadcasted_iota(jnp.int32, (n_sub * n_coarse * capacity, n_coarse * room), 0)
    plane = lax.broadcasted_iota(jnp.int32, (n_sub * n_coarse * capacity, n_coarse * room), 1) // room
    here = place // (n_coarse * capacity) * capacity + place % capacity
    spread = (place // capacity % n_coarse == plane) & (here.astype(F32) == codes_all)
    outgoing = jnp.dot(spread.astype(BF16), coupled, preferred_element_type=F32).astype(BF16)
    incoming = exchange(outgoing.reshape(n_sub, n_coarse * capacity, cases), "sub")
    incoming = incoming.transpose(1, 0, 2).reshape(n_coarse * slots, cases)
    weights = jnp.dot(marks, incoming, preferred_element_type=F32)
    rhs = lax.dynamic_slice_in_dim(weights, coarse_index * piece, piece, axis=0).astype(BF16)
    far = jnp.sum(weights * product(rhs), axis=0)
    remainder = residual - alpha * image
    twice = 2.0 * remainder
    near = jnp.sum(twice * jnp.dot(schur[0], twice.astype(BF16), preferred_element_type=F32), axis=0)
    scalars = jnp.stack([near + far, jnp.sum(remainder * remainder, axis=0)])
    scalars = added(added(scalars, columns), planes)
    beta = scalars[1] / norm_now
    step = scalars[1] / (scalars[0] - beta * beta * curvature)
    return ((alpha + step * beta) * residual + step * remainder)[None]


def solution(mesh):
    return jax.shard_map(
        body,
        mesh=mesh,
        in_specs=(
            P(("sub", "coarse"), None, None),
            P(("sub", "coarse"), None, None),
            P(("sub", "coarse"), None, None),
            P("coarse", "sub"),
            P(("sub", "coarse"), None),
            P(("sub", "coarse"), None),
            P(("sub", "coarse"), None, None),
            P(("sub", "coarse"), None),
        ),
        out_specs=P(("sub", "coarse"), None, None),
        check_vma=False,
    )
```

```python
import jax
import jax.numpy as jnp
from jax import lax
from jax.experimental import pallas as pl
from jax.experimental.pallas import tpu as pltpu
from jax.sharding import PartitionSpec as P

F32, BF16, I32 = jnp.float32, jnp.bfloat16, jnp.int32
CAPACITY = 2
LINES = 4
ROOM = 32
SIDES = 8


def dot(a, b):
    return jnp.dot(a, b, preferred_element_type=F32)


def dot_t(a, b):
    return lax.dot_general(a, b, (((0,), (0,)), ((), ())), preferred_element_type=F32)


def iota(shape, dim):
    return lax.broadcasted_iota(I32, shape, dim)


def ones_where(mask):
    return jnp.where(mask, 1.0, 0.0).astype(BF16)


def in_two(value):
    high = value.astype(BF16)
    return high, (value - high.astype(F32)).astype(BF16)


def in_three(value):
    high = value.astype(BF16)
    rest = value - high.astype(F32)
    middle = rest.astype(BF16)
    return jnp.concatenate([high, middle, (rest - middle.astype(F32)).astype(BF16)], axis=1)


def joined(parts, count):
    wide = parts.shape[1] // count
    out = parts[:, :wide]
    for k in range(1, count):
        out = out + parts[:, k * wide : (k + 1) * wide]
    return out


def run(kernel, outs, *args):
    def spec(x):
        small = jnp.issubdtype(x.dtype, jnp.integer) and x.size <= 8
        return pl.BlockSpec(memory_space=pltpu.SMEM if small else pltpu.VMEM)

    return pl.pallas_call(
        kernel,
        out_shape=[jax.ShapeDtypeStruct(shape, dtype) for shape, dtype in outs],
        in_specs=[spec(x) for x in args],
        out_specs=[pl.BlockSpec(memory_space=pltpu.VMEM)] * len(outs),
        compiler_params=pltpu.CompilerParams(vmem_limit_bytes=32 * 1024 * 1024),
    )(*args)


def body(
    load,
    schur,
    coupling,
    coarse_inverse,
    neighbour_sub,
    neighbour_edge,
    primal_owner,
    primal_offset,
):
    _, order, cases = load.shape
    edges = neighbour_sub.shape[1]
    width = order // edges
    half = edges // 2
    rows, block = coarse_inverse.shape
    prims = primal_offset.shape[1]
    n_sub, n_coarse = lax.axis_size("sub"), lax.axis_size("coarse")
    piece = block // n_coarse
    slots = n_sub * CAPACITY
    lines = n_sub * LINES
    chips = n_sub // 2
    sub_index, coarse_index = lax.axis_index("sub"), lax.axis_index("coarse")
    here = jnp.stack([sub_index, coarse_index])[None].astype(I32)

    to_next = [(i, (i + 1) % n_sub) for i in range(n_sub)]
    to_before = [((i + 1) % n_sub, i) for i in range(n_sub)]
    other_core = [(i, i ^ 1) for i in range(n_sub)]
    same_core = [[2 * chip + core for chip in range(chips)] for core in range(2)]
    near_by = 2 * n_coarse
    devices = n_sub * n_coarse
    columns = [[start + k for k in range(near_by)] for start in range(0, devices, near_by)]
    planes = [[start + k for k in range(0, devices, near_by)] for start in range(near_by)]

    def exchange(blocks, axis, groups=None):
        return lax.all_to_all(blocks, axis, 0, 0, tiled=True, axis_index_groups=groups)

    def faces_next(here_ref, sub_ref, e):
        return lax.rem(lax.div(sub_ref[0, e], n_coarse) - here_ref[0, 0] + n_sub, n_sub) == 1

    def edge(e):
        return slice(e * width, (e + 1) * width)

    def set_up(here_ref, owner_ref, offset_ref, coupling_ref, slotted_ref, asked_ref, codes_ref):
        same = iota((prims, prims), 0) == iota((prims, prims), 1)
        owner_row = jnp.sum(jnp.where(same, owner_ref[...], 0), axis=0, keepdims=True)
        before = (owner_ref[...] == owner_row) & (iota((prims, prims), 0) < iota((prims, prims), 1))
        second = jnp.sum(jnp.where(before, 1, 0), axis=0, keepdims=True)
        line = iota((lines, prims), 0)
        placed = line == owner_row * LINES + second
        slotted_ref[...] = dot(ones_where(placed), coupling_ref[...]).astype(BF16)
        lane = iota((lines, slots), 1)
        asked = jnp.zeros((lines, slots), I32)
        for k in range(CAPACITY):
            named = (line >> 2 == owner_row) & (second == k)
            offset = jnp.sum(jnp.where(named, offset_ref[...] + 1, 0), axis=1, keepdims=True)
            asked = jnp.where(lane == k * n_sub + here_ref[0, 0], offset, asked)
        asked_ref[...] = jnp.where((iota((lines, slots), 0) & (LINES - 1)) == CAPACITY, asked, 0).astype(F32)
        target = owner_row * (n_coarse * CAPACITY) + second + CAPACITY * here_ref[0, 1] + 1
        far_lane = iota((prims, n_coarse * ROOM), 1) == iota((prims, n_coarse * ROOM), 0) + ROOM * here_ref[0, 1]
        target_col = jnp.sum(jnp.where(same, target, 0), axis=1, keepdims=True)
        codes = jnp.sum(jnp.where(far_lane, target_col, 0), axis=0, keepdims=True).astype(F32)
        codes_ref[...] = jnp.zeros((SIDES, cases), F32)
        for k in range(n_coarse * ROOM // cases):
            codes_ref[k + 1 : k + 2, :] = codes[:, k * cases : (k + 1) * cases]

    def first(
        here_ref, sub_ref, edge_ref, load_ref, before_ref, next_ref, schur_ref, slotted_ref, asked_ref, coupling_ref,
        residual_ref, local_ref, out_ref, near_ref, old_ref,
    ):
        for e in range(edges):
            start = pl.multiple_of(edge_ref[0, e] * width, width)
            ahead = next_ref[pl.ds(start, width), :].astype(F32)
            behind = before_ref[pl.ds(start, width), :].astype(F32)
            facing = jnp.where(faces_next(here_ref, sub_ref, e), ahead, behind)
            residual_ref[edge(e), :] = load_ref[edge(e), :].astype(F32) - facing
        twice = 2.0 * residual_ref[...]
        jumps, rest = in_two(twice)
        terms = dot(slotted_ref[...], jumps)
        squares = jnp.sum(twice * twice, axis=0, keepdims=True) * 0.25
        line = iota((lines, cases), 0) & (LINES - 1)
        out_ref[...] = terms + asked_ref[...] + jnp.where(line == LINES - 1, squares, 0.0)
        local = dot(schur_ref[...], jumps)
        local_ref[...] = local
        near_ref[...] = jnp.sum(twice * local, axis=0, keepdims=True)
        old_ref[...] = joined(dot(coupling_ref[...], jnp.concatenate([jumps, rest], axis=1)), 2)

    def line_of(shape, dim):
        return (iota(shape, dim) & (LINES - 1)) * n_sub + (iota(shape, dim) >> 2)

    def owner_sums(in_ref, codes_ref, out_ref, norm_ref):
        given = in_ref[...]
        line = iota((lines, cases), 0) & (LINES - 1)
        asked = jnp.sum(jnp.where(line == CAPACITY, given, 0.0), axis=0, keepdims=True)
        norm_ref[...] = jnp.sum(jnp.where(line == LINES - 1, given, 0.0), axis=0, keepdims=True)
        expand = ones_where(iota((slots, lines), 0) == line_of((slots, lines), 1))
        wide = dot(jnp.broadcast_to(asked, (SIDES, slots)).astype(BF16), expand)[:1]
        marks = ones_where((iota((block, lines), 0) + 1).astype(F32) == wide)
        partial = joined(dot(marks, in_three(given)), 3)
        sides = codes_ref[...] + jnp.where(iota((SIDES, cases), 0) == 0, asked, 0.0)
        for c in range(n_coarse):
            out_ref[c, :piece] = partial[c * piece : (c + 1) * piece]
            out_ref[c, piece:] = sides

    def coarse_sums(in_ref, rhs_ref, marks_ref, codes_ref):
        total = in_ref[0]
        for c in range(1, n_coarse):
            total = total + in_ref[c]
        rhs = total[:piece].astype(BF16)
        for k in range(chips):
            rhs_ref[k] = rhs
        ids = (iota((block, slots), 0) + 1).astype(F32)
        for c in range(n_coarse):
            marks_ref[:, c * slots : (c + 1) * slots] = ones_where(ids == in_ref[c, piece : piece + 1])
        codes_ref[...] = total[piece:]

    def product(here_ref, mine_ref, theirs_ref, inverse_ref, both_ref):
        core = lax.rem(here_ref[0, 0], 2)
        for k in range(chips):
            both_ref[pl.ds(pl.multiple_of((2 * k + core) * piece, piece), piece), :] = mine_ref[k]
            both_ref[pl.ds(pl.multiple_of((2 * k + 1 - core) * piece, piece), piece), :] = theirs_ref[k]
        return dot_t(inverse_ref[...], both_ref[...])

    def answer(here_ref, mine_ref, theirs_ref, inverse_ref, marks_ref, both_ref, out_ref):
        share = in_three(product(here_ref, mine_ref, theirs_ref, inverse_ref, both_ref))
        for c in range(n_coarse):
            out_ref[c] = joined(dot_t(marks_ref[:, c * slots : (c + 1) * slots], share), 3)

    def reply(in_ref, given_ref, near_ref, out_ref):
        solved = in_ref[0]
        for c in range(1, n_coarse):
            solved = solved + in_ref[c]
        expand = ones_where(line_of((lines, slots), 0) == iota((lines, slots), 1))
        wide = dot(expand, solved.astype(BF16))
        line = iota((lines, cases), 0) & (LINES - 1)
        far = near_ref[...] + jnp.sum(jnp.where(line < CAPACITY, given_ref[...] * wide, 0.0), axis=0, keepdims=True)
        high, low = in_two(far)
        wide = jnp.where(line == CAPACITY, high.astype(F32), wide)
        out_ref[...] = jnp.where(line == CAPACITY + 1, low.astype(F32), wide).astype(BF16)

    def back(here_ref, sub_ref, in_ref, slotted_ref, local_ref, image_ref, ahead_ref, behind_ref, curvature_ref):
        replies = in_ref[...]
        image_ref[...] = local_ref[...] + dot_t(slotted_ref[...], replies)
        line = iota((lines, cases), 0) & (LINES - 1)
        curvature_ref[...] = jnp.sum(jnp.where(line >= CAPACITY, replies.astype(F32), 0.0), axis=0, keepdims=True)
        ahead = jnp.int32(0)
        for e in range(edges):
            faces = faces_next(here_ref, sub_ref, e)

            @pl.when(faces)
            def _():
                ahead_ref[pl.ds(pl.multiple_of(ahead * width, width), width), :] = image_ref[edge(e), :]

            @pl.when(jnp.logical_not(faces))
            def _():
                behind_ref[pl.ds(pl.multiple_of((e - ahead) * width, width), width), :] = image_ref[edge(e), :]

            ahead = ahead + faces.astype(I32)

    def coupled_rows(
        here_ref, sub_ref, edge_ref, image_ref, before_ref, next_ref, coupling_ref, old_ref, curvature_ref, norm_ref,
        jump_ref, out_ref,
    ):
        for e in range(edges):
            faces = faces_next(here_ref, sub_ref, e)
            place = jnp.int32(0)
            for other in range(edges):
                alike = faces_next(here_ref, sub_ref, other) == faces
                place = place + (alike & (edge_ref[0, other] < edge_ref[0, e])).astype(I32)
            start = pl.multiple_of(place * width, width)
            facing = jnp.where(faces, next_ref[pl.ds(start, width), :], before_ref[pl.ds(start, width), :])
            jump_ref[edge(e), :] = image_ref[edge(e), :] - facing
        pair = jnp.concatenate(in_two(2.0 * jump_ref[...]), axis=1)
        new = joined(dot(coupling_ref[...], pair), 2)
        line = iota((SIDES, cases), 0)
        tail = jnp.where(line == 0, curvature_ref[...], jnp.where(line == 1, norm_ref[...], 0.0))
        for c in range(n_coarse):
            out_ref[c, :prims] = old_ref[...]
            out_ref[c, prims : 2 * prims] = new
            out_ref[c, 2 * prims :] = tail

    def spread(in_ref, codes_ref, out_ref, scalars_ref):
        tail = in_ref[0, 2 * prims :]
        for c in range(1, n_coarse):
            tail = tail + in_ref[c, 2 * prims :]
        curvature, norm = tail[0:1], tail[1:2]
        alpha = norm / curvature
        line = iota((SIDES, cases), 0)
        scalars_ref[...] = jnp.where(line == 0, alpha, jnp.where(line == 1, curvature, norm))
        empty = jnp.zeros((ROOM - prims, cases), F32)
        parts = []
        for c in range(n_coarse):
            parts += [in_ref[c, :prims] - alpha * in_ref[c, prims : 2 * prims], empty]
        coupled = jnp.concatenate(parts, axis=0).astype(BF16)
        target = jnp.concatenate([codes_ref[k + 1 : k + 2, :] for k in range(n_coarse * ROOM // cases)], axis=1)
        total = n_coarse * slots
        marks = ones_where((iota((total, n_coarse * ROOM), 0) + 1).astype(F32) == target)
        out_ref[...] = dot(marks, coupled).astype(BF16)

    def owner_rows(here_ref, in_ref, marks_ref, weights_ref, rhs_ref):
        weights_ref[...] = dot(marks_ref[...], in_ref[...])
        start = pl.multiple_of(here_ref[0, 1] * piece, piece)
        rhs = weights_ref[pl.ds(start, piece), :].astype(BF16)
        for k in range(chips):
            rhs_ref[k] = rhs

    def second(residual_ref, jump_ref, scalars_ref, schur_ref, remainder_ref, sums_ref):
        remainder = residual_ref[...] - scalars_ref[0:1] * jump_ref[...]
        remainder_ref[...] = remainder
        twice = 2.0 * remainder
        near = jnp.sum(twice * dot(schur_ref[...], twice.astype(BF16)), axis=0, keepdims=True)
        line = iota((SIDES, cases), 0)
        norm = jnp.sum(remainder * remainder, axis=0, keepdims=True)
        sums_ref[...] = jnp.where(line == 0, near, jnp.where(line == 1, norm, 0.0))

    def energy(here_ref, mine_ref, theirs_ref, inverse_ref, weights_ref, sums_ref, both_ref, out_ref):
        share = product(here_ref, mine_ref, theirs_ref, inverse_ref, both_ref)
        far = jnp.sum(weights_ref[...] * share, axis=0, keepdims=True)
        out_ref[...] = sums_ref[...] + jnp.where(iota((SIDES, cases), 0) == 0, far, 0.0)

    field = ((order, cases), F32)
    row = ((1, cases), F32)
    gathered = ((chips, piece, cases), BF16)
    owners = primal_owner.reshape(prims, 1)
    offsets = primal_offset.reshape(1, prims)
    start = load[0]
    from_before = lax.ppermute(start, "sub", to_next)
    from_next = lax.ppermute(start, "sub", to_before)
    slotted, asked, codes = run(
        set_up,
        [((lines, order), BF16), ((lines, slots), F32), ((SIDES, cases), F32)],
        here,
        owners,
        offsets,
        coupling[0],
    )
    residual, local, outgoing, near, old = run(
        first,
        [field, field, ((lines, cases), F32), row, ((prims, cases), F32)],
        here, neighbour_sub, neighbour_edge, start, from_before, from_next, schur[0], slotted, asked, coupling[0],
    )
    given = exchange(outgoing.reshape(n_sub, LINES, cases), "sub").reshape(lines, cases)
    outgoing, norm = run(owner_sums, [((n_coarse, piece + SIDES, cases), F32), row], given, codes)
    incoming = exchange(outgoing, "coarse")
    rhs, marks, codes = run(
        coarse_sums, [gathered, ((block, n_coarse * slots), BF16), ((SIDES, cases), F32)], incoming
    )
    mine = exchange(rhs, "sub", same_core)
    theirs = lax.ppermute(mine, "sub", other_core)
    both = ((rows, cases), BF16)
    _, outgoing = run(answer, [both, ((n_coarse, slots, cases), F32)], here, mine, theirs, coarse_inverse, marks)
    incoming = exchange(outgoing, "coarse")
    (outgoing,) = run(reply, [((lines, cases), BF16)], incoming, given, near)
    replies = exchange(outgoing.reshape(n_sub, LINES, cases), "sub").reshape(lines, cases)
    side = ((half * width, cases), F32)
    image, ahead, behind, curvature = run(
        back, [field, side, side, row], here, neighbour_sub, replies, slotted, local
    )
    from_before = lax.ppermute(ahead, "sub", to_next)
    from_next = lax.ppermute(behind, "sub", to_before)
    image, outgoing = run(
        coupled_rows,
        [field, ((n_coarse, 2 * prims + SIDES, cases), F32)],
        here, neighbour_sub, neighbour_edge, image, from_before, from_next, coupling[0], old, curvature, norm,
    )
    incoming = exchange(outgoing, "coarse")
    outgoing, scalars = run(
        spread, [((n_coarse * slots, cases), BF16), ((SIDES, cases), F32)], incoming, codes
    )
    incoming = exchange(outgoing.reshape(n_sub, n_coarse * CAPACITY, cases), "sub")
    incoming = incoming.transpose(1, 0, 2).reshape(n_coarse * slots, cases)
    weights, rhs = run(owner_rows, [((block, cases), F32), gathered], here, incoming, marks)
    mine = exchange(rhs, "sub", same_core)
    theirs = lax.ppermute(mine, "sub", other_core)
    remainder, sums = run(second, [field, ((SIDES, cases), F32)], residual, image, scalars, schur[0])
    _, sums = run(
        energy, [both, ((SIDES, cases), F32)], here, mine, theirs, coarse_inverse, weights, sums
    )
    sums = sums[:2]
    for groups in (columns, planes):
        wide = jnp.broadcast_to(sums[None], (len(groups[0]),) + sums.shape)
        sums = jnp.sum(exchange(wide, ("sub", "coarse"), groups), axis=0)
    alpha, curvature, norm = scalars[0], scalars[1], scalars[2]
    beta = sums[1] / norm
    step = sums[1] / (sums[0] - beta * beta * curvature)
    return ((alpha + step * beta) * residual + step * remainder)[None]


def solution(mesh):
    return jax.shard_map(
        body,
        mesh=mesh,
        in_specs=(
            P(("sub", "coarse"), None, None),
            P(("sub", "coarse"), None, None),
            P(("sub", "coarse"), None, None),
            P("coarse", "sub"),
            P(("sub", "coarse"), None),
            P(("sub", "coarse"), None),
            P(("sub", "coarse"), None, None),
            P(("sub", "coarse"), None),
        ),
        out_specs=P(("sub", "coarse"), None, None),
        check_vma=False,
    )
```

```python
import jax
import jax.numpy as jnp
from jax import lax
from jax.experimental import pallas as pl
from jax.experimental.pallas import tpu as pltpu
from jax.sharding import PartitionSpec as P

F32, BF16, I32 = jnp.float32, jnp.bfloat16, jnp.int32
CAPACITY = 2
LINES = 4
ROOM = 32
SIDES = 8


def dot(a, b):
    return jnp.dot(a, b, preferred_element_type=F32)


def dot_t(a, b):
    return lax.dot_general(a, b, (((0,), (0,)), ((), ())), preferred_element_type=F32)


def iota(shape, dim):
    return lax.broadcasted_iota(I32, shape, dim)


def ones_where(mask):
    return jnp.where(mask, 1.0, 0.0).astype(BF16)


def in_two(value):
    high = value.astype(BF16)
    return high, (value - high.astype(F32)).astype(BF16)


def in_three(value):
    high = value.astype(BF16)
    rest = value - high.astype(F32)
    middle = rest.astype(BF16)
    return jnp.concatenate([high, middle, (rest - middle.astype(F32)).astype(BF16)], axis=1)


def joined(parts, count):
    wide = parts.shape[1] // count
    out = parts[:, :wide]
    for k in range(1, count):
        out = out + parts[:, k * wide : (k + 1) * wide]
    return out


ANY = pl.BlockSpec(memory_space=pl.ANY)
SMEM = pl.BlockSpec(memory_space=pltpu.SMEM)
VMEM = pl.BlockSpec(memory_space=pltpu.VMEM)


def run(kernel, outs, *args, specs=None, scratch=()):
    def spec(x):
        return SMEM if jnp.issubdtype(x.dtype, jnp.integer) and x.size <= 32 and x.shape[1] <= 8 else VMEM

    return pl.pallas_call(
        kernel,
        out_shape=[jax.ShapeDtypeStruct(shape, dtype) for shape, dtype in outs],
        in_specs=specs or [spec(x) for x in args],
        out_specs=[SMEM if dtype == I32 else VMEM for _, dtype in outs],
        scratch_shapes=scratch,
        compiler_params=pltpu.CompilerParams(vmem_limit_bytes=32 * 1024 * 1024),
    )(*args)


def body(
    load,
    schur,
    coupling,
    coarse_inverse,
    neighbour_sub,
    neighbour_edge,
    primal_owner,
    primal_offset,
):
    _, order, cases = load.shape
    edges = neighbour_sub.shape[1]
    width = order // edges
    half = edges // 2
    rows, block = coarse_inverse.shape
    prims = primal_offset.shape[1]
    n_sub, n_coarse = lax.axis_size("sub"), lax.axis_size("coarse")
    piece = block // n_coarse
    slots = n_sub * CAPACITY
    lines = n_sub * LINES
    chips = n_sub // 2
    sub_index, coarse_index = lax.axis_index("sub"), lax.axis_index("coarse")
    here = jnp.stack([sub_index, coarse_index])[None].astype(I32)

    to_next = [(i, (i + 1) % n_sub) for i in range(n_sub)]
    to_before = [((i + 1) % n_sub, i) for i in range(n_sub)]
    other_core = [(i, i ^ 1) for i in range(n_sub)]
    same_core = [[2 * chip + core for chip in range(chips)] for core in range(2)]
    near_by = 2 * n_coarse
    devices = n_sub * n_coarse
    columns = [[start + k for k in range(near_by)] for start in range(0, devices, near_by)]
    planes = [[start + k for k in range(0, devices, near_by)] for start in range(near_by)]

    def exchange(blocks, axis, groups=None):
        return lax.all_to_all(blocks, axis, 0, 0, tiled=True, axis_index_groups=groups)

    def edge(e):
        return slice(e * width, (e + 1) * width)

    def set_up(
        here_ref, sub_ref, edge_ref, owner_ref, offset_ref, coupling_hbm, schur_hbm, load_hbm,
        slotted_ref, turned_ref, asked_ref, codes_ref, table_ref, coupling_ref, schur_ref, load_ref, sems,
    ):
        moves = [(coupling_hbm, coupling_ref), (load_hbm, load_ref), (schur_hbm, schur_ref)]
        moves = [pltpu.make_async_copy(a, b, sems.at[k]) for k, (a, b) in enumerate(moves)]
        for move in moves:
            move.start()
        faces = []
        for e in range(edges):
            side = lax.rem(lax.div(sub_ref[0, e], n_coarse) - here_ref[0, 0] + n_sub, n_sub) == 1
            faces.append(side.astype(I32))
        ahead = jnp.int32(0)
        for e in range(edges):
            place = jnp.int32(0)
            for other in range(edges):
                if other != e:
                    lower = (faces[other] == faces[e]) & (edge_ref[0, other] < edge_ref[0, e])
                    place = place + lower.astype(I32)
            table_ref[0, e] = faces[e]
            table_ref[1, e] = place
            table_ref[2, e] = faces[e] * ahead + (1 - faces[e]) * (e - ahead)
            ahead = ahead + faces[e]
        same = iota((prims, prims), 0) == iota((prims, prims), 1)
        owner_row = owner_ref[...]
        owner_col = jnp.sum(jnp.where(same, owner_row, 0), axis=1, keepdims=True)
        before = (owner_col == owner_row) & (iota((prims, prims), 0) < iota((prims, prims), 1))
        second = jnp.sum(jnp.where(before, 1, 0), axis=0, keepdims=True)
        line = iota((lines, prims), 0)
        placed = ones_where(line == owner_row * LINES + second)
        lane = iota((lines, slots), 1)
        asked = jnp.zeros((lines, slots), I32)
        for k in range(CAPACITY):
            named = (line >> 2 == owner_row) & (second == k)
            offset = jnp.sum(jnp.where(named, offset_ref[...] + 1, 0), axis=1, keepdims=True)
            asked = jnp.where(lane == k * n_sub + here_ref[0, 0], offset, asked)
        asked_ref[...] = jnp.where((iota((lines, slots), 0) & (LINES - 1)) == CAPACITY, asked, 0).astype(F32)
        target = owner_row * (n_coarse * CAPACITY) + second + CAPACITY * here_ref[0, 1] + 1
        far_lane = iota((prims, n_coarse * ROOM), 1) == iota((prims, n_coarse * ROOM), 0) + ROOM * here_ref[0, 1]
        target_col = jnp.sum(jnp.where(same, target, 0), axis=1, keepdims=True)
        codes = jnp.sum(jnp.where(far_lane, target_col, 0), axis=0, keepdims=True).astype(F32)
        codes_ref[...] = jnp.zeros((SIDES, cases), F32)
        for k in range(n_coarse * ROOM // cases):
            codes_ref[k + 1 : k + 2, :] = codes[:, k * cases : (k + 1) * cases]
        moves[0].wait()
        slotted_ref[...] = dot(placed, coupling_ref[...]).astype(BF16)
        turned_ref[...] = lax.dot_general(
            coupling_ref[...], placed, (((0,), (1,)), ((), ())), preferred_element_type=F32
        ).astype(BF16)
        moves[1].wait()
        moves[2].wait()

    def first(
        table_ref, edge_ref, load_ref, before_ref, next_ref, schur_ref, slotted_ref, asked_ref, coupling_ref,
        residual_ref, local_ref, out_ref, near_ref, old_ref,
    ):
        for e in range(edges):
            start = pl.multiple_of(edge_ref[0, e] * width, width)
            ahead = next_ref[pl.ds(start, width), :].astype(F32)
            behind = before_ref[pl.ds(start, width), :].astype(F32)
            facing = jnp.where(table_ref[0, e] == 1, ahead, behind)
            residual_ref[edge(e), :] = load_ref[edge(e), :].astype(F32) - facing
        twice = 2.0 * residual_ref[...]
        jumps, rest = in_two(twice)
        terms = dot(slotted_ref[...], jumps)
        squares = jnp.sum(twice * twice, axis=0, keepdims=True) * 0.25
        line = iota((lines, cases), 0) & (LINES - 1)
        out_ref[...] = terms + asked_ref[...] + jnp.where(line == LINES - 1, squares, 0.0)
        local = dot(schur_ref[...], jumps)
        local_ref[...] = local
        near_ref[...] = jnp.sum(twice * local, axis=0, keepdims=True)
        old_ref[...] = joined(dot(coupling_ref[...], jnp.concatenate([jumps, rest], axis=1)), 2)

    def line_of(shape, dim):
        return (iota(shape, dim) & (LINES - 1)) * n_sub + (iota(shape, dim) >> 2)

    def owner_sums(in_ref, codes_ref, out_ref, norm_ref):
        given = in_ref[...]
        line = iota((lines, cases), 0) & (LINES - 1)
        asked = jnp.sum(jnp.where(line == CAPACITY, given, 0.0), axis=0, keepdims=True)
        norm_ref[...] = jnp.sum(jnp.where(line == LINES - 1, given, 0.0), axis=0, keepdims=True)
        expand = ones_where(iota((slots, lines), 0) == line_of((slots, lines), 1))
        wide = dot(jnp.broadcast_to(asked, (SIDES, slots)).astype(BF16), expand)[:1]
        marks = ones_where((iota((block, lines), 0) + 1).astype(F32) == wide)
        partial = joined(dot(marks, in_three(given)), 3)
        sides = codes_ref[...] + jnp.where(iota((SIDES, cases), 0) == 0, asked, 0.0)
        for c in range(n_coarse):
            out_ref[c, :piece] = partial[c * piece : (c + 1) * piece]
            out_ref[c, piece:] = sides

    def coarse_sums(in_ref, rhs_ref, marks_ref, turned_ref, codes_ref):
        total = in_ref[0]
        for c in range(1, n_coarse):
            total = total + in_ref[c]
        rhs = total[:piece].astype(BF16)
        for k in range(chips):
            rhs_ref[k] = rhs
        codes_ref[...] = total[piece:]
        down = (iota((block, slots), 0) + 1).astype(F32)
        across = (iota((slots, block), 1) + 1).astype(F32)
        asked = jnp.concatenate([in_ref[c, piece : piece + 1] for c in range(n_coarse)], axis=0)
        turned = jnp.transpose(asked)
        for c in range(n_coarse):
            marks_ref[:, c * slots : (c + 1) * slots] = ones_where(down == asked[c : c + 1])
            turned_ref[c * slots : (c + 1) * slots] = ones_where(across == turned[:, c : c + 1])

    def product(mine, theirs):
        both = jnp.where(
            sub_index % 2 == 0, jnp.concatenate([mine, theirs], axis=1), jnp.concatenate([theirs, mine], axis=1)
        )
        return dot_t(coarse_inverse, both.reshape(rows, cases))

    def answer(share_ref, turned_ref, out_ref):
        out = joined(dot(turned_ref[...], in_three(share_ref[...])), 3)
        for c in range(n_coarse):
            out_ref[c] = out[c * slots : (c + 1) * slots]

    def reply(in_ref, given_ref, near_ref, out_ref):
        solved = in_ref[0]
        for c in range(1, n_coarse):
            solved = solved + in_ref[c]
        expand = ones_where(line_of((lines, slots), 0) == iota((lines, slots), 1))
        wide = dot(expand, solved.astype(BF16))
        line = iota((lines, cases), 0) & (LINES - 1)
        far = near_ref[...] + jnp.sum(jnp.where(line < CAPACITY, given_ref[...] * wide, 0.0), axis=0, keepdims=True)
        high, low = in_two(far)
        wide = jnp.where(line == CAPACITY, high.astype(F32), wide)
        out_ref[...] = jnp.where(line == CAPACITY + 1, low.astype(F32), wide).astype(BF16)

    def back(table_ref, in_ref, turned_ref, local_ref, image_ref, ahead_ref, behind_ref, curvature_ref):
        replies = in_ref[...]
        image_ref[...] = local_ref[...] + dot(turned_ref[...], replies)
        line = iota((lines, cases), 0) & (LINES - 1)
        curvature_ref[...] = jnp.sum(jnp.where(line >= CAPACITY, replies.astype(F32), 0.0), axis=0, keepdims=True)
        for e in range(edges):
            place = pl.ds(pl.multiple_of(table_ref[2, e] * width, width), width)

            @pl.when(table_ref[0, e] == 1)
            def _():
                ahead_ref[place, :] = image_ref[edge(e), :]

            @pl.when(table_ref[0, e] == 0)
            def _():
                behind_ref[place, :] = image_ref[edge(e), :]

    def coupled_rows(
        table_ref, image_ref, before_ref, next_ref, coupling_ref, old_ref, curvature_ref, norm_ref, jump_ref, out_ref
    ):
        for e in range(edges):
            place = pl.ds(pl.multiple_of(table_ref[1, e] * width, width), width)
            facing = jnp.where(table_ref[0, e] == 1, next_ref[place, :], before_ref[place, :])
            jump_ref[edge(e), :] = image_ref[edge(e), :] - facing
        pair = jnp.concatenate(in_two(2.0 * jump_ref[...]), axis=1)
        new = joined(dot(coupling_ref[...], pair), 2)
        line = iota((SIDES, cases), 0)
        tail = jnp.where(line == 0, curvature_ref[...], jnp.where(line == 1, norm_ref[...], 0.0))
        for c in range(n_coarse):
            out_ref[c, :prims] = old_ref[...]
            out_ref[c, prims : 2 * prims] = new
            out_ref[c, 2 * prims :] = tail

    def spread(in_ref, codes_ref, out_ref, scalars_ref):
        tail = in_ref[0, 2 * prims :]
        for c in range(1, n_coarse):
            tail = tail + in_ref[c, 2 * prims :]
        curvature, norm = tail[0:1], tail[1:2]
        alpha = norm / curvature
        line = iota((SIDES, cases), 0)
        scalars_ref[...] = jnp.where(line == 0, alpha, jnp.where(line == 1, curvature, norm))
        empty = jnp.zeros((ROOM - prims, cases), F32)
        parts = []
        for c in range(n_coarse):
            parts += [in_ref[c, :prims] - alpha * in_ref[c, prims : 2 * prims], empty]
        coupled = jnp.concatenate(parts, axis=0).astype(BF16)
        target = jnp.concatenate([codes_ref[k + 1 : k + 2, :] for k in range(n_coarse * ROOM // cases)], axis=1)
        total = n_coarse * slots
        marks = ones_where((iota((total, n_coarse * ROOM), 0) + 1).astype(F32) == target)
        out_ref[...] = dot(marks, coupled).astype(BF16)

    def owner_rows(here_ref, in_ref, marks_ref, weights_ref, rhs_ref):
        weights_ref[...] = dot(marks_ref[...], in_ref[...])
        start = pl.multiple_of(here_ref[0, 1] * piece, piece)
        rhs = weights_ref[pl.ds(start, piece), :].astype(BF16)
        for k in range(chips):
            rhs_ref[k] = rhs

    def second(residual_ref, jump_ref, scalars_ref, schur_ref, remainder_ref, sums_ref):
        remainder = residual_ref[...] - scalars_ref[0:1] * jump_ref[...]
        remainder_ref[...] = remainder
        twice = 2.0 * remainder
        near = jnp.sum(twice * dot(schur_ref[...], twice.astype(BF16)), axis=0, keepdims=True)
        line = iota((SIDES, cases), 0)
        norm = jnp.sum(remainder * remainder, axis=0, keepdims=True)
        sums_ref[...] = jnp.where(line == 0, near, jnp.where(line == 1, norm, 0.0))

    field = ((order, cases), F32)
    row = ((1, cases), F32)
    gathered = ((chips, piece, cases), BF16)
    scalars_shape = ((SIDES, cases), F32)
    owners = primal_owner.reshape(1, prims)
    start = load[0]
    from_before = lax.ppermute(start, "sub", to_next)
    from_next = lax.ppermute(start, "sub", to_before)
    slotted, turned, asked, codes, table, coupling_here, schur_here, load_here = run(
        set_up,
        [
            ((lines, order), BF16),
            ((order, lines), BF16),
            ((lines, slots), F32),
            scalars_shape,
            ((3, edges), I32),
            ((prims, order), BF16),
            ((order, order), BF16),
            ((order, cases), BF16),
        ],
        here, neighbour_sub, neighbour_edge, owners, primal_offset, coupling[0], schur[0], start,
        specs=[SMEM] * 3 + [VMEM] * 2 + [ANY] * 3,
        scratch=[pltpu.SemaphoreType.DMA((3,))],
    )
    residual, local, outgoing, near, old = run(
        first,
        [field, field, ((lines, cases), F32), row, ((prims, cases), F32)],
        table, neighbour_edge, load_here, from_before, from_next, schur_here, slotted, asked, coupling_here,
    )
    given = exchange(outgoing.reshape(n_sub, LINES, cases), "sub").reshape(lines, cases)
    outgoing, norm = run(owner_sums, [((n_coarse, piece + SIDES, cases), F32), row], given, codes)
    incoming = exchange(outgoing, "coarse")
    rhs, marks, marks_turned, codes = run(
        coarse_sums,
        [gathered, ((block, n_coarse * slots), BF16), ((n_coarse * slots, block), BF16), scalars_shape],
        incoming,
    )
    mine = exchange(rhs, "sub", same_core)
    theirs = lax.ppermute(mine, "sub", other_core)
    (outgoing,) = run(answer, [((n_coarse, slots, cases), F32)], product(mine, theirs), marks_turned)
    incoming = exchange(outgoing, "coarse")
    (outgoing,) = run(reply, [((lines, cases), BF16)], incoming, given, near)
    replies = exchange(outgoing.reshape(n_sub, LINES, cases), "sub").reshape(lines, cases)
    side = ((half * width, cases), F32)
    image, ahead, behind, curvature = run(back, [field, side, side, row], table, replies, turned, local)
    from_before = lax.ppermute(ahead, "sub", to_next)
    from_next = lax.ppermute(behind, "sub", to_before)
    image, outgoing = run(
        coupled_rows,
        [field, ((n_coarse, 2 * prims + SIDES, cases), F32)],
        table, image, from_before, from_next, coupling_here, old, curvature, norm,
    )
    incoming = exchange(outgoing, "coarse")
    outgoing, scalars = run(spread, [((n_coarse * slots, cases), BF16), scalars_shape], incoming, codes)
    incoming = exchange(outgoing.reshape(n_sub, n_coarse * CAPACITY, cases), "sub")
    incoming = incoming.transpose(1, 0, 2).reshape(n_coarse * slots, cases)
    weights, rhs = run(owner_rows, [((block, cases), F32), gathered], here, incoming, marks)
    mine = exchange(rhs, "sub", same_core)
    theirs = lax.ppermute(mine, "sub", other_core)
    remainder, sums = run(second, [field, scalars_shape], residual, image, scalars, schur_here)
    far = jnp.sum(weights * product(mine, theirs), axis=0)
    sums = jnp.stack([sums[0] + far, sums[1]])
    for groups in (columns, planes):
        wide = jnp.broadcast_to(sums[None], (len(groups[0]),) + sums.shape)
        sums = jnp.sum(exchange(wide, ("sub", "coarse"), groups), axis=0)
    alpha, curvature, norm = scalars[0], scalars[1], scalars[2]
    beta = sums[1] / norm
    step = sums[1] / (sums[0] - beta * beta * curvature)
    return ((alpha + step * beta) * residual + step * remainder)[None]


def solution(mesh):
    return jax.shard_map(
        body,
        mesh=mesh,
        in_specs=(
            P(("sub", "coarse"), None, None),
            P(("sub", "coarse"), None, None),
            P(("sub", "coarse"), None, None),
            P("coarse", "sub"),
            P(("sub", "coarse"), None),
            P(("sub", "coarse"), None),
            P(("sub", "coarse"), None, None),
            P(("sub", "coarse"), None),
        ),
        out_specs=P(("sub", "coarse"), None, None),
        check_vma=False,
    )
```

```python
import jax
import jax.numpy as jnp
from jax import lax
from jax.experimental import pallas as pl
from jax.experimental.pallas import tpu as pltpu
from jax.sharding import PartitionSpec as P

F32, BF16, I32 = jnp.float32, jnp.bfloat16, jnp.int32
CAPACITY = 2
LINES = 4
ROOM = 32
SIDES = 8


def dot(a, b):
    return jnp.dot(a, b, preferred_element_type=F32)


def dot_t(a, b):
    return lax.dot_general(a, b, (((0,), (0,)), ((), ())), preferred_element_type=F32)


def iota(shape, dim):
    return lax.broadcasted_iota(I32, shape, dim)


def ones_where(mask):
    return jnp.where(mask, 1.0, 0.0).astype(BF16)


def in_two(value):
    high = value.astype(BF16)
    return high, (value - high.astype(F32)).astype(BF16)


def in_three(value):
    high = value.astype(BF16)
    rest = value - high.astype(F32)
    middle = rest.astype(BF16)
    return jnp.concatenate([high, middle, (rest - middle.astype(F32)).astype(BF16)], axis=1)


def joined(parts, count):
    wide = parts.shape[1] // count
    out = parts[:, :wide]
    for k in range(1, count):
        out = out + parts[:, k * wide : (k + 1) * wide]
    return out


HBM = pl.BlockSpec(memory_space=pltpu.HBM)
SMEM = pl.BlockSpec(memory_space=pltpu.SMEM)
VMEM = pl.BlockSpec(memory_space=pltpu.VMEM)


def run(kernel, outs, *args, specs=None, scratch=()):
    def spec(x):
        return SMEM if jnp.issubdtype(x.dtype, jnp.integer) and x.size <= 32 and x.shape[1] <= 8 else VMEM

    return pl.pallas_call(
        kernel,
        out_shape=[jax.ShapeDtypeStruct(shape, dtype) for shape, dtype in outs],
        in_specs=specs or [spec(x) for x in args],
        out_specs=[SMEM if dtype == I32 else VMEM for _, dtype in outs],
        scratch_shapes=scratch,
        compiler_params=pltpu.CompilerParams(vmem_limit_bytes=32 * 1024 * 1024),
    )(*args)


def body(
    load,
    schur,
    coupling,
    coarse_inverse,
    neighbour_sub,
    neighbour_edge,
    primal_owner,
    primal_offset,
):
    _, order, cases = load.shape
    edges = neighbour_sub.shape[1]
    width = order // edges
    half = edges // 2
    rows, block = coarse_inverse.shape
    prims = primal_offset.shape[1]
    n_sub, n_coarse = lax.axis_size("sub"), lax.axis_size("coarse")
    piece = block // n_coarse
    slots = n_sub * CAPACITY
    lines = n_sub * LINES
    chips = n_sub // 2
    sub_index, coarse_index = lax.axis_index("sub"), lax.axis_index("coarse")
    here = jnp.stack([sub_index, coarse_index])[None].astype(I32)

    to_next = [(i, (i + 1) % n_sub) for i in range(n_sub)]
    to_before = [((i + 1) % n_sub, i) for i in range(n_sub)]
    other_core = [(i, i ^ 1) for i in range(n_sub)]
    same_core = [[2 * chip + core for chip in range(chips)] for core in range(2)]
    near_by = 2 * n_coarse
    devices = n_sub * n_coarse
    columns = [[start + k for k in range(near_by)] for start in range(0, devices, near_by)]
    planes = [[start + k for k in range(0, devices, near_by)] for start in range(near_by)]

    def exchange(blocks, axis, groups=None):
        return lax.all_to_all(blocks, axis, 0, 0, tiled=True, axis_index_groups=groups)

    def edge(e):
        return slice(e * width, (e + 1) * width)

    def set_up(
        here_ref, sub_hbm, edge_hbm, owner_hbm, offset_hbm, coupling_hbm, load_hbm, schur_hbm,
        slotted_ref, turned_ref, asked_ref, codes_ref, table_ref, coupling_ref, load_ref, schur_ref,
        sub_ref, edge_ref, owner_ref, offset_ref, sems,
    ):
        moves = [
            (sub_hbm, sub_ref),
            (edge_hbm, edge_ref),
            (owner_hbm, owner_ref),
            (offset_hbm, offset_ref),
            (coupling_hbm, coupling_ref),
            (load_hbm, load_ref),
            (schur_hbm, schur_ref),
        ]
        moves = [pltpu.make_async_copy(a, b, sems.at[k]) for k, (a, b) in enumerate(moves)]
        for move in moves:
            move.start()
        for move in moves[:4]:
            move.wait()
        faces = []
        for e in range(edges):
            side = lax.rem(lax.div(sub_ref[0, e], n_coarse) - here_ref[0, 0] + n_sub, n_sub) == 1
            faces.append(side.astype(I32))
        ahead = jnp.int32(0)
        for e in range(edges):
            place = jnp.int32(0)
            for other in range(edges):
                if other != e:
                    lower = (faces[other] == faces[e]) & (edge_ref[0, other] < edge_ref[0, e])
                    place = place + lower.astype(I32)
            table_ref[0, e] = faces[e]
            table_ref[1, e] = place
            table_ref[2, e] = faces[e] * ahead + (1 - faces[e]) * (e - ahead)
            table_ref[3, e] = edge_ref[0, e]
            ahead = ahead + faces[e]
        same = iota((prims, prims), 0) == iota((prims, prims), 1)
        owner_row = owner_ref[...]
        owner_col = jnp.sum(jnp.where(same, owner_row, 0), axis=1, keepdims=True)
        before = (owner_col == owner_row) & (iota((prims, prims), 0) < iota((prims, prims), 1))
        second = jnp.sum(jnp.where(before, 1, 0), axis=0, keepdims=True)
        line = iota((lines, prims), 0)
        placed = ones_where(line == owner_row * LINES + second)
        lane = iota((lines, slots), 1)
        asked = jnp.zeros((lines, slots), I32)
        for k in range(CAPACITY):
            named = (line >> 2 == owner_row) & (second == k)
            offset = jnp.sum(jnp.where(named, offset_ref[...] + 1, 0), axis=1, keepdims=True)
            asked = jnp.where(lane == k * n_sub + here_ref[0, 0], offset, asked)
        asked_ref[...] = jnp.where((iota((lines, slots), 0) & (LINES - 1)) == CAPACITY, asked, 0).astype(F32)
        target = owner_row * (n_coarse * CAPACITY) + second + CAPACITY * here_ref[0, 1] + 1
        far_lane = iota((prims, n_coarse * ROOM), 1) == iota((prims, n_coarse * ROOM), 0) + ROOM * here_ref[0, 1]
        target_col = jnp.sum(jnp.where(same, target, 0), axis=1, keepdims=True)
        codes = jnp.sum(jnp.where(far_lane, target_col, 0), axis=0, keepdims=True).astype(F32)
        codes_ref[...] = jnp.zeros((SIDES, cases), F32)
        for k in range(n_coarse * ROOM // cases):
            codes_ref[k + 1 : k + 2, :] = codes[:, k * cases : (k + 1) * cases]
        moves[4].wait()
        slotted_ref[...] = dot(placed, coupling_ref[...]).astype(BF16)
        turned_ref[...] = lax.dot_general(
            coupling_ref[...], placed, (((0,), (1,)), ((), ())), preferred_element_type=F32
        ).astype(BF16)
        moves[5].wait()
        moves[6].wait()

    def first(
        table_ref, load_ref, before_ref, next_ref, schur_ref, slotted_ref, asked_ref, coupling_ref,
        residual_ref, local_ref, out_ref, near_ref, old_ref,
    ):
        for e in range(edges):
            start = pl.multiple_of(table_ref[3, e] * width, width)
            ahead = next_ref[pl.ds(start, width), :].astype(F32)
            behind = before_ref[pl.ds(start, width), :].astype(F32)
            facing = jnp.where(table_ref[0, e] == 1, ahead, behind)
            residual_ref[edge(e), :] = load_ref[edge(e), :].astype(F32) - facing
        twice = 2.0 * residual_ref[...]
        jumps, rest = in_two(twice)
        terms = dot(slotted_ref[...], jumps)
        squares = jnp.sum(twice * twice, axis=0, keepdims=True) * 0.25
        line = iota((lines, cases), 0) & (LINES - 1)
        out_ref[...] = terms + asked_ref[...] + jnp.where(line == LINES - 1, squares, 0.0)
        local = dot(schur_ref[...], jumps)
        local_ref[...] = local
        near_ref[...] = jnp.sum(twice * local, axis=0, keepdims=True)
        old_ref[...] = joined(dot(coupling_ref[...], jnp.concatenate([jumps, rest], axis=1)), 2)

    def line_of(shape, dim):
        return (iota(shape, dim) & (LINES - 1)) * n_sub + (iota(shape, dim) >> 2)

    def owner_sums(in_ref, codes_ref, out_ref, norm_ref):
        given = in_ref[...]
        line = iota((lines, cases), 0) & (LINES - 1)
        asked = jnp.sum(jnp.where(line == CAPACITY, given, 0.0), axis=0, keepdims=True)
        norm_ref[...] = jnp.sum(jnp.where(line == LINES - 1, given, 0.0), axis=0, keepdims=True)
        expand = ones_where(iota((slots, lines), 0) == line_of((slots, lines), 1))
        wide = dot(jnp.broadcast_to(asked, (SIDES, slots)).astype(BF16), expand)[:1]
        marks = ones_where((iota((block, lines), 0) + 1).astype(F32) == wide)
        partial = joined(dot(marks, in_three(given)), 3)
        sides = codes_ref[...] + jnp.where(iota((SIDES, cases), 0) == 0, asked, 0.0)
        for c in range(n_coarse):
            out_ref[c, :piece] = partial[c * piece : (c + 1) * piece]
            out_ref[c, piece:] = sides

    def coarse_sums(in_ref, rhs_ref, sides_ref):
        total = in_ref[0]
        for c in range(1, n_coarse):
            total = total + in_ref[c]
        rhs = total[:piece].astype(BF16)
        for k in range(chips):
            rhs_ref[k] = rhs
        for c in range(n_coarse):
            sides_ref[c : c + 1] = in_ref[c, piece : piece + 1]
        sides_ref[n_coarse:] = total[piece:]

    def product(mine, theirs):
        both = jnp.where(
            sub_index % 2 == 0, jnp.concatenate([mine, theirs], axis=1), jnp.concatenate([theirs, mine], axis=1)
        )
        return dot_t(coarse_inverse, both.reshape(rows, cases))

    def answer(share_ref, sides_ref, out_ref):
        asked = jnp.transpose(sides_ref[:n_coarse])
        across = (iota((slots, block), 1) + 1).astype(F32)
        share = in_three(share_ref[...])
        for c in range(n_coarse):
            out_ref[c] = joined(dot(ones_where(across == asked[:, c : c + 1]), share), 3)

    def reply(in_ref, given_ref, near_ref, out_ref):
        solved = in_ref[0]
        for c in range(1, n_coarse):
            solved = solved + in_ref[c]
        expand = ones_where(line_of((lines, slots), 0) == iota((lines, slots), 1))
        wide = dot(expand, solved.astype(BF16))
        line = iota((lines, cases), 0) & (LINES - 1)
        far = near_ref[...] + jnp.sum(jnp.where(line < CAPACITY, given_ref[...] * wide, 0.0), axis=0, keepdims=True)
        high, low = in_two(far)
        wide = jnp.where(line == CAPACITY, high.astype(F32), wide)
        out_ref[...] = jnp.where(line == CAPACITY + 1, low.astype(F32), wide).astype(BF16)

    def back(table_ref, in_ref, turned_ref, local_ref, image_ref, ahead_ref, behind_ref, curvature_ref):
        replies = in_ref[...]
        image_ref[...] = local_ref[...] + dot(turned_ref[...], replies)
        line = iota((lines, cases), 0) & (LINES - 1)
        curvature_ref[...] = jnp.sum(jnp.where(line >= CAPACITY, replies.astype(F32), 0.0), axis=0, keepdims=True)
        for e in range(edges):
            place = pl.ds(pl.multiple_of(table_ref[2, e] * width, width), width)

            @pl.when(table_ref[0, e] == 1)
            def _():
                ahead_ref[place, :] = image_ref[edge(e), :]

            @pl.when(table_ref[0, e] == 0)
            def _():
                behind_ref[place, :] = image_ref[edge(e), :]

    def coupled_rows(
        table_ref, image_ref, before_ref, next_ref, coupling_ref, old_ref, curvature_ref, norm_ref, jump_ref, out_ref
    ):
        for e in range(edges):
            place = pl.ds(pl.multiple_of(table_ref[1, e] * width, width), width)
            facing = jnp.where(table_ref[0, e] == 1, next_ref[place, :], before_ref[place, :])
            jump_ref[edge(e), :] = image_ref[edge(e), :] - facing
        pair = jnp.concatenate(in_two(2.0 * jump_ref[...]), axis=1)
        new = joined(dot(coupling_ref[...], pair), 2)
        line = iota((SIDES, cases), 0)
        tail = jnp.where(line == 0, curvature_ref[...], jnp.where(line == 1, norm_ref[...], 0.0))
        for c in range(n_coarse):
            out_ref[c, :prims] = old_ref[...]
            out_ref[c, prims : 2 * prims] = new
            out_ref[c, 2 * prims :] = tail

    def spread(in_ref, sides_ref, out_ref, scalars_ref):
        tail = in_ref[0, 2 * prims :]
        for c in range(1, n_coarse):
            tail = tail + in_ref[c, 2 * prims :]
        curvature, norm = tail[0:1], tail[1:2]
        alpha = norm / curvature
        line = iota((SIDES, cases), 0)
        scalars_ref[...] = jnp.where(line == 0, alpha, jnp.where(line == 1, curvature, norm))
        empty = jnp.zeros((ROOM - prims, cases), F32)
        parts = []
        for c in range(n_coarse):
            parts += [in_ref[c, :prims] - alpha * in_ref[c, prims : 2 * prims], empty]
        coupled = jnp.concatenate(parts, axis=0).astype(BF16)
        target = jnp.concatenate([sides_ref[n_coarse + k + 1 : n_coarse + k + 2, :] for k in range(n_coarse * ROOM // cases)], axis=1)
        total = n_coarse * slots
        marks = ones_where((iota((total, n_coarse * ROOM), 0) + 1).astype(F32) == target)
        out_ref[...] = dot(marks, coupled).astype(BF16)

    def owner_rows(here_ref, in_ref, sides_ref, weights_ref, rhs_ref):
        down = (iota((block, slots), 0) + 1).astype(F32)
        marks = jnp.concatenate([ones_where(down == sides_ref[c : c + 1]) for c in range(n_coarse)], axis=1)
        weights_ref[...] = dot(marks, in_ref[...])
        start = pl.multiple_of(here_ref[0, 1] * piece, piece)
        rhs = weights_ref[pl.ds(start, piece), :].astype(BF16)
        for k in range(chips):
            rhs_ref[k] = rhs

    def second(residual_ref, jump_ref, scalars_ref, schur_ref, remainder_ref, sums_ref):
        remainder = residual_ref[...] - scalars_ref[0:1] * jump_ref[...]
        remainder_ref[...] = remainder
        twice = 2.0 * remainder
        near = jnp.sum(twice * dot(schur_ref[...], twice.astype(BF16)), axis=0, keepdims=True)
        line = iota((SIDES, cases), 0)
        norm = jnp.sum(remainder * remainder, axis=0, keepdims=True)
        sums_ref[...] = jnp.where(line == 0, near, jnp.where(line == 1, norm, 0.0))

    field = ((order, cases), F32)
    row = ((1, cases), F32)
    gathered = ((chips, piece, cases), BF16)
    scalars_shape = ((SIDES, cases), F32)
    owners = primal_owner.reshape(1, prims)
    start = load[0]
    from_before = lax.ppermute(start, "sub", to_next)
    from_next = lax.ppermute(start, "sub", to_before)
    slotted, turned, asked, codes, table, coupling_here, load_here, schur_here = run(
        set_up,
        [
            ((lines, order), BF16),
            ((order, lines), BF16),
            ((lines, slots), F32),
            scalars_shape,
            ((4, edges), I32),
            ((prims, order), BF16),
            ((order, cases), BF16),
            ((order, order), BF16),
        ],
        here, neighbour_sub, neighbour_edge, owners, primal_offset, coupling[0], start, schur[0],
        specs=[SMEM] + [HBM] * 7,
        scratch=[
            pltpu.SMEM((1, edges), I32),
            pltpu.SMEM((1, edges), I32),
            pltpu.VMEM((1, prims), I32),
            pltpu.VMEM((1, prims), I32),
            pltpu.SemaphoreType.DMA((7,)),
        ],
    )
    residual, local, outgoing, near, old = run(
        first,
        [field, field, ((lines, cases), F32), row, ((prims, cases), F32)],
        table, load_here, from_before, from_next, schur_here, slotted, asked, coupling_here,
    )
    given = exchange(outgoing.reshape(n_sub, LINES, cases), "sub").reshape(lines, cases)
    outgoing, norm = run(owner_sums, [((n_coarse, piece + SIDES, cases), F32), row], given, codes)
    incoming = exchange(outgoing, "coarse")
    rhs, sides = run(coarse_sums, [gathered, ((2 * SIDES, cases), F32)], incoming)
    mine = exchange(rhs, "sub", same_core)
    theirs = lax.ppermute(mine, "sub", other_core)
    (outgoing,) = run(answer, [((n_coarse, slots, cases), F32)], product(mine, theirs), sides)
    incoming = exchange(outgoing, "coarse")
    (outgoing,) = run(reply, [((lines, cases), BF16)], incoming, given, near)
    replies = exchange(outgoing.reshape(n_sub, LINES, cases), "sub").reshape(lines, cases)
    side = ((half * width, cases), F32)
    image, ahead, behind, curvature = run(back, [field, side, side, row], table, replies, turned, local)
    from_before = lax.ppermute(ahead, "sub", to_next)
    from_next = lax.ppermute(behind, "sub", to_before)
    image, outgoing = run(
        coupled_rows,
        [field, ((n_coarse, 2 * prims + SIDES, cases), F32)],
        table, image, from_before, from_next, coupling_here, old, curvature, norm,
    )
    incoming = exchange(outgoing, "coarse")
    outgoing, scalars = run(spread, [((n_coarse * slots, cases), BF16), scalars_shape], incoming, sides)
    incoming = exchange(outgoing.reshape(n_sub, n_coarse * CAPACITY, cases), "sub")
    incoming = incoming.transpose(1, 0, 2).reshape(n_coarse * slots, cases)
    weights, rhs = run(owner_rows, [((block, cases), F32), gathered], here, incoming, sides)
    mine = exchange(rhs, "sub", same_core)
    theirs = lax.ppermute(mine, "sub", other_core)
    remainder, sums = run(second, [field, scalars_shape], residual, image, scalars, schur[0])
    far = jnp.sum(weights * product(mine, theirs), axis=0)
    sums = jnp.stack([sums[0] + far, sums[1]])
    for groups in (columns, planes):
        wide = jnp.broadcast_to(sums[None], (len(groups[0]),) + sums.shape)
        sums = jnp.sum(exchange(wide, ("sub", "coarse"), groups), axis=0)
    alpha, curvature, norm = scalars[0], scalars[1], scalars[2]
    beta = sums[1] / norm
    step = sums[1] / (sums[0] - beta * beta * curvature)
    return ((alpha + step * beta) * residual + step * remainder)[None]


def solution(mesh):
    return jax.shard_map(
        body,
        mesh=mesh,
        in_specs=(
            P(("sub", "coarse"), None, None),
            P(("sub", "coarse"), None, None),
            P(("sub", "coarse"), None, None),
            P("coarse", "sub"),
            P(("sub", "coarse"), None),
            P(("sub", "coarse"), None),
            P(("sub", "coarse"), None, None),
            P(("sub", "coarse"), None),
        ),
        out_specs=P(("sub", "coarse"), None, None),
        check_vma=False,
    )
```

```python
import jax
import jax.numpy as jnp
from jax import lax
from jax.experimental import pallas as pl
from jax.experimental.pallas import tpu as pltpu
from jax.sharding import PartitionSpec as P

F32, BF16, I32 = jnp.float32, jnp.bfloat16, jnp.int32
CAPACITY = 2
LINES = 4
ROOM = 32
SIDES = 8


def dot(a, b):
    return jnp.dot(a, b, preferred_element_type=F32)


def dot_t(a, b):
    return lax.dot_general(a, b, (((0,), (0,)), ((), ())), preferred_element_type=F32)


def iota(shape, dim):
    return lax.broadcasted_iota(I32, shape, dim)


def ones_where(mask):
    return jnp.where(mask, 1.0, 0.0).astype(BF16)


def in_two(value):
    high = value.astype(BF16)
    return high, (value - high.astype(F32)).astype(BF16)


def in_three(value):
    high = value.astype(BF16)
    rest = value - high.astype(F32)
    middle = rest.astype(BF16)
    return jnp.concatenate([high, middle, (rest - middle.astype(F32)).astype(BF16)], axis=1)


def joined(parts, count):
    wide = parts.shape[1] // count
    out = parts[:, :wide]
    for k in range(1, count):
        out = out + parts[:, k * wide : (k + 1) * wide]
    return out


HBM = pl.BlockSpec(memory_space=pltpu.HBM)
SMEM = pl.BlockSpec(memory_space=pltpu.SMEM)
VMEM = pl.BlockSpec(memory_space=pltpu.VMEM)


def run(kernel, outs, *args, specs=None, scratch=()):
    def spec(x):
        return SMEM if jnp.issubdtype(x.dtype, jnp.integer) and x.shape[1] <= 8 else VMEM

    return pl.pallas_call(
        kernel,
        out_shape=[jax.ShapeDtypeStruct(shape, dtype) for shape, dtype in outs],
        in_specs=specs or [spec(x) for x in args],
        out_specs=[SMEM if dtype == I32 else VMEM for _, dtype in outs],
        scratch_shapes=scratch,
        compiler_params=pltpu.CompilerParams(vmem_limit_bytes=32 * 1024 * 1024),
    )(*args)


def body(
    load,
    schur,
    coupling,
    coarse_inverse,
    neighbour_sub,
    neighbour_edge,
    primal_owner,
    primal_offset,
):
    _, order, cases = load.shape
    edges = neighbour_sub.shape[1]
    width = order // edges
    half = edges // 2
    rows, block = coarse_inverse.shape
    prims = primal_offset.shape[1]
    n_sub, n_coarse = lax.axis_size("sub"), lax.axis_size("coarse")
    piece = block // n_coarse
    slots = n_sub * CAPACITY
    lines = n_sub * LINES
    chips = n_sub // 2
    sub_index, coarse_index = lax.axis_index("sub"), lax.axis_index("coarse")
    here = jnp.stack([sub_index, coarse_index])[None].astype(I32)

    to_next = [(i, (i + 1) % n_sub) for i in range(n_sub)]
    to_before = [((i + 1) % n_sub, i) for i in range(n_sub)]
    other_core = [(i, i ^ 1) for i in range(n_sub)]
    same_core = [[2 * chip + core for chip in range(chips)] for core in range(2)]
    near_by = 2 * n_coarse
    devices = n_sub * n_coarse
    columns = [[start + k for k in range(near_by)] for start in range(0, devices, near_by)]
    planes = [[start + k for k in range(0, devices, near_by)] for start in range(near_by)]

    def exchange(blocks, axis, groups=None):
        return lax.all_to_all(blocks, axis, 0, 0, tiled=True, axis_index_groups=groups)

    def edge(e):
        return slice(e * width, (e + 1) * width)

    def set_up(
        ints_ref, row_ref, coupling_ref, load_ref, slotted_ref, turned_ref, asked_ref, codes_ref, table_ref, here_ref
    ):
        here_ref[...] = load_ref[...]
        sub_at, coarse_at = ints_ref[0, 0], ints_ref[0, 1]
        named_sub = [ints_ref[0, 2 + e] for e in range(edges)]
        named_edge = [ints_ref[0, 2 + edges + e] for e in range(edges)]
        owner_row = row_ref[:, 2 + 2 * edges : 2 + 2 * edges + prims]
        offset_row = row_ref[:, 2 + 2 * edges + prims :]
        faces = []
        for e in range(edges):
            side = lax.rem(lax.div(named_sub[e], n_coarse) - sub_at + n_sub, n_sub) == 1
            faces.append(side.astype(I32))
        ahead = jnp.int32(0)
        for e in range(edges):
            place = jnp.int32(0)
            for other in range(edges):
                if other != e:
                    lower = (faces[other] == faces[e]) & (named_edge[other] < named_edge[e])
                    place = place + lower.astype(I32)
            table_ref[0, e] = faces[e]
            table_ref[1, e] = place
            table_ref[2, e] = faces[e] * ahead + (1 - faces[e]) * (e - ahead)
            table_ref[3, e] = named_edge[e]
            table_ref[4, e] = coarse_at
            ahead = ahead + faces[e]
        same = iota((prims, prims), 0) == iota((prims, prims), 1)
        owner_col = jnp.sum(jnp.where(same, owner_row, 0), axis=1, keepdims=True)
        before = (owner_col == owner_row) & (iota((prims, prims), 0) < iota((prims, prims), 1))
        second = jnp.sum(jnp.where(before, 1, 0), axis=0, keepdims=True)
        line = iota((lines, prims), 0)
        placed = ones_where(line == owner_row * LINES + second)
        lane = iota((lines, slots), 1)
        asked = jnp.zeros((lines, slots), I32)
        for k in range(CAPACITY):
            named = (line >> 2 == owner_row) & (second == k)
            offset = jnp.sum(jnp.where(named, offset_row + 1, 0), axis=1, keepdims=True)
            asked = jnp.where(lane == k * n_sub + sub_at, offset, asked)
        asked_ref[...] = jnp.where((iota((lines, slots), 0) & (LINES - 1)) == CAPACITY, asked, 0).astype(F32)
        target = owner_row * (n_coarse * CAPACITY) + second + CAPACITY * coarse_at + 1
        far_lane = iota((prims, n_coarse * ROOM), 1) == iota((prims, n_coarse * ROOM), 0) + ROOM * coarse_at
        target_col = jnp.sum(jnp.where(same, target, 0), axis=1, keepdims=True)
        codes = jnp.sum(jnp.where(far_lane, target_col, 0), axis=0, keepdims=True).astype(F32)
        codes_ref[...] = jnp.zeros((SIDES, cases), F32)
        for k in range(n_coarse * ROOM // cases):
            codes_ref[k + 1 : k + 2, :] = codes[:, k * cases : (k + 1) * cases]
        slotted_ref[...] = dot(placed, coupling_ref[...]).astype(BF16)
        turned_ref[...] = lax.dot_general(
            coupling_ref[...], placed, (((0,), (1,)), ((), ())), preferred_element_type=F32
        ).astype(BF16)

    def first(table_ref, load_ref, before_ref, next_ref, slotted_ref, asked_ref, residual_ref, out_ref):
        for e in range(edges):
            start = pl.multiple_of(table_ref[3, e] * width, width)
            ahead = next_ref[pl.ds(start, width), :].astype(F32)
            behind = before_ref[pl.ds(start, width), :].astype(F32)
            facing = jnp.where(table_ref[0, e] == 1, ahead, behind)
            residual_ref[edge(e), :] = load_ref[edge(e), :].astype(F32) - facing
        twice = 2.0 * residual_ref[...]
        squares = jnp.sum(twice * twice, axis=0, keepdims=True) * 0.25
        line = iota((lines, cases), 0) & (LINES - 1)
        terms = dot(slotted_ref[...], twice.astype(BF16))
        out_ref[...] = terms + asked_ref[...] + jnp.where(line == LINES - 1, squares, 0.0)

    def springs(residual_ref, schur_ref, after_ref, local_ref, near_ref):
        twice = 2.0 * residual_ref[...]
        local = dot(schur_ref[...], twice.astype(BF16))
        local_ref[...] = local
        near_ref[...] = jnp.sum(twice * local, axis=0, keepdims=True)

    def coupled(residual_ref, coupling_ref, after_ref, old_ref):
        old_ref[...] = joined(dot(coupling_ref[...], jnp.concatenate(in_two(2.0 * residual_ref[...]), axis=1)), 2)

    def line_of(shape, dim):
        return (iota(shape, dim) & (LINES - 1)) * n_sub + (iota(shape, dim) >> 2)

    def owner_sums(in_ref, codes_ref, out_ref, norm_ref):
        given = in_ref[...]
        line = iota((lines, cases), 0) & (LINES - 1)
        asked = jnp.sum(jnp.where(line == CAPACITY, given, 0.0), axis=0, keepdims=True)
        norm_ref[...] = jnp.sum(jnp.where(line == LINES - 1, given, 0.0), axis=0, keepdims=True)
        expand = ones_where(iota((slots, lines), 0) == line_of((slots, lines), 1))
        wide = dot(jnp.broadcast_to(asked, (SIDES, slots)).astype(BF16), expand)[:1]
        marks = ones_where((iota((block, lines), 0) + 1).astype(F32) == wide)
        partial = joined(dot(marks, in_three(given)), 3)
        sides = codes_ref[...] + jnp.where(iota((SIDES, cases), 0) == 0, asked, 0.0)
        for c in range(n_coarse):
            out_ref[c, :piece] = partial[c * piece : (c + 1) * piece]
            out_ref[c, piece:] = sides

    def coarse_sums(in_ref, rhs_ref, sides_ref):
        total = in_ref[0]
        for c in range(1, n_coarse):
            total = total + in_ref[c]
        rhs = total[:piece].astype(BF16)
        for k in range(chips):
            rhs_ref[k] = rhs
        for c in range(n_coarse):
            sides_ref[c : c + 1] = in_ref[c, piece : piece + 1]
        sides_ref[n_coarse:] = total[piece:]

    def product(mine, theirs):
        both = jnp.where(
            sub_index % 2 == 0, jnp.concatenate([mine, theirs], axis=1), jnp.concatenate([theirs, mine], axis=1)
        )
        return dot_t(coarse_inverse, both.reshape(rows, cases))

    def answer(share_ref, sides_ref, out_ref):
        asked = jnp.transpose(sides_ref[:n_coarse])
        across = (iota((slots, block), 1) + 1).astype(F32)
        share = in_three(share_ref[...])
        for c in range(n_coarse):
            out_ref[c] = joined(dot(ones_where(across == asked[:, c : c + 1]), share), 3)

    def reply(in_ref, given_ref, near_ref, out_ref):
        solved = in_ref[0]
        for c in range(1, n_coarse):
            solved = solved + in_ref[c]
        expand = ones_where(line_of((lines, slots), 0) == iota((lines, slots), 1))
        wide = dot(expand, solved.astype(BF16))
        line = iota((lines, cases), 0) & (LINES - 1)
        far = near_ref[...] + jnp.sum(jnp.where(line < CAPACITY, given_ref[...] * wide, 0.0), axis=0, keepdims=True)
        high, low = in_two(far)
        wide = jnp.where(line == CAPACITY, high.astype(F32), wide)
        out_ref[...] = jnp.where(line == CAPACITY + 1, low.astype(F32), wide).astype(BF16)

    def back(table_ref, in_ref, turned_ref, local_ref, image_ref, ahead_ref, behind_ref, curvature_ref):
        replies = in_ref[...]
        image_ref[...] = local_ref[...] + dot(turned_ref[...], replies)
        line = iota((lines, cases), 0) & (LINES - 1)
        curvature_ref[...] = jnp.sum(jnp.where(line >= CAPACITY, replies.astype(F32), 0.0), axis=0, keepdims=True)
        for e in range(edges):
            place = pl.ds(pl.multiple_of(table_ref[2, e] * width, width), width)

            @pl.when(table_ref[0, e] == 1)
            def _():
                ahead_ref[place, :] = image_ref[edge(e), :]

            @pl.when(table_ref[0, e] == 0)
            def _():
                behind_ref[place, :] = image_ref[edge(e), :]

    def coupled_rows(
        table_ref, image_ref, before_ref, next_ref, coupling_ref, old_ref, curvature_ref, norm_ref, jump_ref, out_ref
    ):
        for e in range(edges):
            place = pl.ds(pl.multiple_of(table_ref[1, e] * width, width), width)
            facing = jnp.where(table_ref[0, e] == 1, next_ref[place, :], before_ref[place, :])
            jump_ref[edge(e), :] = image_ref[edge(e), :] - facing
        pair = jnp.concatenate(in_two(2.0 * jump_ref[...]), axis=1)
        new = joined(dot(coupling_ref[...], pair), 2)
        line = iota((SIDES, cases), 0)
        tail = jnp.where(line == 0, curvature_ref[...], jnp.where(line == 1, norm_ref[...], 0.0))
        for c in range(n_coarse):
            out_ref[c, :prims] = old_ref[...]
            out_ref[c, prims : 2 * prims] = new
            out_ref[c, 2 * prims :] = tail

    def spread(in_ref, sides_ref, out_ref, scalars_ref):
        tail = in_ref[0, 2 * prims :]
        for c in range(1, n_coarse):
            tail = tail + in_ref[c, 2 * prims :]
        curvature, norm = tail[0:1], tail[1:2]
        alpha = norm / curvature
        line = iota((SIDES, cases), 0)
        scalars_ref[...] = jnp.where(line == 0, alpha, jnp.where(line == 1, curvature, norm))
        empty = jnp.zeros((ROOM - prims, cases), F32)
        parts = []
        for c in range(n_coarse):
            parts += [in_ref[c, :prims] - alpha * in_ref[c, prims : 2 * prims], empty]
        coupled = jnp.concatenate(parts, axis=0).astype(BF16)
        target = jnp.concatenate([sides_ref[n_coarse + k + 1 : n_coarse + k + 2, :] for k in range(n_coarse * ROOM // cases)], axis=1)
        total = n_coarse * slots
        marks = ones_where((iota((total, n_coarse * ROOM), 0) + 1).astype(F32) == target)
        out_ref[...] = dot(marks, coupled).astype(BF16)

    def owner_rows(table_ref, in_ref, sides_ref, weights_ref, rhs_ref):
        down = (iota((block, slots), 0) + 1).astype(F32)
        marks = jnp.concatenate([ones_where(down == sides_ref[c : c + 1]) for c in range(n_coarse)], axis=1)
        weights_ref[...] = dot(marks, in_ref[...])
        start = pl.multiple_of(table_ref[4, 0] * piece, piece)
        rhs = weights_ref[pl.ds(start, piece), :].astype(BF16)
        for k in range(chips):
            rhs_ref[k] = rhs

    def second(residual_ref, jump_ref, scalars_ref, schur_ref, remainder_ref, sums_ref):
        remainder = residual_ref[...] - scalars_ref[0:1] * jump_ref[...]
        remainder_ref[...] = remainder
        twice = 2.0 * remainder
        near = jnp.sum(twice * dot(schur_ref[...], twice.astype(BF16)), axis=0, keepdims=True)
        line = iota((SIDES, cases), 0)
        norm = jnp.sum(remainder * remainder, axis=0, keepdims=True)
        sums_ref[...] = jnp.where(line == 0, near, jnp.where(line == 1, norm, 0.0))

    field = ((order, cases), F32)
    row = ((1, cases), F32)
    gathered = ((chips, piece, cases), BF16)
    scalars_shape = ((SIDES, cases), F32)
    ints = jnp.concatenate(
        [here, neighbour_sub, neighbour_edge, primal_owner.reshape(1, prims), primal_offset], axis=1
    )
    start = load[0]
    from_before = lax.ppermute(start, "sub", to_next)
    from_next = lax.ppermute(start, "sub", to_before)
    slotted, turned, asked, codes, table, start = run(
        set_up,
        [
            ((lines, order), BF16),
            ((order, lines), BF16),
            ((lines, slots), F32),
            scalars_shape,
            ((5, edges), I32),
            ((order, cases), BF16),
        ],
        ints, ints, coupling[0], start,
        specs=[SMEM, VMEM, VMEM, VMEM],
    )
    residual, outgoing = run(
        first, [field, ((lines, cases), F32)], table, start, from_before, from_next, slotted, asked
    )
    given = exchange(outgoing.reshape(n_sub, LINES, cases), "sub").reshape(lines, cases)
    outgoing, norm = run(owner_sums, [((n_coarse, piece + SIDES, cases), F32), row], given, codes)
    incoming = exchange(outgoing, "coarse")
    rhs, sides = run(coarse_sums, [gathered, ((2 * SIDES, cases), F32)], incoming)
    mine = exchange(rhs, "sub", same_core)
    theirs = lax.ppermute(mine, "sub", other_core)
    local, near = run(springs, [field, row], residual, schur[0], mine, specs=[VMEM, VMEM, HBM])
    (outgoing,) = run(answer, [((n_coarse, slots, cases), F32)], product(mine, theirs), sides)
    incoming = exchange(outgoing, "coarse")
    (outgoing,) = run(reply, [((lines, cases), BF16)], incoming, given, near)
    replies = exchange(outgoing.reshape(n_sub, LINES, cases), "sub").reshape(lines, cases)
    side = ((half * width, cases), F32)
    image, ahead, behind, curvature = run(back, [field, side, side, row], table, replies, turned, local)
    from_before = lax.ppermute(ahead, "sub", to_next)
    from_next = lax.ppermute(behind, "sub", to_before)
    (old,) = run(coupled, [((prims, cases), F32)], residual, coupling[0], ahead, specs=[VMEM, VMEM, HBM])
    image, outgoing = run(
        coupled_rows,
        [field, ((n_coarse, 2 * prims + SIDES, cases), F32)],
        table, image, from_before, from_next, coupling[0], old, curvature, norm,
    )
    incoming = exchange(outgoing, "coarse")
    outgoing, scalars = run(spread, [((n_coarse * slots, cases), BF16), scalars_shape], incoming, sides)
    incoming = exchange(outgoing.reshape(n_sub, n_coarse * CAPACITY, cases), "sub")
    incoming = incoming.transpose(1, 0, 2).reshape(n_coarse * slots, cases)
    weights, rhs = run(owner_rows, [((block, cases), F32), gathered], table, incoming, sides)
    mine = exchange(rhs, "sub", same_core)
    theirs = lax.ppermute(mine, "sub", other_core)
    remainder, sums = run(second, [field, scalars_shape], residual, image, scalars, schur[0])
    far = jnp.sum(weights * product(mine, theirs), axis=0)
    sums = jnp.stack([sums[0] + far, sums[1]])
    for groups in (columns, planes):
        wide = jnp.broadcast_to(sums[None], (len(groups[0]),) + sums.shape)
        sums = jnp.sum(exchange(wide, ("sub", "coarse"), groups), axis=0)
    alpha, curvature, norm = scalars[0], scalars[1], scalars[2]
    beta = sums[1] / norm
    step = sums[1] / (sums[0] - beta * beta * curvature)
    return ((alpha + step * beta) * residual + step * remainder)[None]


def solution(mesh):
    return jax.shard_map(
        body,
        mesh=mesh,
        in_specs=(
            P(("sub", "coarse"), None, None),
            P(("sub", "coarse"), None, None),
            P(("sub", "coarse"), None, None),
            P("coarse", "sub"),
            P(("sub", "coarse"), None),
            P(("sub", "coarse"), None),
            P(("sub", "coarse"), None, None),
            P(("sub", "coarse"), None),
        ),
        out_specs=P(("sub", "coarse"), None, None),
        check_vma=False,
    )
```

```python
import jax
import jax.numpy as jnp
from jax import lax
from jax.experimental import pallas as pl
from jax.experimental.pallas import tpu as pltpu
from jax.sharding import PartitionSpec as P

F32, BF16, I32 = jnp.float32, jnp.bfloat16, jnp.int32
CAPACITY = 2
LINES = 4
ROOM = 32
SIDES = 8
REPLIES = 8
NOBODY = -1000.0


def dot(a, b):
    return jnp.dot(a, b, preferred_element_type=F32)


def dot_t(a, b):
    return lax.dot_general(a, b, (((0,), (0,)), ((), ())), preferred_element_type=F32)


def iota(shape, dim):
    return lax.broadcasted_iota(I32, shape, dim)


def ones_where(mask):
    return jnp.where(mask, 1.0, 0.0).astype(BF16)


def in_two(value):
    high = value.astype(BF16)
    return high, (value - high.astype(F32)).astype(BF16)


def in_three(value):
    high = value.astype(BF16)
    rest = value - high.astype(F32)
    middle = rest.astype(BF16)
    return jnp.concatenate([high, middle, (rest - middle.astype(F32)).astype(BF16)], axis=1)


def joined(parts, count):
    wide = parts.shape[1] // count
    out = parts[:, :wide]
    for k in range(1, count):
        out = out + parts[:, k * wide : (k + 1) * wide]
    return out


HBM = pl.BlockSpec(memory_space=pltpu.HBM)
SMEM = pl.BlockSpec(memory_space=pltpu.SMEM)
VMEM = pl.BlockSpec(memory_space=pltpu.VMEM)


def run(kernel, outs, *args, specs=None, scratch=()):
    def spec(x):
        return SMEM if jnp.issubdtype(x.dtype, jnp.integer) and x.shape[1] <= 8 else VMEM

    return pl.pallas_call(
        kernel,
        out_shape=[jax.ShapeDtypeStruct(shape, dtype) for shape, dtype in outs],
        in_specs=specs or [spec(x) for x in args],
        out_specs=[SMEM if dtype == I32 else VMEM for _, dtype in outs],
        scratch_shapes=scratch,
        compiler_params=pltpu.CompilerParams(vmem_limit_bytes=32 * 1024 * 1024),
    )(*args)


def body(
    load,
    schur,
    coupling,
    coarse_inverse,
    neighbour_sub,
    neighbour_edge,
    primal_owner,
    primal_offset,
):
    _, order, cases = load.shape
    edges = neighbour_sub.shape[1]
    width = order // edges
    half = edges // 2
    rows, block = coarse_inverse.shape
    prims = primal_offset.shape[1]
    n_sub, n_coarse = lax.axis_size("sub"), lax.axis_size("coarse")
    piece = block // n_coarse
    slots = n_sub * CAPACITY
    lines = n_sub * LINES
    chips = n_sub // 2
    sub_index, coarse_index = lax.axis_index("sub"), lax.axis_index("coarse")
    here = jnp.stack([sub_index, coarse_index])[None].astype(I32)

    to_next = [(i, (i + 1) % n_sub) for i in range(n_sub)]
    to_before = [((i + 1) % n_sub, i) for i in range(n_sub)]
    other_core = [(i, i ^ 1) for i in range(n_sub)]
    same_core = [[2 * chip + core for chip in range(chips)] for core in range(2)]
    near_by = 2 * n_coarse
    devices = n_sub * n_coarse
    columns = [[start + k for k in range(near_by)] for start in range(0, devices, near_by)]
    planes = [[start + k for k in range(0, devices, near_by)] for start in range(near_by)]

    def exchange(blocks, axis, groups=None):
        return lax.all_to_all(blocks, axis, 0, 0, tiled=True, axis_index_groups=groups)

    def edge(e):
        return slice(e * width, (e + 1) * width)

    def set_up(
        ints_ref, row_ref, coupling_ref, load_ref,
        slotted_ref, turned_ref, asked_ref, codes_ref, table_ref, here_ref, ahead_ref, behind_ref,
    ):
        here_ref[...] = load_ref[...]
        sub_at, coarse_at = ints_ref[0, 0], ints_ref[0, 1]
        named_sub = [ints_ref[0, 2 + e] for e in range(edges)]
        named_edge = [ints_ref[0, 2 + edges + e] for e in range(edges)]
        owner_row = row_ref[:, 2 + 2 * edges : 2 + 2 * edges + prims]
        offset_row = row_ref[:, 2 + 2 * edges + prims :]
        faces = []
        for e in range(edges):
            side = lax.rem(lax.div(named_sub[e], n_coarse) - sub_at + n_sub, n_sub) == 1
            faces.append(side.astype(I32))
        ahead = jnp.int32(0)
        for e in range(edges):
            place = jnp.int32(0)
            for other in range(edges):
                if other != e:
                    lower = (faces[other] == faces[e]) & (named_edge[other] < named_edge[e])
                    place = place + lower.astype(I32)
            table_ref[0, e] = faces[e]
            table_ref[1, e] = place
            table_ref[2, e] = faces[e] * ahead + (1 - faces[e]) * (e - ahead)
            table_ref[3, e] = named_edge[e]
            table_ref[4, e] = coarse_at
            ahead = ahead + faces[e]
        same = iota((prims, prims), 0) == iota((prims, prims), 1)
        owner_col = jnp.sum(jnp.where(same, owner_row, 0), axis=1, keepdims=True)
        before = (owner_col == owner_row) & (iota((prims, prims), 0) < iota((prims, prims), 1))
        second = jnp.sum(jnp.where(before, 1, 0), axis=0, keepdims=True)
        line = iota((lines, prims), 0)
        placed = ones_where(line == owner_row * LINES + second)
        lane = iota((lines, slots), 1)
        asked = jnp.zeros((lines, slots), I32)
        for k in range(CAPACITY):
            named = (line >> 2 == owner_row) & (second == k)
            offset = jnp.sum(jnp.where(named, offset_row + 1, 0), axis=1, keepdims=True)
            asked = jnp.where(lane == k * n_sub + sub_at, offset, asked)
        asked_ref[...] = jnp.where((iota((lines, slots), 0) & (LINES - 1)) == CAPACITY, asked, 0).astype(F32)
        target = owner_row * (n_coarse * CAPACITY) + second + CAPACITY * coarse_at + 1
        far_lane = iota((prims, n_coarse * ROOM), 1) == iota((prims, n_coarse * ROOM), 0) + ROOM * coarse_at
        target_col = jnp.sum(jnp.where(same, target, 0), axis=1, keepdims=True)
        codes = jnp.sum(jnp.where(far_lane, target_col, 0), axis=0, keepdims=True).astype(F32)
        codes_ref[...] = jnp.zeros((SIDES, cases), F32)
        for k in range(n_coarse * ROOM // cases):
            codes_ref[k + 1 : k + 2, :] = codes[:, k * cases : (k + 1) * cases]
        slotted_ref[...] = dot(placed, coupling_ref[...]).astype(BF16)
        wide_eye = iota((prims, cases), 0) == iota((prims, cases), 1)
        turned_ref[...] = dot_t(coupling_ref[...], ones_where(wide_eye)).astype(BF16)
        line_col = jnp.sum(jnp.where(same, owner_row * REPLIES + second, 0), axis=1, keepdims=True)
        line_row = jnp.sum(jnp.where(wide_eye, line_col, 0), axis=0, keepdims=True).astype(F32)
        line_row = jnp.where(iota((1, cases), 1) < prims, line_row, NOBODY)
        lane = iota((1, half * width), 1)
        for side, ref in ((1, ahead_ref), (0, behind_ref)):
            target = jnp.zeros((1, half * width), I32)
            for place in range(half):
                at = jnp.int32(0)
                for e in range(edges):
                    at = at + e * ((faces[e] == side) & (table_ref[2, e] == place)).astype(I32)
                target = jnp.where(lane // width == place, at * width + lane % width, target)
            chosen = ones_where(iota((order, half * width), 0) == target)
            columns_there = dot(coupling_ref[...], chosen)
            for k in range(half * width // cases):
                ref[k * prims : (k + 1) * prims] = columns_there[:, k * cases : (k + 1) * cases]
            ref[half * width // cases * prims :] = jnp.broadcast_to(line_row, (SIDES, cases))

    def first(table_ref, load_ref, before_ref, next_ref, slotted_ref, asked_ref, residual_ref, out_ref):
        for e in range(edges):
            start = pl.multiple_of(table_ref[3, e] * width, width)
            ahead = next_ref[pl.ds(start, width), :].astype(F32)
            behind = before_ref[pl.ds(start, width), :].astype(F32)
            facing = jnp.where(table_ref[0, e] == 1, ahead, behind)
            residual_ref[edge(e), :] = load_ref[edge(e), :].astype(F32) - facing
        twice = 2.0 * residual_ref[...]
        squares = jnp.sum(twice * twice, axis=0, keepdims=True) * 0.25
        line = iota((lines, cases), 0) & (LINES - 1)
        terms = dot(slotted_ref[...], twice.astype(BF16))
        out_ref[...] = terms + asked_ref[...] + jnp.where(line == LINES - 1, squares, 0.0)

    def springs(
        table_ref, residual_ref, schur_ref, ahead_in, behind_in, after_ref, local_ref, near_ref, ahead_ref, behind_ref
    ):
        twice = 2.0 * residual_ref[...]
        local_ref[...] = dot(schur_ref[...], twice.astype(BF16))
        near_ref[...] = jnp.sum(twice * local_ref[...], axis=0, keepdims=True)
        ahead_ref[half * width :] = ahead_in[...]
        behind_ref[half * width :] = behind_in[...]
        for e in range(edges):
            place = pl.ds(pl.multiple_of(table_ref[2, e] * width, width), width)

            @pl.when(table_ref[0, e] == 1)
            def _():
                ahead_ref[place, :] = local_ref[edge(e), :]

            @pl.when(table_ref[0, e] == 0)
            def _():
                behind_ref[place, :] = local_ref[edge(e), :]

    def line_of(shape, dim):
        return (iota(shape, dim) & (LINES - 1)) * n_sub + (iota(shape, dim) >> 2)

    def owner_sums(in_ref, codes_ref, out_ref, norm_ref):
        given = in_ref[...]
        line = iota((lines, cases), 0) & (LINES - 1)
        asked = jnp.sum(jnp.where(line == CAPACITY, given, 0.0), axis=0, keepdims=True)
        norm_ref[...] = jnp.sum(jnp.where(line == LINES - 1, given, 0.0), axis=0, keepdims=True)
        expand = ones_where(iota((slots, lines), 0) == line_of((slots, lines), 1))
        wide = dot(jnp.broadcast_to(asked, (SIDES, slots)).astype(BF16), expand)[:1]
        marks = ones_where((iota((block, lines), 0) + 1).astype(F32) == wide)
        partial = joined(dot(marks, in_three(given)), 3)
        sides = codes_ref[...] + jnp.where(iota((SIDES, cases), 0) == 0, asked, 0.0)
        for c in range(n_coarse):
            out_ref[c, :piece] = partial[c * piece : (c + 1) * piece]
            out_ref[c, piece:] = sides

    def coarse_sums(in_ref, rhs_ref, sides_ref):
        total = in_ref[0]
        for c in range(1, n_coarse):
            total = total + in_ref[c]
        rhs = total[:piece].astype(BF16)
        for k in range(chips):
            rhs_ref[k] = rhs
        for c in range(n_coarse):
            sides_ref[c : c + 1] = in_ref[c, piece : piece + 1]
        sides_ref[n_coarse:] = total[piece:]

    def product(mine, theirs):
        both = jnp.where(
            sub_index % 2 == 0, jnp.concatenate([mine, theirs], axis=1), jnp.concatenate([theirs, mine], axis=1)
        )
        return dot_t(coarse_inverse, both.reshape(rows, cases))

    def answer(share_ref, sides_ref, after_ref, out_ref):
        asked = jnp.transpose(sides_ref[:n_coarse])
        across = (iota((slots, block), 1) + 1).astype(F32)
        share = in_three(share_ref[...])
        for c in range(n_coarse):
            out_ref[c] = joined(dot(ones_where(across == asked[:, c : c + 1]), share), 3)

    def reply(in_ref, given_ref, near_ref, out_ref):
        solved = in_ref[0]
        for c in range(1, n_coarse):
            solved = solved + in_ref[c]
        total = n_sub * REPLIES
        line = iota((total, slots), 0) & (REPLIES - 1)
        shift = jnp.where(line >> 1 == 1, n_sub - 1, line >> 2)
        source = ((iota((total, slots), 0) // REPLIES + shift) & (n_sub - 1)) + (line & 1) * n_sub
        expand = ones_where((source == iota((total, slots), 1)) & (line < 3 * CAPACITY))
        solved = solved.astype(BF16)
        wide = dot(expand, solved)
        given = given_ref[...]
        own = ones_where(line_of((lines, slots), 0) == iota((lines, slots), 1))
        line = iota((lines, cases), 0) & (LINES - 1)
        terms = jnp.where(line < CAPACITY, given * dot(own, solved), 0.0)
        high, low = in_two(near_ref[...] + jnp.sum(terms, axis=0, keepdims=True))
        line = iota((total, cases), 0) & (REPLIES - 1)
        wide = jnp.where(line == 3 * CAPACITY, high.astype(F32), wide)
        out_ref[...] = jnp.where(line == 3 * CAPACITY + 1, low.astype(F32), wide).astype(BF16)

    def join(
        table_ref, in_ref, local_ref, before_ref, next_ref, turned_ref, own_ref, coupling_ref, residual_ref, norm_ref,
        jump_ref, out_ref, behind_ref, ahead_ref,
    ):
        replies = in_ref[...]
        total = n_sub * REPLIES
        line = iota((total, cases), 0) & (REPLIES - 1)
        curvature = jnp.sum(jnp.where(line >= 3 * CAPACITY, replies.astype(F32), 0.0), axis=0, keepdims=True)
        packed = half * width
        codes_at = packed + packed // cases * prims
        codes = [own_ref[packed // cases * prims :], before_ref[codes_at:], next_ref[codes_at:]]
        values = []
        for k, code in enumerate(codes):
            column = jnp.transpose(code)[:, :1] + float(k * CAPACITY)
            chosen = ones_where(iota((cases, total), 1).astype(F32) == column)
            values.append(dot(chosen, replies).astype(BF16))
        wide_eye = ones_where(iota((prims, cases), 0) == iota((prims, cases), 1))
        for side_ref, value, ref in ((before_ref, values[1], behind_ref), (next_ref, values[2], ahead_ref)):
            there = [side_ref[packed + k * prims : packed + (k + 1) * prims] for k in range(packed // cases)]
            turned = dot_t(jnp.concatenate(there, axis=1).astype(BF16), wide_eye).astype(BF16)
            ref[...] = side_ref[:packed] + dot(turned, value)
        image = local_ref[...] + dot(turned_ref[...], values[0])
        for e in range(edges):
            place = pl.ds(pl.multiple_of(table_ref[1, e] * width, width), width)
            facing = jnp.where(table_ref[0, e] == 1, ahead_ref[place, :], behind_ref[place, :])
            jump_ref[edge(e), :] = image[edge(e), :] - facing
        pair = jnp.concatenate(in_two(2.0 * residual_ref[...]) + in_two(2.0 * jump_ref[...]), axis=1)
        rows_there = dot(coupling_ref[...], pair)
        old, new = joined(rows_there[:, : 2 * cases], 2), joined(rows_there[:, 2 * cases :], 2)
        line = iota((SIDES, cases), 0)
        tail = jnp.where(line == 0, curvature, jnp.where(line == 1, norm_ref[...], 0.0))
        for c in range(n_coarse):
            out_ref[c, :prims] = old
            out_ref[c, prims : 2 * prims] = new
            out_ref[c, 2 * prims :] = tail

    def spread(in_ref, sides_ref, out_ref, scalars_ref):
        tail = in_ref[0, 2 * prims :]
        for c in range(1, n_coarse):
            tail = tail + in_ref[c, 2 * prims :]
        curvature, norm = tail[0:1], tail[1:2]
        alpha = norm / curvature
        line = iota((SIDES, cases), 0)
        scalars_ref[...] = jnp.where(line == 0, alpha, jnp.where(line == 1, curvature, norm))
        empty = jnp.zeros((ROOM - prims, cases), F32)
        parts = []
        for c in range(n_coarse):
            parts += [in_ref[c, :prims] - alpha * in_ref[c, prims : 2 * prims], empty]
        coupled = jnp.concatenate(parts, axis=0).astype(BF16)
        target = jnp.concatenate([sides_ref[n_coarse + k + 1 : n_coarse + k + 2, :] for k in range(n_coarse * ROOM // cases)], axis=1)
        total = n_coarse * slots
        marks = ones_where((iota((total, n_coarse * ROOM), 0) + 1).astype(F32) == target)
        out_ref[...] = dot(marks, coupled).astype(BF16)

    def owner_rows(table_ref, in_ref, sides_ref, weights_ref, rhs_ref):
        down = (iota((block, slots), 0) + 1).astype(F32)
        marks = jnp.concatenate([ones_where(down == sides_ref[c : c + 1]) for c in range(n_coarse)], axis=1)
        weights_ref[...] = dot(marks, in_ref[...])
        start = pl.multiple_of(table_ref[4, 0] * piece, piece)
        rhs = weights_ref[pl.ds(start, piece), :].astype(BF16)
        for k in range(chips):
            rhs_ref[k] = rhs

    def second(residual_ref, jump_ref, scalars_ref, schur_ref, remainder_ref, sums_ref):
        remainder = residual_ref[...] - scalars_ref[0:1] * jump_ref[...]
        remainder_ref[...] = remainder
        twice = 2.0 * remainder
        near = jnp.sum(twice * dot(schur_ref[...], twice.astype(BF16)), axis=0, keepdims=True)
        line = iota((SIDES, cases), 0)
        norm = jnp.sum(remainder * remainder, axis=0, keepdims=True)
        sums_ref[...] = jnp.where(line == 0, near, jnp.where(line == 1, norm, 0.0))

    field = ((order, cases), F32)
    row = ((1, cases), F32)
    gathered = ((chips, piece, cases), BF16)
    scalars_shape = ((SIDES, cases), F32)
    ints = jnp.concatenate(
        [here, neighbour_sub, neighbour_edge, primal_owner.reshape(1, prims), primal_offset], axis=1
    )
    start = load[0]
    from_before = lax.ppermute(start, "sub", to_next)
    from_next = lax.ppermute(start, "sub", to_before)
    packed = ((half * width // cases * prims + SIDES, cases), F32)
    slotted, turned, asked, codes, table, start, ahead, behind = run(
        set_up,
        [
            ((lines, order), BF16),
            ((order, cases), BF16),
            ((lines, slots), F32),
            scalars_shape,
            ((5, edges), I32),
            ((order, cases), BF16),
            packed,
            packed,
        ],
        ints, ints, coupling[0], start,
        specs=[SMEM, VMEM, VMEM, VMEM],
    )
    residual, outgoing = run(
        first, [field, ((lines, cases), F32)], table, start, from_before, from_next, slotted, asked
    )
    given = exchange(outgoing.reshape(n_sub, LINES, cases), "sub").reshape(lines, cases)
    outgoing, norm = run(owner_sums, [((n_coarse, piece + SIDES, cases), F32), row], given, codes)
    incoming = exchange(outgoing, "coarse")
    rhs, sides = run(coarse_sums, [gathered, ((2 * SIDES, cases), F32)], incoming)
    mine = exchange(rhs, "sub", same_core)
    theirs = lax.ppermute(mine, "sub", other_core)
    side = ((half * width + packed[0][0], cases), F32)
    local, near, to_ahead, to_behind = run(
        springs,
        [field, row, side, side],
        table, residual, schur[0], ahead, behind, mine,
        specs=[SMEM, VMEM, VMEM, VMEM, VMEM, HBM],
    )
    from_before = lax.ppermute(to_ahead, "sub", to_next)
    from_next = lax.ppermute(to_behind, "sub", to_before)
    (outgoing,) = run(
        answer,
        [((n_coarse, slots, cases), F32)],
        product(mine, theirs), sides, near,
        specs=[VMEM, VMEM, HBM],
    )
    incoming = exchange(outgoing, "coarse")
    (outgoing,) = run(reply, [((n_sub * REPLIES, cases), BF16)], incoming, given, near)
    replies = exchange(outgoing.reshape(n_sub, REPLIES, cases), "sub").reshape(n_sub * REPLIES, cases)
    image, outgoing = run(
        join,
        [field, ((n_coarse, 2 * prims + SIDES, cases), F32)],
        table, replies, local, from_before, from_next, turned, ahead, coupling[0], residual, norm,
        scratch=[pltpu.VMEM((half * width, cases), F32)] * 2,
    )
    incoming = exchange(outgoing, "coarse")
    outgoing, scalars = run(spread, [((n_coarse * slots, cases), BF16), scalars_shape], incoming, sides)
    incoming = exchange(outgoing.reshape(n_sub, n_coarse * CAPACITY, cases), "sub")
    incoming = incoming.transpose(1, 0, 2).reshape(n_coarse * slots, cases)
    weights, rhs = run(owner_rows, [((block, cases), F32), gathered], table, incoming, sides)
    mine = exchange(rhs, "sub", same_core)
    theirs = lax.ppermute(mine, "sub", other_core)
    remainder, sums = run(second, [field, scalars_shape], residual, image, scalars, schur[0])
    far = jnp.sum(weights * product(mine, theirs), axis=0)
    sums = jnp.stack([sums[0] + far, sums[1]])
    for groups in (columns, planes):
        wide = jnp.broadcast_to(sums[None], (len(groups[0]),) + sums.shape)
        sums = jnp.sum(exchange(wide, ("sub", "coarse"), groups), axis=0)
    alpha, curvature, norm = scalars[0], scalars[1], scalars[2]
    beta = sums[1] / norm
    step = sums[1] / (sums[0] - beta * beta * curvature)
    return ((alpha + step * beta) * residual + step * remainder)[None]


def solution(mesh):
    return jax.shard_map(
        body,
        mesh=mesh,
        in_specs=(
            P(("sub", "coarse"), None, None),
            P(("sub", "coarse"), None, None),
            P(("sub", "coarse"), None, None),
            P("coarse", "sub"),
            P(("sub", "coarse"), None),
            P(("sub", "coarse"), None),
            P(("sub", "coarse"), None, None),
            P(("sub", "coarse"), None),
        ),
        out_specs=P(("sub", "coarse"), None, None),
        check_vma=False,
    )
```

```python
import jax
import jax.numpy as jnp
from jax import lax
from jax.experimental import pallas as pl
from jax.experimental.pallas import tpu as pltpu
from jax.sharding import PartitionSpec as P

F32, BF16, I32 = jnp.float32, jnp.bfloat16, jnp.int32
CAPACITY = 2
LINES = 4
ROOM = 32
SIDES = 8
REPLIES = 8
NOBODY = -1000.0


def dot(a, b):
    return jnp.dot(a, b, preferred_element_type=F32)


def dot_t(a, b):
    return lax.dot_general(a, b, (((0,), (0,)), ((), ())), preferred_element_type=F32)


def iota(shape, dim):
    return lax.broadcasted_iota(I32, shape, dim)


def ones_where(mask):
    return jnp.where(mask, 1.0, 0.0).astype(BF16)


def in_two(value):
    high = value.astype(BF16)
    return high, (value - high.astype(F32)).astype(BF16)


def in_three(value):
    high = value.astype(BF16)
    rest = value - high.astype(F32)
    middle = rest.astype(BF16)
    return jnp.concatenate([high, middle, (rest - middle.astype(F32)).astype(BF16)], axis=1)


def joined(parts, count):
    wide = parts.shape[1] // count
    out = parts[:, :wide]
    for k in range(1, count):
        out = out + parts[:, k * wide : (k + 1) * wide]
    return out


HBM = pl.BlockSpec(memory_space=pltpu.HBM)
SMEM = pl.BlockSpec(memory_space=pltpu.SMEM)
VMEM = pl.BlockSpec(memory_space=pltpu.VMEM)


def run(kernel, outs, *args, specs=None, scratch=()):
    def spec(x):
        return SMEM if jnp.issubdtype(x.dtype, jnp.integer) and x.shape[1] <= 8 else VMEM

    return pl.pallas_call(
        kernel,
        out_shape=[jax.ShapeDtypeStruct(shape, dtype) for shape, dtype in outs],
        in_specs=specs or [spec(x) for x in args],
        out_specs=[SMEM if dtype == I32 else VMEM for _, dtype in outs],
        scratch_shapes=scratch,
        compiler_params=pltpu.CompilerParams(vmem_limit_bytes=32 * 1024 * 1024),
    )(*args)


def body(
    load,
    schur,
    coupling,
    coarse_inverse,
    neighbour_sub,
    neighbour_edge,
    primal_owner,
    primal_offset,
):
    _, order, cases = load.shape
    edges = neighbour_sub.shape[1]
    width = order // edges
    half = edges // 2
    rows, block = coarse_inverse.shape
    prims = primal_offset.shape[1]
    n_sub, n_coarse = lax.axis_size("sub"), lax.axis_size("coarse")
    piece = block // n_coarse
    slots = n_sub * CAPACITY
    lines = n_sub * LINES
    chips = n_sub // 2
    sub_index, coarse_index = lax.axis_index("sub"), lax.axis_index("coarse")
    here = jnp.stack([sub_index, coarse_index])[None].astype(I32)

    to_next = [(i, (i + 1) % n_sub) for i in range(n_sub)]
    to_before = [((i + 1) % n_sub, i) for i in range(n_sub)]
    other_core = [(i, i ^ 1) for i in range(n_sub)]
    same_core = [[2 * chip + core for chip in range(chips)] for core in range(2)]
    near_by = 2 * n_coarse
    devices = n_sub * n_coarse
    columns = [[start + k for k in range(near_by)] for start in range(0, devices, near_by)]
    planes = [[start + k for k in range(0, devices, near_by)] for start in range(near_by)]

    def exchange(blocks, axis, groups=None):
        return lax.all_to_all(blocks, axis, 0, 0, tiled=True, axis_index_groups=groups)

    def edge(e):
        return slice(e * width, (e + 1) * width)

    def set_up(
        ints_ref, row_ref, coupling_ref, load_ref,
        slotted_ref, turned_ref, asked_ref, codes_ref, table_ref, here_ref, ahead_ref, behind_ref,
    ):
        here_ref[...] = load_ref[...]
        sub_at, coarse_at = ints_ref[0, 0], ints_ref[0, 1]
        named_sub = [ints_ref[0, 2 + e] for e in range(edges)]
        named_edge = [ints_ref[0, 2 + edges + e] for e in range(edges)]
        owner_row = row_ref[:, 2 + 2 * edges : 2 + 2 * edges + prims]
        offset_row = row_ref[:, 2 + 2 * edges + prims :]
        faces = []
        for e in range(edges):
            side = lax.rem(lax.div(named_sub[e], n_coarse) - sub_at + n_sub, n_sub) == 1
            faces.append(side.astype(I32))
        ahead = jnp.int32(0)
        for e in range(edges):
            place = jnp.int32(0)
            for other in range(edges):
                if other != e:
                    lower = (faces[other] == faces[e]) & (named_edge[other] < named_edge[e])
                    place = place + lower.astype(I32)
            table_ref[0, e] = faces[e]
            table_ref[1, e] = place
            table_ref[2, e] = faces[e] * ahead + (1 - faces[e]) * (e - ahead)
            table_ref[3, e] = named_edge[e]
            table_ref[4, e] = coarse_at
            ahead = ahead + faces[e]
        same = iota((prims, prims), 0) == iota((prims, prims), 1)
        owner_col = jnp.sum(jnp.where(same, owner_row, 0), axis=1, keepdims=True)
        before = (owner_col == owner_row) & (iota((prims, prims), 0) < iota((prims, prims), 1))
        second = jnp.sum(jnp.where(before, 1, 0), axis=0, keepdims=True)
        line = iota((lines, prims), 0)
        placed = ones_where(line == owner_row * LINES + second)
        lane = iota((lines, slots), 1)
        asked = jnp.zeros((lines, slots), I32)
        for k in range(CAPACITY):
            named = (line >> 2 == owner_row) & (second == k)
            offset = jnp.sum(jnp.where(named, offset_row + 1, 0), axis=1, keepdims=True)
            asked = jnp.where(lane == k * n_sub + sub_at, offset, asked)
        asked_ref[...] = jnp.where((iota((lines, slots), 0) & (LINES - 1)) == CAPACITY, asked, 0).astype(F32)
        target = owner_row * (n_coarse * CAPACITY) + second + CAPACITY * coarse_at + 1
        far_lane = iota((prims, n_coarse * ROOM), 1) == iota((prims, n_coarse * ROOM), 0) + ROOM * coarse_at
        target_col = jnp.sum(jnp.where(same, target, 0), axis=1, keepdims=True)
        codes = jnp.sum(jnp.where(far_lane, target_col, 0), axis=0, keepdims=True).astype(F32)
        codes_ref[...] = jnp.zeros((SIDES, cases), F32)
        for k in range(n_coarse * ROOM // cases):
            codes_ref[k + 1 : k + 2, :] = codes[:, k * cases : (k + 1) * cases]
        slotted_ref[...] = dot(placed, coupling_ref[...]).astype(BF16)
        wide_eye = iota((prims, cases), 0) == iota((prims, cases), 1)
        turned_ref[...] = dot_t(coupling_ref[...], ones_where(wide_eye)).astype(BF16)
        line_col = jnp.sum(jnp.where(same, owner_row * REPLIES + second, 0), axis=1, keepdims=True)
        line_row = jnp.sum(jnp.where(wide_eye, line_col, 0), axis=0, keepdims=True).astype(F32)
        line_row = jnp.where(iota((1, cases), 1) < prims, line_row, NOBODY)
        lane = iota((1, half * width), 1)
        for side, ref in ((1, ahead_ref), (0, behind_ref)):
            target = jnp.zeros((1, half * width), I32)
            for place in range(half):
                at = jnp.int32(0)
                for e in range(edges):
                    at = at + e * ((faces[e] == side) & (table_ref[2, e] == place)).astype(I32)
                target = jnp.where(lane // width == place, at * width + lane % width, target)
            chosen = ones_where(iota((order, half * width), 0) == target)
            columns_there = dot(coupling_ref[...], chosen)
            for k in range(half * width // cases):
                ref[k * prims : (k + 1) * prims] = columns_there[:, k * cases : (k + 1) * cases]
            ref[half * width // cases * prims :] = jnp.broadcast_to(line_row, (SIDES, cases))

    def first(table_ref, load_ref, before_ref, next_ref, slotted_ref, asked_ref, residual_ref, out_ref):
        for e in range(edges):
            start = pl.multiple_of(table_ref[3, e] * width, width)
            ahead = next_ref[pl.ds(start, width), :].astype(F32)
            behind = before_ref[pl.ds(start, width), :].astype(F32)
            facing = jnp.where(table_ref[0, e] == 1, ahead, behind)
            residual_ref[edge(e), :] = load_ref[edge(e), :].astype(F32) - facing
        twice = 2.0 * residual_ref[...]
        squares = jnp.sum(twice * twice, axis=0, keepdims=True) * 0.25
        line = iota((lines, cases), 0) & (LINES - 1)
        terms = dot(slotted_ref[...], twice.astype(BF16))
        out_ref[...] = terms + asked_ref[...] + jnp.where(line == LINES - 1, squares, 0.0)

    def springs(
        table_ref, residual_ref, schur_ref, ahead_in, behind_in, after_ref, local_ref, near_ref, ahead_ref, behind_ref
    ):
        twice = 2.0 * residual_ref[...]
        local_ref[...] = dot(schur_ref[...], twice.astype(BF16))
        near_ref[...] = jnp.sum(twice * local_ref[...], axis=0, keepdims=True)
        ahead_ref[half * width :] = ahead_in[...]
        behind_ref[half * width :] = behind_in[...]
        for e in range(edges):
            place = pl.ds(pl.multiple_of(table_ref[2, e] * width, width), width)

            @pl.when(table_ref[0, e] == 1)
            def _():
                ahead_ref[place, :] = local_ref[edge(e), :]

            @pl.when(table_ref[0, e] == 0)
            def _():
                behind_ref[place, :] = local_ref[edge(e), :]

    def line_of(shape, dim):
        return (iota(shape, dim) & (LINES - 1)) * n_sub + (iota(shape, dim) >> 2)

    def owner_sums(in_ref, codes_ref, out_ref, norm_ref):
        given = in_ref[...]
        line = iota((lines, cases), 0) & (LINES - 1)
        asked = jnp.sum(jnp.where(line == CAPACITY, given, 0.0), axis=0, keepdims=True)
        norm_ref[...] = jnp.sum(jnp.where(line == LINES - 1, given, 0.0), axis=0, keepdims=True)
        expand = ones_where(iota((slots, lines), 0) == line_of((slots, lines), 1))
        wide = dot(jnp.broadcast_to(asked, (SIDES, slots)).astype(BF16), expand)[:1]
        marks = ones_where((iota((block, lines), 0) + 1).astype(F32) == wide)
        partial = joined(dot(marks, in_three(given)), 3)
        sides = codes_ref[...] + jnp.where(iota((SIDES, cases), 0) == 0, asked, 0.0)
        for c in range(n_coarse):
            out_ref[c, :piece] = partial[c * piece : (c + 1) * piece]
            out_ref[c, piece:] = sides

    def coarse_sums(in_ref, rhs_ref, sides_ref):
        total = in_ref[0]
        for c in range(1, n_coarse):
            total = total + in_ref[c]
        rhs = total[:piece].astype(BF16)
        for k in range(chips):
            rhs_ref[k] = rhs
        for c in range(n_coarse):
            sides_ref[c : c + 1] = in_ref[c, piece : piece + 1]
        sides_ref[n_coarse:] = total[piece:]

    def product(mine, theirs):
        both = jnp.where(
            sub_index % 2 == 0, jnp.concatenate([mine, theirs], axis=1), jnp.concatenate([theirs, mine], axis=1)
        )
        return dot_t(coarse_inverse, both.reshape(rows, cases))

    def answer(share_ref, sides_ref, after_ref, out_ref):
        asked = jnp.transpose(sides_ref[:n_coarse])
        across = (iota((slots, block), 1) + 1).astype(F32)
        share = in_three(share_ref[...])
        for c in range(n_coarse):
            out_ref[c] = joined(dot(ones_where(across == asked[:, c : c + 1]), share), 3)

    def reply(in_ref, given_ref, near_ref, before_ref, next_ref, out_ref):
        solved = in_ref[0]
        for c in range(1, n_coarse):
            solved = solved + in_ref[c]
        total = n_sub * REPLIES
        line = iota((total, slots), 0) & (REPLIES - 1)
        shift = jnp.where(line >> 1 == 1, n_sub - 1, line >> 2)
        source = ((iota((total, slots), 0) // REPLIES + shift) & (n_sub - 1)) + (line & 1) * n_sub
        expand = ones_where((source == iota((total, slots), 1)) & (line < 3 * CAPACITY))
        solved = solved.astype(BF16)
        wide = dot(expand, solved)
        given = given_ref[...]
        own = ones_where(line_of((lines, slots), 0) == iota((lines, slots), 1))
        line = iota((lines, cases), 0) & (LINES - 1)
        terms = jnp.where(line < CAPACITY, given * dot(own, solved), 0.0)
        high, low = in_two(near_ref[...] + jnp.sum(terms, axis=0, keepdims=True))
        line = iota((total, cases), 0) & (REPLIES - 1)
        wide = jnp.where(line == 3 * CAPACITY, high.astype(F32), wide)
        out_ref[...] = jnp.where(line == 3 * CAPACITY + 1, low.astype(F32), wide).astype(BF16)

    def join(
        table_ref, in_ref, local_ref, before_ref, next_ref, turned_ref, own_ref, coupling_ref, residual_ref, norm_ref,
        jump_ref, out_ref, behind_ref, ahead_ref,
    ):
        replies = in_ref[...]
        total = n_sub * REPLIES
        line = iota((total, cases), 0) & (REPLIES - 1)
        curvature = jnp.sum(jnp.where(line >= 3 * CAPACITY, replies.astype(F32), 0.0), axis=0, keepdims=True)
        packed = half * width
        codes_at = packed + packed // cases * prims
        codes = [own_ref[packed // cases * prims :], before_ref[codes_at:], next_ref[codes_at:]]
        values = []
        for k, code in enumerate(codes):
            column = jnp.transpose(code)[:, :1] + float(k * CAPACITY)
            chosen = ones_where(iota((cases, total), 1).astype(F32) == column)
            values.append(dot(chosen, replies).astype(BF16))
        wide_eye = ones_where(iota((prims, cases), 0) == iota((prims, cases), 1))
        for side_ref, value, ref in ((before_ref, values[1], behind_ref), (next_ref, values[2], ahead_ref)):
            there = [side_ref[packed + k * prims : packed + (k + 1) * prims] for k in range(packed // cases)]
            turned = dot_t(jnp.concatenate(there, axis=1).astype(BF16), wide_eye).astype(BF16)
            ref[...] = side_ref[:packed] + dot(turned, value)
        image = local_ref[...] + dot(turned_ref[...], values[0])
        for e in range(edges):
            place = pl.ds(pl.multiple_of(table_ref[1, e] * width, width), width)
            facing = jnp.where(table_ref[0, e] == 1, ahead_ref[place, :], behind_ref[place, :])
            jump_ref[edge(e), :] = image[edge(e), :] - facing
        pair = jnp.concatenate(in_two(2.0 * residual_ref[...]) + in_two(2.0 * jump_ref[...]), axis=1)
        rows_there = dot(coupling_ref[...], pair)
        old, new = joined(rows_there[:, : 2 * cases], 2), joined(rows_there[:, 2 * cases :], 2)
        line = iota((SIDES, cases), 0)
        tail = jnp.where(line == 0, curvature, jnp.where(line == 1, norm_ref[...], 0.0))
        for c in range(n_coarse):
            out_ref[c, :prims] = old
            out_ref[c, prims : 2 * prims] = new
            out_ref[c, 2 * prims :] = tail

    def spread(in_ref, sides_ref, out_ref, scalars_ref):
        tail = in_ref[0, 2 * prims :]
        for c in range(1, n_coarse):
            tail = tail + in_ref[c, 2 * prims :]
        curvature, norm = tail[0:1], tail[1:2]
        alpha = norm / curvature
        line = iota((SIDES, cases), 0)
        scalars_ref[...] = jnp.where(line == 0, alpha, jnp.where(line == 1, curvature, norm))
        empty = jnp.zeros((ROOM - prims, cases), F32)
        parts = []
        for c in range(n_coarse):
            parts += [in_ref[c, :prims] - alpha * in_ref[c, prims : 2 * prims], empty]
        coupled = jnp.concatenate(parts, axis=0).astype(BF16)
        target = jnp.concatenate([sides_ref[n_coarse + k + 1 : n_coarse + k + 2, :] for k in range(n_coarse * ROOM // cases)], axis=1)
        total = n_coarse * slots
        marks = ones_where((iota((total, n_coarse * ROOM), 0) + 1).astype(F32) == target)
        out_ref[...] = dot(marks, coupled).astype(BF16)

    def owner_rows(table_ref, in_ref, sides_ref, weights_ref, rhs_ref):
        down = (iota((block, slots), 0) + 1).astype(F32)
        marks = jnp.concatenate([ones_where(down == sides_ref[c : c + 1]) for c in range(n_coarse)], axis=1)
        weights_ref[...] = dot(marks, in_ref[...])
        start = pl.multiple_of(table_ref[4, 0] * piece, piece)
        rhs = weights_ref[pl.ds(start, piece), :].astype(BF16)
        for k in range(chips):
            rhs_ref[k] = rhs

    def second(residual_ref, jump_ref, scalars_ref, schur_ref, remainder_ref, sums_ref):
        remainder = residual_ref[...] - scalars_ref[0:1] * jump_ref[...]
        remainder_ref[...] = remainder
        twice = 2.0 * remainder
        near = jnp.sum(twice * dot(schur_ref[...], twice.astype(BF16)), axis=0, keepdims=True)
        line = iota((SIDES, cases), 0)
        norm = jnp.sum(remainder * remainder, axis=0, keepdims=True)
        sums_ref[...] = jnp.where(line == 0, near, jnp.where(line == 1, norm, 0.0))

    field = ((order, cases), F32)
    row = ((1, cases), F32)
    gathered = ((chips, piece, cases), BF16)
    scalars_shape = ((SIDES, cases), F32)
    ints = jnp.concatenate(
        [here, neighbour_sub, neighbour_edge, primal_owner.reshape(1, prims), primal_offset], axis=1
    )
    start = load[0]
    from_before = lax.ppermute(start, "sub", to_next)
    from_next = lax.ppermute(start, "sub", to_before)
    packed = ((half * width // cases * prims + SIDES, cases), F32)
    slotted, turned, asked, codes, table, start, ahead, behind = run(
        set_up,
        [
            ((lines, order), BF16),
            ((order, cases), BF16),
            ((lines, slots), F32),
            scalars_shape,
            ((5, edges), I32),
            ((order, cases), BF16),
            packed,
            packed,
        ],
        ints, ints, coupling[0], start,
        specs=[SMEM, VMEM, VMEM, VMEM],
    )
    residual, outgoing = run(
        first, [field, ((lines, cases), F32)], table, start, from_before, from_next, slotted, asked
    )
    given = exchange(outgoing.reshape(n_sub, LINES, cases), "sub").reshape(lines, cases)
    outgoing, norm = run(owner_sums, [((n_coarse, piece + SIDES, cases), F32), row], given, codes)
    incoming = exchange(outgoing, "coarse")
    rhs, sides = run(coarse_sums, [gathered, ((2 * SIDES, cases), F32)], incoming)
    mine = exchange(rhs, "sub", same_core)
    theirs = lax.ppermute(mine, "sub", other_core)
    side = ((half * width + packed[0][0], cases), F32)
    local, near, to_ahead, to_behind = run(
        springs,
        [field, row, side, side],
        table, residual, schur[0], ahead, behind, mine,
        specs=[SMEM, VMEM, VMEM, VMEM, VMEM, HBM],
    )
    from_before = lax.ppermute(to_ahead, "sub", to_next)
    from_next = lax.ppermute(to_behind, "sub", to_before)
    (outgoing,) = run(
        answer,
        [((n_coarse, slots, cases), F32)],
        product(mine, theirs), sides, near,
        specs=[VMEM, VMEM, HBM],
    )
    incoming = exchange(outgoing, "coarse")
    (outgoing,) = run(
        reply,
        [((n_sub * REPLIES, cases), BF16)],
        incoming, given, near, from_before, from_next,
        specs=[VMEM, VMEM, VMEM, HBM, HBM],
    )
    replies = exchange(outgoing.reshape(n_sub, REPLIES, cases), "sub").reshape(n_sub * REPLIES, cases)
    image, outgoing = run(
        join,
        [field, ((n_coarse, 2 * prims + SIDES, cases), F32)],
        table, replies, local, from_before, from_next, turned, ahead, coupling[0], residual, norm,
        scratch=[pltpu.VMEM((half * width, cases), F32)] * 2,
    )
    incoming = exchange(outgoing, "coarse")
    outgoing, scalars = run(spread, [((n_coarse * slots, cases), BF16), scalars_shape], incoming, sides)
    incoming = exchange(outgoing.reshape(n_sub, n_coarse * CAPACITY, cases), "sub")
    incoming = incoming.transpose(1, 0, 2).reshape(n_coarse * slots, cases)
    weights, rhs = run(owner_rows, [((block, cases), F32), gathered], table, incoming, sides)
    mine = exchange(rhs, "sub", same_core)
    theirs = lax.ppermute(mine, "sub", other_core)
    remainder, sums = run(second, [field, scalars_shape], residual, image, scalars, schur[0])
    far = jnp.sum(weights * product(mine, theirs), axis=0)
    sums = jnp.stack([sums[0] + far, sums[1]])
    for groups in (columns, planes):
        wide = jnp.broadcast_to(sums[None], (len(groups[0]),) + sums.shape)
        sums = jnp.sum(exchange(wide, ("sub", "coarse"), groups), axis=0)
    alpha, curvature, norm = scalars[0], scalars[1], scalars[2]
    beta = sums[1] / norm
    step = sums[1] / (sums[0] - beta * beta * curvature)
    return ((alpha + step * beta) * residual + step * remainder)[None]


def solution(mesh):
    return jax.shard_map(
        body,
        mesh=mesh,
        in_specs=(
            P(("sub", "coarse"), None, None),
            P(("sub", "coarse"), None, None),
            P(("sub", "coarse"), None, None),
            P("coarse", "sub"),
            P(("sub", "coarse"), None),
            P(("sub", "coarse"), None),
            P(("sub", "coarse"), None, None),
            P(("sub", "coarse"), None),
        ),
        out_specs=P(("sub", "coarse"), None, None),
        check_vma=False,
    )
```

```python
import jax
import jax.numpy as jnp
from jax import lax
from jax.experimental import pallas as pl
from jax.experimental.pallas import tpu as pltpu
from jax.sharding import PartitionSpec as P

F32, BF16, I32 = jnp.float32, jnp.bfloat16, jnp.int32
CAPACITY = 2
LINES = 4
ROOM = 32
SIDES = 8
REPLIES = 8
NOBODY = -1000.0


def dot(a, b):
    return jnp.dot(a, b, preferred_element_type=F32)


def dot_t(a, b):
    return lax.dot_general(a, b, (((0,), (0,)), ((), ())), preferred_element_type=F32)


def iota(shape, dim):
    return lax.broadcasted_iota(I32, shape, dim)


def ones_where(mask):
    return jnp.where(mask, 1.0, 0.0).astype(BF16)


def in_two(value):
    high = value.astype(BF16)
    return high, (value - high.astype(F32)).astype(BF16)


def in_three(value):
    high = value.astype(BF16)
    rest = value - high.astype(F32)
    middle = rest.astype(BF16)
    return jnp.concatenate([high, middle, (rest - middle.astype(F32)).astype(BF16)], axis=1)


def joined(parts, count):
    wide = parts.shape[1] // count
    out = parts[:, :wide]
    for k in range(1, count):
        out = out + parts[:, k * wide : (k + 1) * wide]
    return out


HBM = pl.BlockSpec(memory_space=pltpu.HBM)
SMEM = pl.BlockSpec(memory_space=pltpu.SMEM)
VMEM = pl.BlockSpec(memory_space=pltpu.VMEM)


def run(kernel, outs, *args, specs=None, scratch=()):
    def spec(x):
        return SMEM if jnp.issubdtype(x.dtype, jnp.integer) and x.shape[1] <= 8 else VMEM

    return pl.pallas_call(
        kernel,
        out_shape=[jax.ShapeDtypeStruct(shape, dtype) for shape, dtype in outs],
        in_specs=specs or [spec(x) for x in args],
        out_specs=[SMEM if dtype == I32 else VMEM for _, dtype in outs],
        scratch_shapes=scratch,
        compiler_params=pltpu.CompilerParams(vmem_limit_bytes=32 * 1024 * 1024),
    )(*args)


def body(
    load,
    schur,
    coupling,
    coarse_inverse,
    neighbour_sub,
    neighbour_edge,
    primal_owner,
    primal_offset,
):
    _, order, cases = load.shape
    edges = neighbour_sub.shape[1]
    width = order // edges
    half = edges // 2
    rows, block = coarse_inverse.shape
    prims = primal_offset.shape[1]
    n_sub, n_coarse = lax.axis_size("sub"), lax.axis_size("coarse")
    piece = block // n_coarse
    slots = n_sub * CAPACITY
    lines = n_sub * LINES
    chips = n_sub // 2
    sub_index, coarse_index = lax.axis_index("sub"), lax.axis_index("coarse")
    here = jnp.stack([sub_index, coarse_index])[None].astype(I32)

    to_next = [(i, (i + 1) % n_sub) for i in range(n_sub)]
    to_before = [((i + 1) % n_sub, i) for i in range(n_sub)]
    other_core = [(i, i ^ 1) for i in range(n_sub)]
    same_core = [[2 * chip + core for chip in range(chips)] for core in range(2)]
    near_by = 2 * n_coarse
    devices = n_sub * n_coarse
    columns = [[start + k for k in range(near_by)] for start in range(0, devices, near_by)]
    planes = [[start + k for k in range(0, devices, near_by)] for start in range(near_by)]

    def exchange(blocks, axis, groups=None):
        return lax.all_to_all(blocks, axis, 0, 0, tiled=True, axis_index_groups=groups)

    def edge(e):
        return slice(e * width, (e + 1) * width)

    def set_up(
        ints_ref, row_ref, coupling_ref, load_ref,
        slotted_ref, asked_ref, codes_ref, table_ref, here_ref, ahead_ref, behind_ref,
    ):
        here_ref[...] = load_ref[...]
        sub_at, coarse_at = ints_ref[0, 0], ints_ref[0, 1]
        named_sub = [ints_ref[0, 2 + e] for e in range(edges)]
        named_edge = [ints_ref[0, 2 + edges + e] for e in range(edges)]
        owner_row = row_ref[:, 2 + 2 * edges : 2 + 2 * edges + prims]
        offset_row = row_ref[:, 2 + 2 * edges + prims :]
        faces = []
        for e in range(edges):
            side = lax.rem(lax.div(named_sub[e], n_coarse) - sub_at + n_sub, n_sub) == 1
            faces.append(side.astype(I32))
        ahead = jnp.int32(0)
        for e in range(edges):
            place = jnp.int32(0)
            for other in range(edges):
                if other != e:
                    lower = (faces[other] == faces[e]) & (named_edge[other] < named_edge[e])
                    place = place + lower.astype(I32)
            table_ref[0, e] = faces[e]
            table_ref[1, e] = place
            table_ref[2, e] = faces[e] * ahead + (1 - faces[e]) * (e - ahead)
            table_ref[3, e] = named_edge[e]
            table_ref[4, e] = coarse_at
            ahead = ahead + faces[e]
        same = iota((prims, prims), 0) == iota((prims, prims), 1)
        owner_col = jnp.sum(jnp.where(same, owner_row, 0), axis=1, keepdims=True)
        before = (owner_col == owner_row) & (iota((prims, prims), 0) < iota((prims, prims), 1))
        second = jnp.sum(jnp.where(before, 1, 0), axis=0, keepdims=True)
        line = iota((lines, prims), 0)
        placed = ones_where(line == owner_row * LINES + second)
        lane = iota((lines, slots), 1)
        asked = jnp.zeros((lines, slots), I32)
        for k in range(CAPACITY):
            named = (line >> 2 == owner_row) & (second == k)
            offset = jnp.sum(jnp.where(named, offset_row + 1, 0), axis=1, keepdims=True)
            asked = jnp.where(lane == k * n_sub + sub_at, offset, asked)
        asked_ref[...] = jnp.where((iota((lines, slots), 0) & (LINES - 1)) == CAPACITY, asked, 0).astype(F32)
        target = owner_row * (n_coarse * CAPACITY) + second + CAPACITY * coarse_at + 1
        far_lane = iota((prims, n_coarse * ROOM), 1) == iota((prims, n_coarse * ROOM), 0) + ROOM * coarse_at
        target_col = jnp.sum(jnp.where(same, target, 0), axis=1, keepdims=True)
        codes = jnp.sum(jnp.where(far_lane, target_col, 0), axis=0, keepdims=True).astype(F32)
        codes_ref[...] = jnp.zeros((SIDES, cases), F32)
        for k in range(n_coarse * ROOM // cases):
            codes_ref[k + 1 : k + 2, :] = codes[:, k * cases : (k + 1) * cases]
        slotted_ref[...] = dot(placed, coupling_ref[...]).astype(BF16)
        wide_eye = iota((prims, cases), 0) == iota((prims, cases), 1)
        line_col = jnp.sum(jnp.where(same, owner_row * REPLIES + second, 0), axis=1, keepdims=True)
        line_row = jnp.sum(jnp.where(wide_eye, line_col, 0), axis=0, keepdims=True).astype(F32)
        line_row = jnp.where(iota((1, cases), 1) < prims, line_row, NOBODY)
        lane = iota((1, half * width), 1)
        for side, ref in ((1, ahead_ref), (0, behind_ref)):
            target = jnp.zeros((1, half * width), I32)
            for place in range(half):
                at = jnp.int32(0)
                for e in range(edges):
                    at = at + e * ((faces[e] == side) & (table_ref[2, e] == place)).astype(I32)
                target = jnp.where(lane // width == place, at * width + lane % width, target)
            chosen = ones_where(iota((order, half * width), 0) == target)
            columns_there = dot(coupling_ref[...], chosen)
            for k in range(half * width // cases):
                ref[k * prims : (k + 1) * prims] = columns_there[:, k * cases : (k + 1) * cases]
            ref[half * width // cases * prims :] = jnp.broadcast_to(line_row, (SIDES, cases))

    def first(table_ref, load_ref, before_ref, next_ref, slotted_ref, asked_ref, residual_ref, out_ref):
        for e in range(edges):
            start = pl.multiple_of(table_ref[3, e] * width, width)
            ahead = next_ref[pl.ds(start, width), :].astype(F32)
            behind = before_ref[pl.ds(start, width), :].astype(F32)
            facing = jnp.where(table_ref[0, e] == 1, ahead, behind)
            residual_ref[edge(e), :] = load_ref[edge(e), :].astype(F32) - facing
        twice = 2.0 * residual_ref[...]
        squares = jnp.sum(twice * twice, axis=0, keepdims=True) * 0.25
        line = iota((lines, cases), 0) & (LINES - 1)
        terms = dot(slotted_ref[...], twice.astype(BF16))
        out_ref[...] = terms + asked_ref[...] + jnp.where(line == LINES - 1, squares, 0.0)

    def springs(
        table_ref, residual_ref, schur_ref, coupling_ref, ahead_in, behind_in, after_ref,
        near_ref, old_ref, ahead_ref, behind_ref, local_ref,
    ):
        jumps, rest = in_two(2.0 * residual_ref[...])
        local_ref[...] = dot(schur_ref[...], jumps)
        ahead_ref[half * width :] = ahead_in[...]
        behind_ref[half * width :] = behind_in[...]
        for e in range(edges):
            place = pl.ds(pl.multiple_of(table_ref[2, e] * width, width), width)

            @pl.when(table_ref[0, e] == 1)
            def _():
                ahead_ref[place, :] = local_ref[edge(e), :]

            @pl.when(table_ref[0, e] == 0)
            def _():
                behind_ref[place, :] = local_ref[edge(e), :]

        near_ref[...] = 2.0 * jnp.sum(residual_ref[...] * local_ref[...], axis=0, keepdims=True)
        old_ref[...] = joined(dot(coupling_ref[...], jnp.concatenate([jumps, rest], axis=1)), 2)

    def line_of(shape, dim):
        return (iota(shape, dim) & (LINES - 1)) * n_sub + (iota(shape, dim) >> 2)

    def owner_sums(in_ref, codes_ref, out_ref, norm_ref, kept_ref):
        given = in_ref[...]
        line = iota((lines, cases), 0) & (LINES - 1)
        asked = jnp.sum(jnp.where(line == CAPACITY, given, 0.0), axis=0, keepdims=True)
        norm_ref[...] = jnp.sum(jnp.where(line == LINES - 1, given, 0.0), axis=0, keepdims=True)
        expand = ones_where(iota((slots, lines), 0) == line_of((slots, lines), 1))
        wide = dot(jnp.broadcast_to(asked, (SIDES, slots)).astype(BF16), expand)[:1]
        marks = ones_where((iota((block, lines), 0) + 1).astype(F32) == wide)
        parts = in_three(given)
        partial = joined(dot(marks, parts), 3)
        kept_ref[...] = joined(dot(expand, parts), 3)
        sides = codes_ref[...] + jnp.where(iota((SIDES, cases), 0) == 0, asked, 0.0)
        for c in range(n_coarse):
            out_ref[c, :piece] = partial[c * piece : (c + 1) * piece]
            out_ref[c, piece:] = sides

    def coarse_sums(in_ref, rhs_ref, sides_ref):
        total = in_ref[0]
        for c in range(1, n_coarse):
            total = total + in_ref[c]
        rhs = total[:piece].astype(BF16)
        for k in range(chips):
            rhs_ref[k] = rhs
        for c in range(n_coarse):
            sides_ref[c : c + 1] = in_ref[c, piece : piece + 1]
        sides_ref[n_coarse:] = total[piece:]

    def product(mine, theirs):
        both = jnp.where(
            sub_index % 2 == 0, jnp.concatenate([mine, theirs], axis=1), jnp.concatenate([theirs, mine], axis=1)
        )
        return dot_t(coarse_inverse, both.reshape(rows, cases))

    def answer(share_ref, sides_ref, after_ref, out_ref):
        asked = jnp.transpose(sides_ref[:n_coarse])
        across = (iota((slots, block), 1) + 1).astype(F32)
        share = in_three(share_ref[...])
        for c in range(n_coarse):
            out_ref[c] = joined(dot(ones_where(across == asked[:, c : c + 1]), share), 3)

    def reply(in_ref, given_ref, near_ref, before_ref, next_ref, out_ref):
        solved = in_ref[0]
        for c in range(1, n_coarse):
            solved = solved + in_ref[c]
        total = n_sub * REPLIES
        line = iota((total, slots), 0) & (REPLIES - 1)
        shift = jnp.where(line >> 1 == 1, n_sub - 1, line >> 2)
        source = ((iota((total, slots), 0) // REPLIES + shift) & (n_sub - 1)) + (line & 1) * n_sub
        expand = ones_where((source == iota((total, slots), 1)) & (line < 3 * CAPACITY))
        solved = solved.astype(BF16)
        wide = dot(expand, solved)
        far = jnp.sum(given_ref[...] * solved.astype(F32), axis=0, keepdims=True)
        high, low = in_two(near_ref[...] + far)
        line = iota((total, cases), 0) & (REPLIES - 1)
        wide = jnp.where(line == 3 * CAPACITY, high.astype(F32), wide)
        out_ref[...] = jnp.where(line == 3 * CAPACITY + 1, low.astype(F32), wide).astype(BF16)

    def join(
        table_ref, in_ref, own_ahead_ref, own_behind_ref, before_ref, next_ref, coupling_ref, old_ref, norm_ref,
        jump_ref, out_ref, behind_ref, ahead_ref,
    ):
        replies = in_ref[...]
        total = n_sub * REPLIES
        line = iota((total, cases), 0) & (REPLIES - 1)
        curvature = jnp.sum(jnp.where(line >= 3 * CAPACITY, replies.astype(F32), 0.0), axis=0, keepdims=True)
        packed = half * width
        codes_at = packed + packed // cases * prims
        codes = [own_ahead_ref[codes_at:], before_ref[codes_at:], next_ref[codes_at:]]
        values = []
        for k, code in enumerate(codes):
            column = jnp.transpose(code)[:, :1] + float(k * CAPACITY)
            chosen = ones_where(iota((cases, total), 1).astype(F32) == column)
            values.append(dot(chosen, replies).astype(BF16))
        wide_eye = ones_where(iota((prims, cases), 0) == iota((prims, cases), 1))
        for side_ref, value, ref in ((before_ref, values[1], behind_ref), (next_ref, values[2], ahead_ref)):
            there = [side_ref[packed + k * prims : packed + (k + 1) * prims] for k in range(packed // cases)]
            turned = dot_t(jnp.concatenate(there, axis=1).astype(BF16), wide_eye).astype(BF16)
            ref[...] = side_ref[:packed] + dot(turned, value)
        back = dot(dot_t(coupling_ref[...], wide_eye).astype(BF16), values[0])
        for e in range(edges):
            place = pl.ds(pl.multiple_of(table_ref[1, e] * width, width), width)
            facing = jnp.where(table_ref[0, e] == 1, ahead_ref[place, :], behind_ref[place, :])
            place = pl.ds(pl.multiple_of(table_ref[2, e] * width, width), width)
            own = jnp.where(table_ref[0, e] == 1, own_ahead_ref[place, :], own_behind_ref[place, :])
            jump_ref[edge(e), :] = own + back[edge(e), :] - facing
        new = joined(dot(coupling_ref[...], jnp.concatenate(in_two(2.0 * jump_ref[...]), axis=1)), 2)
        line = iota((SIDES, cases), 0)
        tail = jnp.where(line == 0, curvature, jnp.where(line == 1, norm_ref[...], 0.0))
        for c in range(n_coarse):
            out_ref[c, :prims] = old_ref[...]
            out_ref[c, prims : 2 * prims] = new
            out_ref[c, 2 * prims :] = tail

    def spread(in_ref, sides_ref, out_ref, scalars_ref):
        tail = in_ref[0, 2 * prims :]
        for c in range(1, n_coarse):
            tail = tail + in_ref[c, 2 * prims :]
        curvature, norm = tail[0:1], tail[1:2]
        alpha = norm / curvature
        line = iota((SIDES, cases), 0)
        scalars_ref[...] = jnp.where(line == 0, alpha, jnp.where(line == 1, curvature, norm))
        empty = jnp.zeros((ROOM - prims, cases), F32)
        parts = []
        for c in range(n_coarse):
            parts += [in_ref[c, :prims] - alpha * in_ref[c, prims : 2 * prims], empty]
        coupled = jnp.concatenate(parts, axis=0).astype(BF16)
        target = jnp.concatenate([sides_ref[n_coarse + k + 1 : n_coarse + k + 2, :] for k in range(n_coarse * ROOM // cases)], axis=1)
        total = n_coarse * slots
        marks = ones_where((iota((total, n_coarse * ROOM), 0) + 1).astype(F32) == target)
        out_ref[...] = dot(marks, coupled).astype(BF16)

    def owner_rows(table_ref, in_ref, sides_ref, weights_ref, rhs_ref):
        down = (iota((block, slots), 0) + 1).astype(F32)
        marks = jnp.concatenate([ones_where(down == sides_ref[c : c + 1]) for c in range(n_coarse)], axis=1)
        weights_ref[...] = dot(marks, in_ref[...])
        start = pl.multiple_of(table_ref[4, 0] * piece, piece)
        rhs = weights_ref[pl.ds(start, piece), :].astype(BF16)
        for k in range(chips):
            rhs_ref[k] = rhs

    def second(residual_ref, jump_ref, scalars_ref, schur_ref, remainder_ref, sums_ref):
        remainder = residual_ref[...] - scalars_ref[0:1] * jump_ref[...]
        remainder_ref[...] = remainder
        twice = 2.0 * remainder
        near = jnp.sum(twice * dot(schur_ref[...], twice.astype(BF16)), axis=0, keepdims=True)
        line = iota((SIDES, cases), 0)
        norm = jnp.sum(remainder * remainder, axis=0, keepdims=True)
        sums_ref[...] = jnp.where(line == 0, near, jnp.where(line == 1, norm, 0.0))

    field = ((order, cases), F32)
    row = ((1, cases), F32)
    gathered = ((chips, piece, cases), BF16)
    scalars_shape = ((SIDES, cases), F32)
    ints = jnp.concatenate(
        [here, neighbour_sub, neighbour_edge, primal_owner.reshape(1, prims), primal_offset], axis=1
    )
    start = load[0]
    from_before = lax.ppermute(start, "sub", to_next)
    from_next = lax.ppermute(start, "sub", to_before)
    packed = ((half * width // cases * prims + SIDES, cases), F32)
    slotted, asked, codes, table, start, ahead, behind = run(
        set_up,
        [
            ((lines, order), BF16),
            ((lines, slots), F32),
            scalars_shape,
            ((5, edges), I32),
            ((order, cases), BF16),
            packed,
            packed,
        ],
        ints, ints, coupling[0], start,
        specs=[SMEM, VMEM, VMEM, VMEM],
    )
    residual, outgoing = run(
        first, [field, ((lines, cases), F32)], table, start, from_before, from_next, slotted, asked
    )
    given = exchange(outgoing.reshape(n_sub, LINES, cases), "sub").reshape(lines, cases)
    outgoing, norm, kept = run(
        owner_sums, [((n_coarse, piece + SIDES, cases), F32), row, ((slots, cases), F32)], given, codes
    )
    incoming = exchange(outgoing, "coarse")
    rhs, sides = run(coarse_sums, [gathered, ((2 * SIDES, cases), F32)], incoming)
    mine = exchange(rhs, "sub", same_core)
    theirs = lax.ppermute(mine, "sub", other_core)
    side = ((half * width + packed[0][0], cases), F32)
    near, old, to_ahead, to_behind = run(
        springs,
        [row, ((prims, cases), F32), side, side],
        table, residual, schur[0], coupling[0], ahead, behind, mine,
        specs=[SMEM, VMEM, VMEM, VMEM, VMEM, VMEM, HBM],
        scratch=[pltpu.VMEM((order, cases), F32)],
    )
    from_before = lax.ppermute(to_ahead, "sub", to_next)
    from_next = lax.ppermute(to_behind, "sub", to_before)
    (outgoing,) = run(
        answer,
        [((n_coarse, slots, cases), F32)],
        product(mine, theirs), sides, near,
        specs=[VMEM, VMEM, HBM],
    )
    incoming = exchange(outgoing, "coarse")
    (outgoing,) = run(
        reply,
        [((n_sub * REPLIES, cases), BF16)],
        incoming, kept, near, from_before, from_next,
        specs=[VMEM, VMEM, VMEM, HBM, HBM],
    )
    replies = exchange(outgoing.reshape(n_sub, REPLIES, cases), "sub").reshape(n_sub * REPLIES, cases)
    image, outgoing = run(
        join,
        [field, ((n_coarse, 2 * prims + SIDES, cases), F32)],
        table, replies, to_ahead, to_behind, from_before, from_next, coupling[0], old, norm,
        scratch=[pltpu.VMEM((half * width, cases), F32)] * 2,
    )
    incoming = exchange(outgoing, "coarse")
    outgoing, scalars = run(spread, [((n_coarse * slots, cases), BF16), scalars_shape], incoming, sides)
    incoming = exchange(outgoing.reshape(n_sub, n_coarse * CAPACITY, cases), "sub")
    incoming = incoming.transpose(1, 0, 2).reshape(n_coarse * slots, cases)
    weights, rhs = run(owner_rows, [((block, cases), F32), gathered], table, incoming, sides)
    mine = exchange(rhs, "sub", same_core)
    theirs = lax.ppermute(mine, "sub", other_core)
    remainder, sums = run(second, [field, scalars_shape], residual, image, scalars, schur[0])
    far = jnp.sum(weights * product(mine, theirs), axis=0)
    sums = jnp.stack([sums[0] + far, sums[1]])
    for groups in (columns, planes):
        wide = jnp.broadcast_to(sums[None], (len(groups[0]),) + sums.shape)
        sums = jnp.sum(exchange(wide, ("sub", "coarse"), groups), axis=0)
    alpha, curvature, norm = scalars[0], scalars[1], scalars[2]
    beta = sums[1] / norm
    step = sums[1] / (sums[0] - beta * beta * curvature)
    return ((alpha + step * beta) * residual + step * remainder)[None]


def solution(mesh):
    return jax.shard_map(
        body,
        mesh=mesh,
        in_specs=(
            P(("sub", "coarse"), None, None),
            P(("sub", "coarse"), None, None),
            P(("sub", "coarse"), None, None),
            P("coarse", "sub"),
            P(("sub", "coarse"), None),
            P(("sub", "coarse"), None),
            P(("sub", "coarse"), None, None),
            P(("sub", "coarse"), None),
        ),
        out_specs=P(("sub", "coarse"), None, None),
        check_vma=False,
    )
```

```python
import jax
import jax.numpy as jnp
from jax import lax
from jax.experimental import pallas as pl
from jax.experimental.pallas import tpu as pltpu
from jax.sharding import PartitionSpec as P

F32, BF16, I32 = jnp.float32, jnp.bfloat16, jnp.int32
CAPACITY = 2
LINES = 4
ROOM = 32
SIDES = 8
REPLIES = 8
NOBODY = -1000.0


def dot(a, b):
    return jnp.dot(a, b, preferred_element_type=F32)


def dot_t(a, b):
    return lax.dot_general(a, b, (((0,), (0,)), ((), ())), preferred_element_type=F32)


def iota(shape, dim):
    return lax.broadcasted_iota(I32, shape, dim)


def ones_where(mask):
    return jnp.where(mask, 1.0, 0.0).astype(BF16)


def in_two(value):
    high = value.astype(BF16)
    return high, (value - high.astype(F32)).astype(BF16)


def in_three(value):
    high = value.astype(BF16)
    rest = value - high.astype(F32)
    middle = rest.astype(BF16)
    return jnp.concatenate([high, middle, (rest - middle.astype(F32)).astype(BF16)], axis=1)


def joined(parts, count):
    wide = parts.shape[1] // count
    out = parts[:, :wide]
    for k in range(1, count):
        out = out + parts[:, k * wide : (k + 1) * wide]
    return out


HBM = pl.BlockSpec(memory_space=pltpu.HBM)
SMEM = pl.BlockSpec(memory_space=pltpu.SMEM)
VMEM = pl.BlockSpec(memory_space=pltpu.VMEM)


def run(kernel, outs, *args, specs=None, scratch=()):
    def spec(x):
        return SMEM if jnp.issubdtype(x.dtype, jnp.integer) and x.shape[1] <= 8 else VMEM

    return pl.pallas_call(
        kernel,
        out_shape=[jax.ShapeDtypeStruct(shape, dtype) for shape, dtype in outs],
        in_specs=specs or [spec(x) for x in args],
        out_specs=[SMEM if dtype == I32 else VMEM for _, dtype in outs],
        scratch_shapes=scratch,
        compiler_params=pltpu.CompilerParams(vmem_limit_bytes=32 * 1024 * 1024),
    )(*args)


def body(
    load,
    schur,
    coupling,
    coarse_inverse,
    neighbour_sub,
    neighbour_edge,
    primal_owner,
    primal_offset,
):
    _, order, cases = load.shape
    edges = neighbour_sub.shape[1]
    width = order // edges
    half = edges // 2
    rows, block = coarse_inverse.shape
    prims = primal_offset.shape[1]
    n_sub, n_coarse = lax.axis_size("sub"), lax.axis_size("coarse")
    piece = block // n_coarse
    slots = n_sub * CAPACITY
    lines = n_sub * LINES
    chips = n_sub // 2
    sub_index, coarse_index = lax.axis_index("sub"), lax.axis_index("coarse")
    here = jnp.stack([sub_index, coarse_index])[None].astype(I32)

    to_next = [(i, (i + 1) % n_sub) for i in range(n_sub)]
    to_before = [((i + 1) % n_sub, i) for i in range(n_sub)]
    other_core = [(i, i ^ 1) for i in range(n_sub)]
    same_core = [[2 * chip + core for chip in range(chips)] for core in range(2)]
    near_by = 2 * n_coarse
    devices = n_sub * n_coarse
    columns = [[start + k for k in range(near_by)] for start in range(0, devices, near_by)]
    planes = [[start + k for k in range(0, devices, near_by)] for start in range(near_by)]

    def exchange(blocks, axis, groups=None):
        return lax.all_to_all(blocks, axis, 0, 0, tiled=True, axis_index_groups=groups)

    def edge(e):
        return slice(e * width, (e + 1) * width)

    def set_up(
        ints_ref, row_ref, coupling_ref, load_ref,
        slotted_ref, asked_ref, codes_ref, table_ref, here_ref, ahead_ref, behind_ref,
    ):
        here_ref[...] = load_ref[...]
        sub_at, coarse_at = ints_ref[0, 0], ints_ref[0, 1]
        named_sub = [ints_ref[0, 2 + e] for e in range(edges)]
        named_edge = [ints_ref[0, 2 + edges + e] for e in range(edges)]
        owner_row = row_ref[:, 2 + 2 * edges : 2 + 2 * edges + prims]
        offset_row = row_ref[:, 2 + 2 * edges + prims :]
        faces = []
        for e in range(edges):
            side = lax.rem(lax.div(named_sub[e], n_coarse) - sub_at + n_sub, n_sub) == 1
            faces.append(side.astype(I32))
        ahead = jnp.int32(0)
        for e in range(edges):
            place = jnp.int32(0)
            for other in range(edges):
                if other != e:
                    lower = (faces[other] == faces[e]) & (named_edge[other] < named_edge[e])
                    place = place + lower.astype(I32)
            table_ref[0, e] = faces[e]
            table_ref[1, e] = place
            table_ref[2, e] = faces[e] * ahead + (1 - faces[e]) * (e - ahead)
            table_ref[3, e] = named_edge[e]
            table_ref[4, e] = coarse_at
            ahead = ahead + faces[e]
        same = iota((prims, prims), 0) == iota((prims, prims), 1)
        owner_col = jnp.sum(jnp.where(same, owner_row, 0), axis=1, keepdims=True)
        before = (owner_col == owner_row) & (iota((prims, prims), 0) < iota((prims, prims), 1))
        second = jnp.sum(jnp.where(before, 1, 0), axis=0, keepdims=True)
        line = iota((lines, prims), 0)
        placed = ones_where(line == owner_row * LINES + second)
        lane = iota((lines, slots), 1)
        asked = jnp.zeros((lines, slots), I32)
        for k in range(CAPACITY):
            named = (line >> 2 == owner_row) & (second == k)
            offset = jnp.sum(jnp.where(named, offset_row + 1, 0), axis=1, keepdims=True)
            asked = jnp.where(lane == k * n_sub + sub_at, offset, asked)
        asked_ref[...] = jnp.where((iota((lines, slots), 0) & (LINES - 1)) == CAPACITY, asked, 0).astype(F32)
        target = owner_row * (n_coarse * CAPACITY) + second + CAPACITY * coarse_at + 1
        far_lane = iota((prims, n_coarse * ROOM), 1) == iota((prims, n_coarse * ROOM), 0) + ROOM * coarse_at
        target_col = jnp.sum(jnp.where(same, target, 0), axis=1, keepdims=True)
        codes = jnp.sum(jnp.where(far_lane, target_col, 0), axis=0, keepdims=True).astype(F32)
        codes_ref[...] = jnp.zeros((SIDES, cases), F32)
        for k in range(n_coarse * ROOM // cases):
            codes_ref[k + 1 : k + 2, :] = codes[:, k * cases : (k + 1) * cases]
        slotted_ref[...] = dot(placed, coupling_ref[...]).astype(BF16)
        wide_eye = iota((prims, cases), 0) == iota((prims, cases), 1)
        line_col = jnp.sum(jnp.where(same, owner_row * REPLIES + second, 0), axis=1, keepdims=True)
        line_row = jnp.sum(jnp.where(wide_eye, line_col, 0), axis=0, keepdims=True).astype(F32)
        line_row = jnp.where(iota((1, cases), 1) < prims, line_row, NOBODY)
        lane = iota((1, half * width), 1)
        for side, ref in ((1, ahead_ref), (0, behind_ref)):
            target = jnp.zeros((1, half * width), I32)
            for place in range(half):
                at = jnp.int32(0)
                for e in range(edges):
                    at = at + e * ((faces[e] == side) & (table_ref[2, e] == place)).astype(I32)
                target = jnp.where(lane // width == place, at * width + lane % width, target)
            chosen = ones_where(iota((order, half * width), 0) == target)
            columns_there = dot(coupling_ref[...], chosen)
            for k in range(half * width // cases):
                ref[k * prims : (k + 1) * prims] = columns_there[:, k * cases : (k + 1) * cases]
            ref[half * width // cases * prims :] = jnp.broadcast_to(line_row, (SIDES, cases))

    def first(table_ref, load_ref, before_ref, next_ref, slotted_ref, asked_ref, residual_ref, out_ref):
        for e in range(edges):
            start = pl.multiple_of(table_ref[3, e] * width, width)
            ahead = next_ref[pl.ds(start, width), :].astype(F32)
            behind = before_ref[pl.ds(start, width), :].astype(F32)
            facing = jnp.where(table_ref[0, e] == 1, ahead, behind)
            residual_ref[edge(e), :] = load_ref[edge(e), :].astype(F32) - facing
        twice = 2.0 * residual_ref[...]
        squares = jnp.sum(twice * twice, axis=0, keepdims=True) * 0.25
        line = iota((lines, cases), 0) & (LINES - 1)
        terms = dot(slotted_ref[...], twice.astype(BF16))
        out_ref[...] = terms + asked_ref[...] + jnp.where(line == LINES - 1, squares, 0.0)

    def springs(
        table_ref, residual_ref, schur_ref, coupling_ref, ahead_in, behind_in, after_ref,
        near_ref, old_ref, ahead_ref, behind_ref, local_ref,
    ):
        jumps, rest = in_two(2.0 * residual_ref[...])
        local_ref[...] = dot(schur_ref[...], jumps)
        ahead_ref[half * width :] = ahead_in[...]
        behind_ref[half * width :] = behind_in[...]
        for e in range(edges):
            place = pl.ds(pl.multiple_of(table_ref[2, e] * width, width), width)

            @pl.when(table_ref[0, e] == 1)
            def _():
                ahead_ref[place, :] = local_ref[edge(e), :]

            @pl.when(table_ref[0, e] == 0)
            def _():
                behind_ref[place, :] = local_ref[edge(e), :]

        near_ref[...] = 2.0 * jnp.sum(residual_ref[...] * local_ref[...], axis=0, keepdims=True)
        old_ref[...] = joined(dot(coupling_ref[...], jnp.concatenate([jumps, rest], axis=1)), 2)

    def line_of(shape, dim):
        return (iota(shape, dim) & (LINES - 1)) * n_sub + (iota(shape, dim) >> 2)

    def owner_sums(in_ref, codes_ref, before_ref, next_ref, out_ref, norm_ref, kept_ref):
        given = in_ref[...]
        line = iota((lines, cases), 0) & (LINES - 1)
        asked = jnp.sum(jnp.where(line == CAPACITY, given, 0.0), axis=0, keepdims=True)
        norm_ref[...] = jnp.sum(jnp.where(line == LINES - 1, given, 0.0), axis=0, keepdims=True)
        expand = ones_where(iota((slots, lines), 0) == line_of((slots, lines), 1))
        wide = dot(jnp.broadcast_to(asked, (SIDES, slots)).astype(BF16), expand)[:1]
        marks = ones_where((iota((block, lines), 0) + 1).astype(F32) == wide)
        parts = in_three(given)
        partial = joined(dot(marks, parts), 3)
        kept_ref[...] = joined(dot(expand, parts), 3)
        sides = codes_ref[...] + jnp.where(iota((SIDES, cases), 0) == 0, asked, 0.0)
        for c in range(n_coarse):
            out_ref[c, :piece] = partial[c * piece : (c + 1) * piece]
            out_ref[c, piece:] = sides

    def coarse_sums(in_ref, rhs_ref, sides_ref):
        total = in_ref[0]
        for c in range(1, n_coarse):
            total = total + in_ref[c]
        rhs = total[:piece].astype(BF16)
        for k in range(chips):
            rhs_ref[k] = rhs
        for c in range(n_coarse):
            sides_ref[c : c + 1] = in_ref[c, piece : piece + 1]
        sides_ref[n_coarse:] = total[piece:]

    def product(mine, theirs):
        both = jnp.where(
            sub_index % 2 == 0, jnp.concatenate([mine, theirs], axis=1), jnp.concatenate([theirs, mine], axis=1)
        )
        return dot_t(coarse_inverse, both.reshape(rows, cases))

    def answer(share_ref, sides_ref, out_ref):
        asked = jnp.transpose(sides_ref[:n_coarse])
        across = (iota((slots, block), 1) + 1).astype(F32)
        share = in_three(share_ref[...])
        for c in range(n_coarse):
            out_ref[c] = joined(dot(ones_where(across == asked[:, c : c + 1]), share), 3)

    def reply(in_ref, given_ref, near_ref, out_ref):
        solved = in_ref[0]
        for c in range(1, n_coarse):
            solved = solved + in_ref[c]
        total = n_sub * REPLIES
        line = iota((total, slots), 0) & (REPLIES - 1)
        shift = jnp.where(line >> 1 == 1, n_sub - 1, line >> 2)
        source = ((iota((total, slots), 0) // REPLIES + shift) & (n_sub - 1)) + (line & 1) * n_sub
        expand = ones_where((source == iota((total, slots), 1)) & (line < 3 * CAPACITY))
        solved = solved.astype(BF16)
        wide = dot(expand, solved)
        far = jnp.sum(given_ref[...] * solved.astype(F32), axis=0, keepdims=True)
        high, low = in_two(near_ref[...] + far)
        line = iota((total, cases), 0) & (REPLIES - 1)
        wide = jnp.where(line == 3 * CAPACITY, high.astype(F32), wide)
        out_ref[...] = jnp.where(line == 3 * CAPACITY + 1, low.astype(F32), wide).astype(BF16)

    def join(
        table_ref, in_ref, own_ahead_ref, own_behind_ref, before_ref, next_ref, coupling_ref, old_ref, norm_ref,
        jump_ref, out_ref, behind_ref, ahead_ref,
    ):
        replies = in_ref[...]
        total = n_sub * REPLIES
        line = iota((total, cases), 0) & (REPLIES - 1)
        curvature = jnp.sum(jnp.where(line >= 3 * CAPACITY, replies.astype(F32), 0.0), axis=0, keepdims=True)
        packed = half * width
        codes_at = packed + packed // cases * prims
        codes = [own_ahead_ref[codes_at:], before_ref[codes_at:], next_ref[codes_at:]]
        values = []
        for k, code in enumerate(codes):
            column = jnp.transpose(code)[:, :1] + float(k * CAPACITY)
            chosen = ones_where(iota((cases, total), 1).astype(F32) == column)
            values.append(dot(chosen, replies).astype(BF16))
        wide_eye = ones_where(iota((prims, cases), 0) == iota((prims, cases), 1))
        for side_ref, value, ref in ((before_ref, values[1], behind_ref), (next_ref, values[2], ahead_ref)):
            there = [side_ref[packed + k * prims : packed + (k + 1) * prims] for k in range(packed // cases)]
            turned = dot_t(jnp.concatenate(there, axis=1).astype(BF16), wide_eye).astype(BF16)
            ref[...] = side_ref[:packed] + dot(turned, value)
        back = dot(dot_t(coupling_ref[...], wide_eye).astype(BF16), values[0])
        for e in range(edges):
            place = pl.ds(pl.multiple_of(table_ref[1, e] * width, width), width)
            facing = jnp.where(table_ref[0, e] == 1, ahead_ref[place, :], behind_ref[place, :])
            place = pl.ds(pl.multiple_of(table_ref[2, e] * width, width), width)
            own = jnp.where(table_ref[0, e] == 1, own_ahead_ref[place, :], own_behind_ref[place, :])
            jump_ref[edge(e), :] = own + back[edge(e), :] - facing
        new = joined(dot(coupling_ref[...], jnp.concatenate(in_two(2.0 * jump_ref[...]), axis=1)), 2)
        line = iota((SIDES, cases), 0)
        tail = jnp.where(line == 0, curvature, jnp.where(line == 1, norm_ref[...], 0.0))
        for c in range(n_coarse):
            out_ref[c, :prims] = old_ref[...]
            out_ref[c, prims : 2 * prims] = new
            out_ref[c, 2 * prims :] = tail

    def spread(in_ref, sides_ref, out_ref, scalars_ref):
        tail = in_ref[0, 2 * prims :]
        for c in range(1, n_coarse):
            tail = tail + in_ref[c, 2 * prims :]
        curvature, norm = tail[0:1], tail[1:2]
        alpha = norm / curvature
        line = iota((SIDES, cases), 0)
        scalars_ref[...] = jnp.where(line == 0, alpha, jnp.where(line == 1, curvature, norm))
        empty = jnp.zeros((ROOM - prims, cases), F32)
        parts = []
        for c in range(n_coarse):
            parts += [in_ref[c, :prims] - alpha * in_ref[c, prims : 2 * prims], empty]
        coupled = jnp.concatenate(parts, axis=0).astype(BF16)
        target = jnp.concatenate([sides_ref[n_coarse + k + 1 : n_coarse + k + 2, :] for k in range(n_coarse * ROOM // cases)], axis=1)
        total = n_coarse * slots
        marks = ones_where((iota((total, n_coarse * ROOM), 0) + 1).astype(F32) == target)
        out_ref[...] = dot(marks, coupled).astype(BF16)

    def owner_rows(table_ref, in_ref, sides_ref, weights_ref, rhs_ref):
        down = (iota((block, slots), 0) + 1).astype(F32)
        marks = jnp.concatenate([ones_where(down == sides_ref[c : c + 1]) for c in range(n_coarse)], axis=1)
        weights_ref[...] = dot(marks, in_ref[...])
        start = pl.multiple_of(table_ref[4, 0] * piece, piece)
        rhs = weights_ref[pl.ds(start, piece), :].astype(BF16)
        for k in range(chips):
            rhs_ref[k] = rhs

    def second(residual_ref, jump_ref, scalars_ref, schur_ref, remainder_ref, sums_ref):
        remainder = residual_ref[...] - scalars_ref[0:1] * jump_ref[...]
        remainder_ref[...] = remainder
        twice = 2.0 * remainder
        near = jnp.sum(twice * dot(schur_ref[...], twice.astype(BF16)), axis=0, keepdims=True)
        line = iota((SIDES, cases), 0)
        norm = jnp.sum(remainder * remainder, axis=0, keepdims=True)
        sums_ref[...] = jnp.where(line == 0, near, jnp.where(line == 1, norm, 0.0))

    field = ((order, cases), F32)
    row = ((1, cases), F32)
    gathered = ((chips, piece, cases), BF16)
    scalars_shape = ((SIDES, cases), F32)
    ints = jnp.concatenate(
        [here, neighbour_sub, neighbour_edge, primal_owner.reshape(1, prims), primal_offset], axis=1
    )
    start = load[0]
    from_before = lax.ppermute(start, "sub", to_next)
    from_next = lax.ppermute(start, "sub", to_before)
    packed = ((half * width // cases * prims + SIDES, cases), F32)
    slotted, asked, codes, table, start, ahead, behind = run(
        set_up,
        [
            ((lines, order), BF16),
            ((lines, slots), F32),
            scalars_shape,
            ((5, edges), I32),
            ((order, cases), BF16),
            packed,
            packed,
        ],
        ints, ints, coupling[0], start,
        specs=[SMEM, VMEM, VMEM, VMEM],
    )
    residual, outgoing = run(
        first, [field, ((lines, cases), F32)], table, start, from_before, from_next, slotted, asked
    )
    side = ((half * width + packed[0][0], cases), F32)
    near, old, to_ahead, to_behind = run(
        springs,
        [row, ((prims, cases), F32), side, side],
        table, residual, schur[0], coupling[0], ahead, behind, outgoing,
        specs=[SMEM, VMEM, VMEM, VMEM, VMEM, VMEM, HBM],
        scratch=[pltpu.VMEM((order, cases), F32)],
    )
    from_before = lax.ppermute(to_ahead, "sub", to_next)
    from_next = lax.ppermute(to_behind, "sub", to_before)
    given = exchange(outgoing.reshape(n_sub, LINES, cases), "sub").reshape(lines, cases)
    outgoing, norm, kept = run(
        owner_sums,
        [((n_coarse, piece + SIDES, cases), F32), row, ((slots, cases), F32)],
        given, codes, from_before, from_next,
        specs=[VMEM, VMEM, HBM, HBM],
    )
    incoming = exchange(outgoing, "coarse")
    rhs, sides = run(coarse_sums, [gathered, ((2 * SIDES, cases), F32)], incoming)
    mine = exchange(rhs, "sub", same_core)
    theirs = lax.ppermute(mine, "sub", other_core)
    (outgoing,) = run(answer, [((n_coarse, slots, cases), F32)], product(mine, theirs), sides)
    incoming = exchange(outgoing, "coarse")
    (outgoing,) = run(reply, [((n_sub * REPLIES, cases), BF16)], incoming, kept, near)
    replies = exchange(outgoing.reshape(n_sub, REPLIES, cases), "sub").reshape(n_sub * REPLIES, cases)
    image, outgoing = run(
        join,
        [field, ((n_coarse, 2 * prims + SIDES, cases), F32)],
        table, replies, to_ahead, to_behind, from_before, from_next, coupling[0], old, norm,
        scratch=[pltpu.VMEM((half * width, cases), F32)] * 2,
    )
    incoming = exchange(outgoing, "coarse")
    outgoing, scalars = run(spread, [((n_coarse * slots, cases), BF16), scalars_shape], incoming, sides)
    incoming = exchange(outgoing.reshape(n_sub, n_coarse * CAPACITY, cases), "sub")
    incoming = incoming.transpose(1, 0, 2).reshape(n_coarse * slots, cases)
    weights, rhs = run(owner_rows, [((block, cases), F32), gathered], table, incoming, sides)
    mine = exchange(rhs, "sub", same_core)
    theirs = lax.ppermute(mine, "sub", other_core)
    remainder, sums = run(second, [field, scalars_shape], residual, image, scalars, schur[0])
    far = jnp.sum(weights * product(mine, theirs), axis=0)
    sums = jnp.stack([sums[0] + far, sums[1]])
    for groups in (columns, planes):
        wide = jnp.broadcast_to(sums[None], (len(groups[0]),) + sums.shape)
        sums = jnp.sum(exchange(wide, ("sub", "coarse"), groups), axis=0)
    alpha, curvature, norm = scalars[0], scalars[1], scalars[2]
    beta = sums[1] / norm
    step = sums[1] / (sums[0] - beta * beta * curvature)
    return ((alpha + step * beta) * residual + step * remainder)[None]


def solution(mesh):
    return jax.shard_map(
        body,
        mesh=mesh,
        in_specs=(
            P(("sub", "coarse"), None, None),
            P(("sub", "coarse"), None, None),
            P(("sub", "coarse"), None, None),
            P("coarse", "sub"),
            P(("sub", "coarse"), None),
            P(("sub", "coarse"), None),
            P(("sub", "coarse"), None, None),
            P(("sub", "coarse"), None),
        ),
        out_specs=P(("sub", "coarse"), None, None),
        check_vma=False,
    )
```

```python
import jax
import jax.numpy as jnp
from jax import lax
from jax.experimental import pallas as pl
from jax.experimental.pallas import tpu as pltpu
from jax.sharding import PartitionSpec as P

F32, BF16, I32 = jnp.float32, jnp.bfloat16, jnp.int32
CAPACITY = 2
LINES = 4
ROOM = 32
SIDES = 8
REPLIES = 8
NOBODY = -1000.0


def dot(a, b):
    return jnp.dot(a, b, preferred_element_type=F32)


def dot_t(a, b):
    return lax.dot_general(a, b, (((0,), (0,)), ((), ())), preferred_element_type=F32)


def iota(shape, dim):
    return lax.broadcasted_iota(I32, shape, dim)


def ones_where(mask):
    return jnp.where(mask, 1.0, 0.0).astype(BF16)


def in_two(value):
    high = value.astype(BF16)
    return high, (value - high.astype(F32)).astype(BF16)


def in_three(value):
    high = value.astype(BF16)
    rest = value - high.astype(F32)
    middle = rest.astype(BF16)
    return jnp.concatenate([high, middle, (rest - middle.astype(F32)).astype(BF16)], axis=1)


def joined(parts, count):
    wide = parts.shape[1] // count
    out = parts[:, :wide]
    for k in range(1, count):
        out = out + parts[:, k * wide : (k + 1) * wide]
    return out


HBM = pl.BlockSpec(memory_space=pltpu.HBM)
SMEM = pl.BlockSpec(memory_space=pltpu.SMEM)
VMEM = pl.BlockSpec(memory_space=pltpu.VMEM)


def run(kernel, outs, *args, specs=None, out_specs=None, scratch=()):
    def spec(x):
        return SMEM if jnp.issubdtype(x.dtype, jnp.integer) and x.shape[1] <= 8 else VMEM

    return pl.pallas_call(
        kernel,
        out_shape=[jax.ShapeDtypeStruct(shape, dtype) for shape, dtype in outs],
        in_specs=specs or [spec(x) for x in args],
        out_specs=out_specs or [SMEM if dtype == I32 else VMEM for _, dtype in outs],
        scratch_shapes=scratch,
        compiler_params=pltpu.CompilerParams(vmem_limit_bytes=32 * 1024 * 1024),
    )(*args)


def body(
    load,
    schur,
    coupling,
    coarse_inverse,
    neighbour_sub,
    neighbour_edge,
    primal_owner,
    primal_offset,
):
    _, order, cases = load.shape
    edges = neighbour_sub.shape[1]
    width = order // edges
    half = edges // 2
    rows, block = coarse_inverse.shape
    prims = primal_offset.shape[1]
    n_sub, n_coarse = lax.axis_size("sub"), lax.axis_size("coarse")
    piece = block // n_coarse
    slots = n_sub * CAPACITY
    lines = n_sub * LINES
    chips = n_sub // 2
    sub_index, coarse_index = lax.axis_index("sub"), lax.axis_index("coarse")
    here = jnp.stack([sub_index, coarse_index])[None].astype(I32)

    to_next = [(i, (i + 1) % n_sub) for i in range(n_sub)]
    to_before = [((i + 1) % n_sub, i) for i in range(n_sub)]
    other_core = [(i, i ^ 1) for i in range(n_sub)]
    same_core = [[2 * chip + core for chip in range(chips)] for core in range(2)]
    near_by = 2 * n_coarse
    devices = n_sub * n_coarse
    columns = [[start + k for k in range(near_by)] for start in range(0, devices, near_by)]
    planes = [[start + k for k in range(0, devices, near_by)] for start in range(near_by)]

    def exchange(blocks, axis, groups=None):
        return lax.all_to_all(blocks, axis, 0, 0, tiled=True, axis_index_groups=groups)

    def edge(e):
        return slice(e * width, (e + 1) * width)

    def set_up(
        ints_ref, row_ref, coupling_ref, load_ref,
        slotted_ref, asked_ref, codes_ref, table_ref, here_ref, ahead_ref, behind_ref,
    ):
        here_ref[...] = load_ref[...]
        sub_at, coarse_at = ints_ref[0, 0], ints_ref[0, 1]
        named_sub = [ints_ref[0, 2 + e] for e in range(edges)]
        named_edge = [ints_ref[0, 2 + edges + e] for e in range(edges)]
        owner_row = row_ref[:, 2 + 2 * edges : 2 + 2 * edges + prims]
        offset_row = row_ref[:, 2 + 2 * edges + prims :]
        faces = []
        for e in range(edges):
            side = lax.rem(lax.div(named_sub[e], n_coarse) - sub_at + n_sub, n_sub) == 1
            faces.append(side.astype(I32))
        ahead = jnp.int32(0)
        for e in range(edges):
            place = jnp.int32(0)
            for other in range(edges):
                if other != e:
                    lower = (faces[other] == faces[e]) & (named_edge[other] < named_edge[e])
                    place = place + lower.astype(I32)
            table_ref[0, e] = faces[e]
            table_ref[1, e] = place
            table_ref[2, e] = faces[e] * ahead + (1 - faces[e]) * (e - ahead)
            table_ref[3, e] = named_edge[e]
            table_ref[4, e] = coarse_at
            ahead = ahead + faces[e]
        same = iota((prims, prims), 0) == iota((prims, prims), 1)
        owner_col = jnp.sum(jnp.where(same, owner_row, 0), axis=1, keepdims=True)
        before = (owner_col == owner_row) & (iota((prims, prims), 0) < iota((prims, prims), 1))
        second = jnp.sum(jnp.where(before, 1, 0), axis=0, keepdims=True)
        line = iota((lines, prims), 0)
        placed = ones_where(line == owner_row * LINES + second)
        lane = iota((lines, slots), 1)
        asked = jnp.zeros((lines, slots), I32)
        for k in range(CAPACITY):
            named = (line >> 2 == owner_row) & (second == k)
            offset = jnp.sum(jnp.where(named, offset_row + 1, 0), axis=1, keepdims=True)
            asked = jnp.where(lane == k * n_sub + sub_at, offset, asked)
        asked_ref[...] = jnp.where((iota((lines, slots), 0) & (LINES - 1)) == CAPACITY, asked, 0).astype(F32)
        target = owner_row * (n_coarse * CAPACITY) + second + CAPACITY * coarse_at + 1
        far_lane = iota((prims, n_coarse * ROOM), 1) == iota((prims, n_coarse * ROOM), 0) + ROOM * coarse_at
        target_col = jnp.sum(jnp.where(same, target, 0), axis=1, keepdims=True)
        codes = jnp.sum(jnp.where(far_lane, target_col, 0), axis=0, keepdims=True).astype(F32)
        codes_ref[...] = jnp.zeros((SIDES, cases), F32)
        for k in range(n_coarse * ROOM // cases):
            codes_ref[k + 1 : k + 2, :] = codes[:, k * cases : (k + 1) * cases]
        slotted_ref[...] = dot(placed, coupling_ref[...]).astype(BF16)
        wide_eye = iota((prims, cases), 0) == iota((prims, cases), 1)
        line_col = jnp.sum(jnp.where(same, owner_row * REPLIES + second, 0), axis=1, keepdims=True)
        line_row = jnp.sum(jnp.where(wide_eye, line_col, 0), axis=0, keepdims=True).astype(F32)
        line_row = jnp.where(iota((1, cases), 1) < prims, line_row, NOBODY)
        lane = iota((1, half * width), 1)
        for side, ref in ((1, ahead_ref), (0, behind_ref)):
            target = jnp.zeros((1, half * width), I32)
            for place in range(half):
                at = jnp.int32(0)
                for e in range(edges):
                    at = at + e * ((faces[e] == side) & (table_ref[2, e] == place)).astype(I32)
                target = jnp.where(lane // width == place, at * width + lane % width, target)
            chosen = ones_where(iota((order, half * width), 0) == target)
            columns_there = dot(coupling_ref[...], chosen)
            for k in range(half * width // cases):
                ref[k * prims : (k + 1) * prims] = columns_there[:, k * cases : (k + 1) * cases]
            ref[half * width // cases * prims :] = jnp.broadcast_to(line_row, (SIDES, cases))

    def first(table_ref, load_ref, before_ref, next_ref, slotted_ref, asked_ref, residual_ref, out_ref):
        for e in range(edges):
            start = pl.multiple_of(table_ref[3, e] * width, width)
            ahead = next_ref[pl.ds(start, width), :].astype(F32)
            behind = before_ref[pl.ds(start, width), :].astype(F32)
            facing = jnp.where(table_ref[0, e] == 1, ahead, behind)
            residual_ref[edge(e), :] = load_ref[edge(e), :].astype(F32) - facing
        twice = 2.0 * residual_ref[...]
        squares = jnp.sum(twice * twice, axis=0, keepdims=True) * 0.25
        line = iota((lines, cases), 0) & (LINES - 1)
        terms = dot(slotted_ref[...], twice.astype(BF16))
        out_ref[...] = terms + asked_ref[...] + jnp.where(line == LINES - 1, squares, 0.0)

    def springs(
        table_ref, residual_ref, schur_ref, coupling_ref, ahead_in, behind_in, after_ref,
        near_ref, old_ref, ahead_ref, behind_ref, local_ref,
    ):
        jumps, rest = in_two(2.0 * residual_ref[...])
        local_ref[...] = dot(schur_ref[...], jumps)
        ahead_ref[half * width :] = ahead_in[...]
        behind_ref[half * width :] = behind_in[...]
        for e in range(edges):
            place = pl.ds(pl.multiple_of(table_ref[2, e] * width, width), width)

            @pl.when(table_ref[0, e] == 1)
            def _():
                ahead_ref[place, :] = local_ref[edge(e), :]

            @pl.when(table_ref[0, e] == 0)
            def _():
                behind_ref[place, :] = local_ref[edge(e), :]

        near_ref[...] = 2.0 * jnp.sum(residual_ref[...] * local_ref[...], axis=0, keepdims=True)
        old_ref[...] = joined(dot(coupling_ref[...], jnp.concatenate([jumps, rest], axis=1)), 2)

    def line_of(shape, dim):
        return (iota(shape, dim) & (LINES - 1)) * n_sub + (iota(shape, dim) >> 2)

    def owner_sums(in_ref, codes_ref, out_ref, norm_ref, kept_ref):
        given = in_ref[...]
        line = iota((lines, cases), 0) & (LINES - 1)
        asked = jnp.sum(jnp.where(line == CAPACITY, given, 0.0), axis=0, keepdims=True)
        norm_ref[...] = jnp.sum(jnp.where(line == LINES - 1, given, 0.0), axis=0, keepdims=True)
        expand = ones_where(iota((slots, lines), 0) == line_of((slots, lines), 1))
        wide = dot(jnp.broadcast_to(asked, (SIDES, slots)).astype(BF16), expand)[:1]
        marks = ones_where((iota((block, lines), 0) + 1).astype(F32) == wide)
        parts = in_three(given)
        partial = joined(dot(marks, parts), 3)
        kept_ref[...] = joined(dot(expand, parts), 3)
        sides = codes_ref[...] + jnp.where(iota((SIDES, cases), 0) == 0, asked, 0.0)
        for c in range(n_coarse):
            out_ref[c, :piece] = partial[c * piece : (c + 1) * piece]
            out_ref[c, piece:] = sides

    def coarse_sums(in_ref, rhs_ref, sides_ref):
        total = in_ref[0]
        for c in range(1, n_coarse):
            total = total + in_ref[c]
        rhs = total[:piece].astype(BF16)
        for k in range(chips):
            rhs_ref[k] = rhs
        for c in range(n_coarse):
            sides_ref[c : c + 1] = in_ref[c, piece : piece + 1]
        sides_ref[n_coarse:] = total[piece:]

    def product(mine, theirs):
        both = jnp.where(
            sub_index % 2 == 0, jnp.concatenate([mine, theirs], axis=1), jnp.concatenate([theirs, mine], axis=1)
        )
        return dot_t(coarse_inverse, both.reshape(rows, cases))

    def answer(share_ref, sides_ref, after_ref, out_ref, block_ref, sems):
        asked = jnp.transpose(sides_ref[:n_coarse])
        across = (iota((slots, block), 1) + 1).astype(F32)
        share = in_three(share_ref[...])
        moves = []
        for c in range(n_coarse):
            block_ref[c] = joined(dot(ones_where(across == asked[:, c : c + 1]), share), 3)
            moves.append(pltpu.make_async_copy(block_ref.at[c], out_ref.at[c], sems.at[c]))
            moves[c].start()
        for move in moves:
            move.wait()

    def reply(in_ref, given_ref, near_ref, before_ref, next_ref, out_ref):
        solved = in_ref[0]
        for c in range(1, n_coarse):
            solved = solved + in_ref[c]
        total = n_sub * REPLIES
        line = iota((total, slots), 0) & (REPLIES - 1)
        shift = jnp.where(line >> 1 == 1, n_sub - 1, line >> 2)
        source = ((iota((total, slots), 0) // REPLIES + shift) & (n_sub - 1)) + (line & 1) * n_sub
        expand = ones_where((source == iota((total, slots), 1)) & (line < 3 * CAPACITY))
        solved = solved.astype(BF16)
        wide = dot(expand, solved)
        far = jnp.sum(given_ref[...] * solved.astype(F32), axis=0, keepdims=True)
        high, low = in_two(near_ref[...] + far)
        line = iota((total, cases), 0) & (REPLIES - 1)
        wide = jnp.where(line == 3 * CAPACITY, high.astype(F32), wide)
        out_ref[...] = jnp.where(line == 3 * CAPACITY + 1, low.astype(F32), wide).astype(BF16)

    def join(
        table_ref, in_ref, own_ahead_ref, own_behind_ref, before_ref, next_ref, coupling_ref, old_ref, norm_ref,
        jump_ref, out_ref, behind_ref, ahead_ref,
    ):
        replies = in_ref[...]
        total = n_sub * REPLIES
        line = iota((total, cases), 0) & (REPLIES - 1)
        curvature = jnp.sum(jnp.where(line >= 3 * CAPACITY, replies.astype(F32), 0.0), axis=0, keepdims=True)
        packed = half * width
        codes_at = packed + packed // cases * prims
        line = iota((SIDES, cases), 0)
        codes = jnp.where(line == 0, own_ahead_ref[codes_at:], before_ref[codes_at:])
        codes = jnp.transpose(jnp.where(line == 2, next_ref[codes_at:], codes))
        column = jnp.concatenate([codes[:ROOM, k : k + 1] + float(k * CAPACITY) for k in range(3)], axis=0)
        chosen = ones_where(iota((3 * ROOM, total), 1).astype(F32) == column)
        values = dot(chosen, replies).astype(BF16)
        for k, side_ref, ref in ((1, before_ref, behind_ref), (2, next_ref, ahead_ref)):
            there = [side_ref[packed + n * prims : packed + (n + 1) * prims] for n in range(packed // cases)]
            there = jnp.concatenate(there, axis=1).astype(BF16)
            ref[...] = side_ref[:packed] + dot_t(there, values[k * ROOM : k * ROOM + prims])
        back = dot_t(coupling_ref[...], values[:prims])
        for e in range(edges):
            place = pl.ds(pl.multiple_of(table_ref[1, e] * width, width), width)
            facing = jnp.where(table_ref[0, e] == 1, ahead_ref[place, :], behind_ref[place, :])
            place = pl.ds(pl.multiple_of(table_ref[2, e] * width, width), width)
            own = jnp.where(table_ref[0, e] == 1, own_ahead_ref[place, :], own_behind_ref[place, :])
            jump_ref[edge(e), :] = own + back[edge(e), :] - facing
        new = joined(dot(coupling_ref[...], jnp.concatenate(in_two(2.0 * jump_ref[...]), axis=1)), 2)
        line = iota((SIDES, cases), 0)
        tail = jnp.where(line == 0, curvature, jnp.where(line == 1, norm_ref[...], 0.0))
        for c in range(n_coarse):
            out_ref[c, :prims] = old_ref[...]
            out_ref[c, prims : 2 * prims] = new
            out_ref[c, 2 * prims :] = tail

    def spread(in_ref, sides_ref, out_ref, scalars_ref):
        tail = in_ref[0, 2 * prims :]
        for c in range(1, n_coarse):
            tail = tail + in_ref[c, 2 * prims :]
        curvature, norm = tail[0:1], tail[1:2]
        alpha = norm / curvature
        line = iota((SIDES, cases), 0)
        scalars_ref[...] = jnp.where(line == 0, alpha, jnp.where(line == 1, curvature, norm))
        empty = jnp.zeros((ROOM - prims, cases), F32)
        parts = []
        for c in range(n_coarse):
            parts += [in_ref[c, :prims] - alpha * in_ref[c, prims : 2 * prims], empty]
        coupled = jnp.concatenate(parts, axis=0).astype(BF16)
        target = jnp.concatenate([sides_ref[n_coarse + k + 1 : n_coarse + k + 2, :] for k in range(n_coarse * ROOM // cases)], axis=1)
        total = n_coarse * slots
        marks = ones_where((iota((total, n_coarse * ROOM), 0) + 1).astype(F32) == target)
        out_ref[...] = dot(marks, coupled).astype(BF16)

    def owner_rows(table_ref, in_ref, sides_ref, weights_ref, rhs_ref):
        down = (iota((block, slots), 0) + 1).astype(F32)
        marks = jnp.concatenate([ones_where(down == sides_ref[c : c + 1]) for c in range(n_coarse)], axis=1)
        weights_ref[...] = dot(marks, in_ref[...])
        start = pl.multiple_of(table_ref[4, 0] * piece, piece)
        rhs = weights_ref[pl.ds(start, piece), :].astype(BF16)
        for k in range(chips):
            rhs_ref[k] = rhs

    def second(residual_ref, jump_ref, scalars_ref, schur_ref, remainder_ref, sums_ref):
        remainder = residual_ref[...] - scalars_ref[0:1] * jump_ref[...]
        remainder_ref[...] = remainder
        twice = 2.0 * remainder
        near = jnp.sum(twice * dot(schur_ref[...], twice.astype(BF16)), axis=0, keepdims=True)
        line = iota((SIDES, cases), 0)
        norm = jnp.sum(remainder * remainder, axis=0, keepdims=True)
        sums_ref[...] = jnp.where(line == 0, near, jnp.where(line == 1, norm, 0.0))

    field = ((order, cases), F32)
    row = ((1, cases), F32)
    gathered = ((chips, piece, cases), BF16)
    scalars_shape = ((SIDES, cases), F32)
    ints = jnp.concatenate(
        [here, neighbour_sub, neighbour_edge, primal_owner.reshape(1, prims), primal_offset], axis=1
    )
    start = load[0]
    from_before = lax.ppermute(start, "sub", to_next)
    from_next = lax.ppermute(start, "sub", to_before)
    packed = ((half * width // cases * prims + SIDES, cases), F32)
    slotted, asked, codes, table, start, ahead, behind = run(
        set_up,
        [
            ((lines, order), BF16),
            ((lines, slots), F32),
            scalars_shape,
            ((5, edges), I32),
            ((order, cases), BF16),
            packed,
            packed,
        ],
        ints, ints, coupling[0], start,
        specs=[SMEM, VMEM, VMEM, VMEM],
    )
    residual, outgoing = run(
        first, [field, ((lines, cases), F32)], table, start, from_before, from_next, slotted, asked
    )
    given = exchange(outgoing.reshape(n_sub, LINES, cases), "sub").reshape(lines, cases)
    outgoing, norm, kept = run(
        owner_sums, [((n_coarse, piece + SIDES, cases), F32), row, ((slots, cases), F32)], given, codes
    )
    incoming = exchange(outgoing, "coarse")
    rhs, sides = run(coarse_sums, [gathered, ((2 * SIDES, cases), F32)], incoming)
    mine = exchange(rhs, "sub", same_core)
    theirs = lax.ppermute(mine, "sub", other_core)
    side = ((half * width + packed[0][0], cases), F32)
    near, old, to_ahead, to_behind = run(
        springs,
        [row, ((prims, cases), F32), side, side],
        table, residual, schur[0], coupling[0], ahead, behind, mine,
        specs=[SMEM, VMEM, VMEM, VMEM, VMEM, VMEM, HBM],
        scratch=[pltpu.VMEM((order, cases), F32)],
    )
    from_before = lax.ppermute(to_ahead, "sub", to_next)
    from_next = lax.ppermute(to_behind, "sub", to_before)
    (outgoing,) = run(
        answer,
        [((n_coarse, slots, cases), F32)],
        product(mine, theirs), sides, near,
        specs=[VMEM, VMEM, HBM],
        out_specs=[HBM],
        scratch=[pltpu.VMEM((n_coarse, slots, cases), F32), pltpu.SemaphoreType.DMA((n_coarse,))],
    )
    incoming = exchange(outgoing, "coarse")
    (outgoing,) = run(
        reply,
        [((n_sub * REPLIES, cases), BF16)],
        incoming, kept, near, from_before, from_next,
        specs=[VMEM, VMEM, VMEM, HBM, HBM],
    )
    replies = exchange(outgoing.reshape(n_sub, REPLIES, cases), "sub").reshape(n_sub * REPLIES, cases)
    image, outgoing = run(
        join,
        [field, ((n_coarse, 2 * prims + SIDES, cases), F32)],
        table, replies, to_ahead, to_behind, from_before, from_next, coupling[0], old, norm,
        scratch=[pltpu.VMEM((half * width, cases), F32)] * 2,
    )
    incoming = exchange(outgoing, "coarse")
    outgoing, scalars = run(spread, [((n_coarse * slots, cases), BF16), scalars_shape], incoming, sides)
    incoming = exchange(outgoing.reshape(n_sub, n_coarse * CAPACITY, cases), "sub")
    incoming = incoming.transpose(1, 0, 2).reshape(n_coarse * slots, cases)
    weights, rhs = run(owner_rows, [((block, cases), F32), gathered], table, incoming, sides)
    mine = exchange(rhs, "sub", same_core)
    theirs = lax.ppermute(mine, "sub", other_core)
    remainder, sums = run(second, [field, scalars_shape], residual, image, scalars, schur[0])
    far = jnp.sum(weights * product(mine, theirs), axis=0)
    sums = jnp.stack([sums[0] + far, sums[1]])
    for groups in (columns, planes):
        wide = jnp.broadcast_to(sums[None], (len(groups[0]),) + sums.shape)
        sums = jnp.sum(exchange(wide, ("sub", "coarse"), groups), axis=0)
    alpha, curvature, norm = scalars[0], scalars[1], scalars[2]
    beta = sums[1] / norm
    step = sums[1] / (sums[0] - beta * beta * curvature)
    return ((alpha + step * beta) * residual + step * remainder)[None]


def solution(mesh):
    return jax.shard_map(
        body,
        mesh=mesh,
        in_specs=(
            P(("sub", "coarse"), None, None),
            P(("sub", "coarse"), None, None),
            P(("sub", "coarse"), None, None),
            P("coarse", "sub"),
            P(("sub", "coarse"), None),
            P(("sub", "coarse"), None),
            P(("sub", "coarse"), None, None),
            P(("sub", "coarse"), None),
        ),
        out_specs=P(("sub", "coarse"), None, None),
        check_vma=False,
    )
```

```python
import jax
import jax.numpy as jnp
from jax import lax
from jax.experimental import pallas as pl
from jax.experimental.pallas import tpu as pltpu
from jax.sharding import PartitionSpec as P

F32, BF16, I32 = jnp.float32, jnp.bfloat16, jnp.int32
CAPACITY = 2
LINES = 4
ROOM = 32
SIDES = 8
REPLIES = 8
NOBODY = -1000.0


def dot(a, b):
    return jnp.dot(a, b, preferred_element_type=F32)


def dot_t(a, b):
    return lax.dot_general(a, b, (((0,), (0,)), ((), ())), preferred_element_type=F32)


def iota(shape, dim):
    return lax.broadcasted_iota(I32, shape, dim)


def ones_where(mask):
    return jnp.where(mask, 1.0, 0.0).astype(BF16)


def in_two(value):
    high = value.astype(BF16)
    return high, (value - high.astype(F32)).astype(BF16)


def in_three(value):
    high = value.astype(BF16)
    rest = value - high.astype(F32)
    middle = rest.astype(BF16)
    return jnp.concatenate([high, middle, (rest - middle.astype(F32)).astype(BF16)], axis=1)


def joined(parts, count):
    wide = parts.shape[1] // count
    out = parts[:, :wide]
    for k in range(1, count):
        out = out + parts[:, k * wide : (k + 1) * wide]
    return out


HBM = pl.BlockSpec(memory_space=pltpu.HBM)
SMEM = pl.BlockSpec(memory_space=pltpu.SMEM)
VMEM = pl.BlockSpec(memory_space=pltpu.VMEM)


def run(kernel, outs, *args, specs=None, out_specs=None, scratch=()):
    def spec(x):
        return SMEM if jnp.issubdtype(x.dtype, jnp.integer) and x.shape[1] <= 8 else VMEM

    return pl.pallas_call(
        kernel,
        out_shape=[jax.ShapeDtypeStruct(shape, dtype) for shape, dtype in outs],
        in_specs=specs or [spec(x) for x in args],
        out_specs=out_specs or [SMEM if dtype == I32 else VMEM for _, dtype in outs],
        scratch_shapes=scratch,
        compiler_params=pltpu.CompilerParams(vmem_limit_bytes=32 * 1024 * 1024),
    )(*args)


def body(
    load,
    schur,
    coupling,
    coarse_inverse,
    neighbour_sub,
    neighbour_edge,
    primal_owner,
    primal_offset,
):
    _, order, cases = load.shape
    edges = neighbour_sub.shape[1]
    width = order // edges
    half = edges // 2
    rows, block = coarse_inverse.shape
    prims = primal_offset.shape[1]
    n_sub, n_coarse = lax.axis_size("sub"), lax.axis_size("coarse")
    piece = block // n_coarse
    slots = n_sub * CAPACITY
    lines = n_sub * LINES
    chips = n_sub // 2
    sub_index, coarse_index = lax.axis_index("sub"), lax.axis_index("coarse")
    here = jnp.stack([sub_index, coarse_index])[None].astype(I32)

    to_next = [(i, (i + 1) % n_sub) for i in range(n_sub)]
    to_before = [((i + 1) % n_sub, i) for i in range(n_sub)]
    other_core = [(i, i ^ 1) for i in range(n_sub)]
    same_core = [[2 * chip + core for chip in range(chips)] for core in range(2)]
    near_by = 2 * n_coarse
    devices = n_sub * n_coarse
    columns = [[start + k for k in range(near_by)] for start in range(0, devices, near_by)]
    planes = [[start + k for k in range(0, devices, near_by)] for start in range(near_by)]

    def exchange(blocks, axis, groups=None):
        return lax.all_to_all(blocks, axis, 0, 0, tiled=True, axis_index_groups=groups)

    def edge(e):
        return slice(e * width, (e + 1) * width)

    def set_up(
        ints_ref, row_ref, coupling_ref, load_ref,
        slotted_ref, asked_ref, codes_ref, table_ref, here_ref, ahead_ref, behind_ref,
    ):
        here_ref[...] = load_ref[...]
        sub_at, coarse_at = ints_ref[0, 0], ints_ref[0, 1]
        named_sub = [ints_ref[0, 2 + e] for e in range(edges)]
        named_edge = [ints_ref[0, 2 + edges + e] for e in range(edges)]
        owner_row = row_ref[:, 2 + 2 * edges : 2 + 2 * edges + prims]
        offset_row = row_ref[:, 2 + 2 * edges + prims :]
        faces = []
        for e in range(edges):
            side = lax.rem(lax.div(named_sub[e], n_coarse) - sub_at + n_sub, n_sub) == 1
            faces.append(side.astype(I32))
        ahead = jnp.int32(0)
        for e in range(edges):
            place = jnp.int32(0)
            for other in range(edges):
                if other != e:
                    lower = (faces[other] == faces[e]) & (named_edge[other] < named_edge[e])
                    place = place + lower.astype(I32)
            table_ref[0, e] = faces[e]
            table_ref[1, e] = lax.rem(place, half)
            table_ref[2, e] = lax.rem(faces[e] * ahead + (1 - faces[e]) * (e - ahead), half)
            table_ref[3, e] = named_edge[e]
            table_ref[4, e] = coarse_at
            ahead = ahead + faces[e]
        same = iota((prims, prims), 0) == iota((prims, prims), 1)
        owner_col = jnp.sum(jnp.where(same, owner_row, 0), axis=1, keepdims=True)
        before = (owner_col == owner_row) & (iota((prims, prims), 0) < iota((prims, prims), 1))
        second = jnp.sum(jnp.where(before, 1, 0), axis=0, keepdims=True)
        line = iota((lines, prims), 0)
        placed = ones_where(line == owner_row * LINES + second)
        lane = iota((lines, slots), 1)
        asked = jnp.zeros((lines, slots), I32)
        for k in range(CAPACITY):
            named = (line >> 2 == owner_row) & (second == k)
            offset = jnp.sum(jnp.where(named, offset_row + 1, 0), axis=1, keepdims=True)
            asked = jnp.where(lane == k * n_sub + sub_at, offset, asked)
        asked_ref[...] = jnp.where((iota((lines, slots), 0) & (LINES - 1)) == CAPACITY, asked, 0).astype(F32)
        target = owner_row * (n_coarse * CAPACITY) + second + CAPACITY * coarse_at + 1
        far_lane = iota((prims, n_coarse * ROOM), 1) == iota((prims, n_coarse * ROOM), 0) + ROOM * coarse_at
        target_col = jnp.sum(jnp.where(same, target, 0), axis=1, keepdims=True)
        codes = jnp.sum(jnp.where(far_lane, target_col, 0), axis=0, keepdims=True).astype(F32)
        codes_ref[...] = jnp.zeros((SIDES, cases), F32)
        for k in range(n_coarse * ROOM // cases):
            codes_ref[k + 1 : k + 2, :] = codes[:, k * cases : (k + 1) * cases]
        slotted_ref[...] = dot(placed, coupling_ref[...]).astype(BF16)
        wide_eye = iota((prims, cases), 0) == iota((prims, cases), 1)
        line_col = jnp.sum(jnp.where(same, owner_row * REPLIES + second, 0), axis=1, keepdims=True)
        line_row = jnp.sum(jnp.where(wide_eye, line_col, 0), axis=0, keepdims=True).astype(F32)
        line_row = jnp.where(iota((1, cases), 1) < prims, line_row, NOBODY)
        lane = iota((1, half * width), 1)
        for side, ref in ((1, ahead_ref), (0, behind_ref)):
            target = jnp.zeros((1, half * width), I32)
            for place in range(half):
                at = jnp.int32(0)
                for e in range(edges):
                    at = at + e * ((faces[e] == side) & (table_ref[2, e] == place)).astype(I32)
                target = jnp.where(lane // width == place, at * width + lane % width, target)
            chosen = ones_where(iota((order, half * width), 0) == target)
            columns_there = dot(coupling_ref[...], chosen)
            for k in range(half * width // cases):
                ref[k * prims : (k + 1) * prims] = columns_there[:, k * cases : (k + 1) * cases]
            ref[half * width // cases * prims :] = jnp.broadcast_to(line_row, (SIDES, cases))

    def first(table_ref, load_ref, before_ref, next_ref, slotted_ref, asked_ref, residual_ref, out_ref):
        for e in range(edges):
            start = pl.multiple_of(table_ref[3, e] * width, width)
            ahead = next_ref[pl.ds(start, width), :].astype(F32)
            behind = before_ref[pl.ds(start, width), :].astype(F32)
            facing = jnp.where(table_ref[0, e] == 1, ahead, behind)
            residual_ref[edge(e), :] = load_ref[edge(e), :].astype(F32) - facing
        twice = 2.0 * residual_ref[...]
        squares = jnp.sum(twice * twice, axis=0, keepdims=True) * 0.25
        line = iota((lines, cases), 0) & (LINES - 1)
        terms = dot(slotted_ref[...], twice.astype(BF16))
        out_ref[...] = terms + asked_ref[...] + jnp.where(line == LINES - 1, squares, 0.0)

    def springs(
        table_ref, residual_ref, schur_ref, coupling_ref, ahead_in, behind_in, after_ref,
        near_ref, old_ref, ahead_ref, behind_ref, local_ref,
    ):
        jumps, rest = in_two(2.0 * residual_ref[...])
        local_ref[...] = dot(schur_ref[...], jumps)
        ahead_ref[half * width :] = ahead_in[...]
        behind_ref[half * width :] = behind_in[...]
        for e in range(edges):
            place = pl.ds(pl.multiple_of(table_ref[2, e] * width, width), width)

            @pl.when(table_ref[0, e] == 1)
            def _():
                ahead_ref[place, :] = local_ref[edge(e), :]

            @pl.when(table_ref[0, e] == 0)
            def _():
                behind_ref[place, :] = local_ref[edge(e), :]

        near_ref[...] = 2.0 * jnp.sum(residual_ref[...] * local_ref[...], axis=0, keepdims=True)
        old_ref[...] = joined(dot(coupling_ref[...], jnp.concatenate([jumps, rest], axis=1)), 2)

    def line_of(shape, dim):
        return (iota(shape, dim) & (LINES - 1)) * n_sub + (iota(shape, dim) >> 2)

    def owner_sums(in_ref, codes_ref, out_ref, norm_ref, kept_ref):
        given = in_ref[...]
        line = iota((lines, cases), 0) & (LINES - 1)
        asked = jnp.sum(jnp.where(line == CAPACITY, given, 0.0), axis=0, keepdims=True)
        norm_ref[...] = jnp.sum(jnp.where(line == LINES - 1, given, 0.0), axis=0, keepdims=True)
        expand = ones_where(iota((slots, lines), 0) == line_of((slots, lines), 1))
        wide = dot(jnp.broadcast_to(asked, (SIDES, slots)).astype(BF16), expand)[:1]
        marks = ones_where((iota((block, lines), 0) + 1).astype(F32) == wide)
        parts = in_three(given)
        partial = joined(dot(marks, parts), 3)
        kept_ref[...] = joined(dot(expand, parts), 3)
        sides = codes_ref[...] + jnp.where(iota((SIDES, cases), 0) == 0, asked, 0.0)
        for c in range(n_coarse):
            out_ref[c, :piece] = partial[c * piece : (c + 1) * piece]
            out_ref[c, piece:] = sides

    def coarse_sums(in_ref, rhs_ref, sides_ref):
        total = in_ref[0]
        for c in range(1, n_coarse):
            total = total + in_ref[c]
        rhs = total[:piece].astype(BF16)
        for k in range(chips):
            rhs_ref[k] = rhs
        for c in range(n_coarse):
            sides_ref[c : c + 1] = in_ref[c, piece : piece + 1]
        sides_ref[n_coarse:] = total[piece:]

    def product(mine, theirs):
        both = jnp.where(
            sub_index % 2 == 0, jnp.concatenate([mine, theirs], axis=1), jnp.concatenate([theirs, mine], axis=1)
        )
        return dot_t(coarse_inverse, both.reshape(rows, cases))

    def answer(share_ref, sides_ref, after_ref, out_ref, block_ref, sems):
        asked = jnp.transpose(sides_ref[:n_coarse])
        across = (iota((slots, block), 1) + 1).astype(F32)
        share = in_three(share_ref[...])
        moves = []
        for c in range(n_coarse):
            block_ref[c] = joined(dot(ones_where(across == asked[:, c : c + 1]), share), 3)
            moves.append(pltpu.make_async_copy(block_ref.at[c], out_ref.at[c], sems.at[c]))
            moves[c].start()
        for move in moves:
            move.wait()

    def reply(in_ref, given_ref, near_ref, before_ref, next_ref, out_ref):
        solved = in_ref[0]
        for c in range(1, n_coarse):
            solved = solved + in_ref[c]
        total = n_sub * REPLIES
        line = iota((total, slots), 0) & (REPLIES - 1)
        shift = jnp.where(line >> 1 == 1, n_sub - 1, line >> 2)
        source = ((iota((total, slots), 0) // REPLIES + shift) & (n_sub - 1)) + (line & 1) * n_sub
        expand = ones_where((source == iota((total, slots), 1)) & (line < 3 * CAPACITY))
        solved = solved.astype(BF16)
        wide = dot(expand, solved)
        far = jnp.sum(given_ref[...] * solved.astype(F32), axis=0, keepdims=True)
        high, low = in_two(near_ref[...] + far)
        line = iota((total, cases), 0) & (REPLIES - 1)
        wide = jnp.where(line == 3 * CAPACITY, high.astype(F32), wide)
        out_ref[...] = jnp.where(line == 3 * CAPACITY + 1, low.astype(F32), wide).astype(BF16)

    def join(
        table_ref, in_ref, own_ahead_ref, own_behind_ref, before_ref, next_ref, coupling_ref, old_ref, norm_ref,
        jump_ref, out_ref, behind_ref, ahead_ref,
    ):
        replies = in_ref[...]
        total = n_sub * REPLIES
        line = iota((total, cases), 0) & (REPLIES - 1)
        curvature = jnp.sum(jnp.where(line >= 3 * CAPACITY, replies.astype(F32), 0.0), axis=0, keepdims=True)
        packed = half * width
        codes_at = packed + packed // cases * prims
        line = iota((SIDES, cases), 0)
        codes = jnp.where(line == 0, own_ahead_ref[codes_at:], before_ref[codes_at:])
        codes = jnp.transpose(jnp.where(line == 2, next_ref[codes_at:], codes))
        column = jnp.concatenate([codes[:ROOM, k : k + 1] + float(k * CAPACITY) for k in range(3)], axis=0)
        chosen = ones_where(iota((3 * ROOM, total), 1).astype(F32) == column)
        values = dot(chosen, replies).astype(BF16)
        for k, side_ref, ref in ((1, before_ref, behind_ref), (2, next_ref, ahead_ref)):
            there = [side_ref[packed + n * prims : packed + (n + 1) * prims] for n in range(packed // cases)]
            there = jnp.concatenate(there, axis=1).astype(BF16)
            ref[...] = side_ref[:packed] + dot_t(there, values[k * ROOM : k * ROOM + prims])
        back = dot_t(coupling_ref[...], values[:prims])
        for e in range(edges):
            place = pl.ds(pl.multiple_of(table_ref[1, e] * width, width), width)
            facing = jnp.where(table_ref[0, e] == 1, ahead_ref[place, :], behind_ref[place, :])
            place = pl.ds(pl.multiple_of(table_ref[2, e] * width, width), width)
            own = jnp.where(table_ref[0, e] == 1, own_ahead_ref[place, :], own_behind_ref[place, :])
            jump_ref[edge(e), :] = own + back[edge(e), :] - facing
        new = joined(dot(coupling_ref[...], jnp.concatenate(in_two(2.0 * jump_ref[...]), axis=1)), 2)
        line = iota((SIDES, cases), 0)
        tail = jnp.where(line == 0, curvature, jnp.where(line == 1, norm_ref[...], 0.0))
        for c in range(n_coarse):
            out_ref[c, :prims] = old_ref[...]
            out_ref[c, prims : 2 * prims] = new
            out_ref[c, 2 * prims :] = tail

    def spread(in_ref, sides_ref, out_ref, scalars_ref):
        tail = in_ref[0, 2 * prims :]
        for c in range(1, n_coarse):
            tail = tail + in_ref[c, 2 * prims :]
        curvature, norm = tail[0:1], tail[1:2]
        alpha = norm / curvature
        line = iota((SIDES, cases), 0)
        scalars_ref[...] = jnp.where(line == 0, alpha, jnp.where(line == 1, curvature, norm))
        empty = jnp.zeros((ROOM - prims, cases), F32)
        parts = []
        for c in range(n_coarse):
            parts += [in_ref[c, :prims] - alpha * in_ref[c, prims : 2 * prims], empty]
        coupled = jnp.concatenate(parts, axis=0).astype(BF16)
        target = jnp.concatenate([sides_ref[n_coarse + k + 1 : n_coarse + k + 2, :] for k in range(n_coarse * ROOM // cases)], axis=1)
        total = n_coarse * slots
        marks = ones_where((iota((total, n_coarse * ROOM), 0) + 1).astype(F32) == target)
        out_ref[...] = dot(marks, coupled).astype(BF16)

    def owner_rows(table_ref, in_ref, sides_ref, weights_ref, rhs_ref):
        down = (iota((block, slots), 0) + 1).astype(F32)
        marks = jnp.concatenate([ones_where(down == sides_ref[c : c + 1]) for c in range(n_coarse)], axis=1)
        weights_ref[...] = dot(marks, in_ref[...])
        start = pl.multiple_of(table_ref[4, 0] * piece, piece)
        rhs = weights_ref[pl.ds(start, piece), :].astype(BF16)
        for k in range(chips):
            rhs_ref[k] = rhs

    def second(residual_ref, jump_ref, scalars_ref, schur_ref, remainder_ref, sums_ref):
        remainder = residual_ref[...] - scalars_ref[0:1] * jump_ref[...]
        remainder_ref[...] = remainder
        twice = 2.0 * remainder
        near = jnp.sum(twice * dot(schur_ref[...], twice.astype(BF16)), axis=0, keepdims=True)
        line = iota((SIDES, cases), 0)
        norm = jnp.sum(remainder * remainder, axis=0, keepdims=True)
        sums_ref[...] = jnp.where(line == 0, near, jnp.where(line == 1, norm, 0.0))

    field = ((order, cases), F32)
    row = ((1, cases), F32)
    gathered = ((chips, piece, cases), BF16)
    scalars_shape = ((SIDES, cases), F32)
    ints = jnp.concatenate(
        [here, neighbour_sub, neighbour_edge, primal_owner.reshape(1, prims), primal_offset], axis=1
    )
    start = load[0]
    from_before = lax.ppermute(start, "sub", to_next)
    from_next = lax.ppermute(start, "sub", to_before)
    packed = ((half * width // cases * prims + SIDES, cases), F32)
    slotted, asked, codes, table, start, ahead, behind = run(
        set_up,
        [
            ((lines, order), BF16),
            ((lines, slots), F32),
            scalars_shape,
            ((5, edges), I32),
            ((order, cases), BF16),
            packed,
            packed,
        ],
        ints, ints, coupling[0], start,
        specs=[SMEM, VMEM, VMEM, VMEM],
    )
    residual, outgoing = run(
        first, [field, ((lines, cases), F32)], table, start, from_before, from_next, slotted, asked
    )
    given = exchange(outgoing.reshape(n_sub, LINES, cases), "sub").reshape(lines, cases)
    outgoing, norm, kept = run(
        owner_sums, [((n_coarse, piece + SIDES, cases), F32), row, ((slots, cases), F32)], given, codes
    )
    incoming = exchange(outgoing, "coarse")
    rhs, sides = run(coarse_sums, [gathered, ((2 * SIDES, cases), F32)], incoming)
    mine = exchange(rhs, "sub", same_core)
    theirs = lax.ppermute(mine, "sub", other_core)
    side = ((half * width + packed[0][0], cases), F32)
    near, old, to_ahead, to_behind = run(
        springs,
        [row, ((prims, cases), F32), side, side],
        table, residual, schur[0], coupling[0], ahead, behind, mine,
        specs=[SMEM, VMEM, VMEM, VMEM, VMEM, VMEM, HBM],
        scratch=[pltpu.VMEM((order, cases), F32)],
    )
    from_before = lax.ppermute(to_ahead, "sub", to_next)
    from_next = lax.ppermute(to_behind, "sub", to_before)
    (outgoing,) = run(
        answer,
        [((n_coarse, slots, cases), F32)],
        product(mine, theirs), sides, near,
        specs=[VMEM, VMEM, HBM],
        out_specs=[HBM],
        scratch=[pltpu.VMEM((n_coarse, slots, cases), F32), pltpu.SemaphoreType.DMA((n_coarse,))],
    )
    incoming = exchange(outgoing, "coarse")
    (outgoing,) = run(
        reply,
        [((n_sub * REPLIES, cases), BF16)],
        incoming, kept, near, from_before, from_next,
        specs=[VMEM, VMEM, VMEM, HBM, HBM],
    )
    replies = exchange(outgoing.reshape(n_sub, REPLIES, cases), "sub").reshape(n_sub * REPLIES, cases)
    image, outgoing = run(
        join,
        [field, ((n_coarse, 2 * prims + SIDES, cases), F32)],
        table, replies, to_ahead, to_behind, from_before, from_next, coupling[0], old, norm,
        scratch=[pltpu.VMEM((half * width, cases), F32)] * 2,
    )
    incoming = exchange(outgoing, "coarse")
    outgoing, scalars = run(spread, [((n_coarse * slots, cases), BF16), scalars_shape], incoming, sides)
    incoming = exchange(outgoing.reshape(n_sub, n_coarse * CAPACITY, cases), "sub")
    incoming = incoming.transpose(1, 0, 2).reshape(n_coarse * slots, cases)
    weights, rhs = run(owner_rows, [((block, cases), F32), gathered], table, incoming, sides)
    mine = exchange(rhs, "sub", same_core)
    theirs = lax.ppermute(mine, "sub", other_core)
    remainder, sums = run(second, [field, scalars_shape], residual, image, scalars, schur[0])
    far = jnp.sum(weights * product(mine, theirs), axis=0)
    sums = jnp.stack([sums[0] + far, sums[1]])
    for groups in (columns, planes):
        wide = jnp.broadcast_to(sums[None], (len(groups[0]),) + sums.shape)
        sums = jnp.sum(exchange(wide, ("sub", "coarse"), groups), axis=0)
    alpha, curvature, norm = scalars[0], scalars[1], scalars[2]
    beta = sums[1] / norm
    step = sums[1] / (sums[0] - beta * beta * curvature)
    return ((alpha + step * beta) * residual + step * remainder)[None]


def solution(mesh):
    return jax.shard_map(
        body,
        mesh=mesh,
        in_specs=(
            P(("sub", "coarse"), None, None),
            P(("sub", "coarse"), None, None),
            P(("sub", "coarse"), None, None),
            P("coarse", "sub"),
            P(("sub", "coarse"), None),
            P(("sub", "coarse"), None),
            P(("sub", "coarse"), None, None),
            P(("sub", "coarse"), None),
        ),
        out_specs=P(("sub", "coarse"), None, None),
        check_vma=False,
    )
```

```python
import jax
import jax.numpy as jnp
from jax import lax
from jax.experimental import pallas as pl
from jax.experimental.pallas import tpu as pltpu
from jax.sharding import PartitionSpec as P

F32, BF16, I32 = jnp.float32, jnp.bfloat16, jnp.int32
CAPACITY = 2
LINES = 4
ROOM = 32
SIDES = 8
REPLIES = 8
NOBODY = -1000.0


def dot(a, b):
    return jnp.dot(a, b, preferred_element_type=F32)


def dot_t(a, b):
    return lax.dot_general(a, b, (((0,), (0,)), ((), ())), preferred_element_type=F32)


def iota(shape, dim):
    return lax.broadcasted_iota(I32, shape, dim)


def ones_where(mask):
    return jnp.where(mask, 1.0, 0.0).astype(BF16)


def in_two(value):
    high = value.astype(BF16)
    return high, (value - high.astype(F32)).astype(BF16)


def in_three(value):
    high = value.astype(BF16)
    rest = value - high.astype(F32)
    middle = rest.astype(BF16)
    return jnp.concatenate([high, middle, (rest - middle.astype(F32)).astype(BF16)], axis=1)


def joined(parts, count):
    wide = parts.shape[1] // count
    out = parts[:, :wide]
    for k in range(1, count):
        out = out + parts[:, k * wide : (k + 1) * wide]
    return out


HBM = pl.BlockSpec(memory_space=pltpu.HBM)
SMEM = pl.BlockSpec(memory_space=pltpu.SMEM)
VMEM = pl.BlockSpec(memory_space=pltpu.VMEM)


def run(kernel, outs, *args, specs=None, out_specs=None, scratch=()):
    def spec(x):
        return SMEM if jnp.issubdtype(x.dtype, jnp.integer) and x.shape[1] <= 8 else VMEM

    return pl.pallas_call(
        kernel,
        out_shape=[jax.ShapeDtypeStruct(shape, dtype) for shape, dtype in outs],
        in_specs=specs or [spec(x) for x in args],
        out_specs=out_specs or [SMEM if dtype == I32 else VMEM for _, dtype in outs],
        scratch_shapes=scratch,
        compiler_params=pltpu.CompilerParams(vmem_limit_bytes=32 * 1024 * 1024),
    )(*args)


def body(
    load,
    schur,
    coupling,
    coarse_inverse,
    neighbour_sub,
    neighbour_edge,
    primal_owner,
    primal_offset,
):
    _, order, cases = load.shape
    edges = neighbour_sub.shape[1]
    width = order // edges
    half = edges // 2
    rows, block = coarse_inverse.shape
    prims = primal_offset.shape[1]
    n_sub, n_coarse = lax.axis_size("sub"), lax.axis_size("coarse")
    piece = block // n_coarse
    slots = n_sub * CAPACITY
    lines = n_sub * LINES
    chips = n_sub // 2
    sub_index, coarse_index = lax.axis_index("sub"), lax.axis_index("coarse")
    here = jnp.stack([sub_index, coarse_index])[None].astype(I32)

    to_next = [(i, (i + 1) % n_sub) for i in range(n_sub)]
    to_before = [((i + 1) % n_sub, i) for i in range(n_sub)]
    other_core = [(i, i ^ 1) for i in range(n_sub)]
    same_core = [[2 * chip + core for chip in range(chips)] for core in range(2)]
    near_by = 2 * n_coarse
    devices = n_sub * n_coarse
    columns = [[start + k for k in range(near_by)] for start in range(0, devices, near_by)]
    planes = [[start + k for k in range(0, devices, near_by)] for start in range(near_by)]

    def exchange(blocks, axis, groups=None):
        return lax.all_to_all(blocks, axis, 0, 0, tiled=True, axis_index_groups=groups)

    def edge(e):
        return slice(e * width, (e + 1) * width)

    def set_up(
        ints_ref, row_ref, coupling_ref, load_ref,
        slotted_ref, asked_ref, codes_ref, table_ref, here_ref, ahead_ref, behind_ref,
    ):
        here_ref[...] = load_ref[...]
        sub_at, coarse_at = ints_ref[0, 0], ints_ref[0, 1]
        named_sub = [ints_ref[0, 2 + e] for e in range(edges)]
        named_edge = [ints_ref[0, 2 + edges + e] for e in range(edges)]
        owner_row = row_ref[:, 2 + 2 * edges : 2 + 2 * edges + prims]
        offset_row = row_ref[:, 2 + 2 * edges + prims :]
        faces = []
        for e in range(edges):
            side = lax.rem(lax.div(named_sub[e], n_coarse) - sub_at + n_sub, n_sub) == 1
            faces.append(side.astype(I32))
        ahead = jnp.int32(0)
        for e in range(edges):
            place = jnp.int32(0)
            for other in range(edges):
                if other != e:
                    lower = (faces[other] == faces[e]) & (named_edge[other] < named_edge[e])
                    place = place + lower.astype(I32)
            table_ref[0, e] = faces[e]
            table_ref[1, e] = lax.rem(place, half)
            table_ref[2, e] = lax.rem(faces[e] * ahead + (1 - faces[e]) * (e - ahead), half)
            table_ref[3, e] = named_edge[e]
            table_ref[4, e] = coarse_at
            ahead = ahead + faces[e]
        same = iota((prims, prims), 0) == iota((prims, prims), 1)
        owner_col = jnp.sum(jnp.where(same, owner_row, 0), axis=1, keepdims=True)
        before = (owner_col == owner_row) & (iota((prims, prims), 0) < iota((prims, prims), 1))
        second = jnp.sum(jnp.where(before, 1, 0), axis=0, keepdims=True)
        line = iota((lines, prims), 0)
        placed = ones_where(line == owner_row * LINES + second)
        lane = iota((lines, slots), 1)
        asked = jnp.zeros((lines, slots), I32)
        for k in range(CAPACITY):
            named = (line >> 2 == owner_row) & (second == k)
            offset = jnp.sum(jnp.where(named, offset_row + 1, 0), axis=1, keepdims=True)
            asked = jnp.where(lane == k * n_sub + sub_at, offset, asked)
        asked_ref[...] = jnp.where((iota((lines, slots), 0) & (LINES - 1)) == CAPACITY, asked, 0).astype(F32)
        target = owner_row * (n_coarse * CAPACITY) + second + CAPACITY * coarse_at + 1
        far_lane = iota((prims, n_coarse * ROOM), 1) == iota((prims, n_coarse * ROOM), 0) + ROOM * coarse_at
        target_col = jnp.sum(jnp.where(same, target, 0), axis=1, keepdims=True)
        codes = jnp.sum(jnp.where(far_lane, target_col, 0), axis=0, keepdims=True).astype(F32)
        codes_ref[...] = jnp.zeros((SIDES, cases), F32)
        for k in range(n_coarse * ROOM // cases):
            codes_ref[k + 1 : k + 2, :] = codes[:, k * cases : (k + 1) * cases]
        slotted_ref[...] = dot(placed, coupling_ref[...]).astype(BF16)
        wide_eye = iota((prims, cases), 0) == iota((prims, cases), 1)
        line_col = jnp.sum(jnp.where(same, owner_row * REPLIES + second, 0), axis=1, keepdims=True)
        line_row = jnp.sum(jnp.where(wide_eye, line_col, 0), axis=0, keepdims=True).astype(F32)
        line_row = jnp.where(iota((1, cases), 1) < prims, line_row, NOBODY)
        lane = iota((1, half * width), 1)
        for side, ref in ((1, ahead_ref), (0, behind_ref)):
            target = jnp.zeros((1, half * width), I32)
            for place in range(half):
                at = jnp.int32(0)
                for e in range(edges):
                    at = at + e * ((faces[e] == side) & (table_ref[2, e] == place)).astype(I32)
                target = jnp.where(lane // width == place, at * width + lane % width, target)
            chosen = ones_where(iota((order, half * width), 0) == target)
            columns_there = dot(coupling_ref[...], chosen)
            for k in range(half * width // cases):
                ref[k * prims : (k + 1) * prims] = columns_there[:, k * cases : (k + 1) * cases]
            ref[half * width // cases * prims :] = jnp.broadcast_to(line_row, (SIDES, cases))

    def first(table_ref, load_ref, before_ref, next_ref, slotted_ref, asked_ref, residual_ref, out_ref):
        for e in range(edges):
            start = pl.multiple_of(table_ref[3, e] * width, width)
            ahead = next_ref[pl.ds(start, width), :].astype(F32)
            behind = before_ref[pl.ds(start, width), :].astype(F32)
            facing = jnp.where(table_ref[0, e] == 1, ahead, behind)
            residual_ref[edge(e), :] = load_ref[edge(e), :].astype(F32) - facing
        twice = 2.0 * residual_ref[...]
        squares = jnp.sum(twice * twice, axis=0, keepdims=True) * 0.25
        line = iota((lines, cases), 0) & (LINES - 1)
        terms = dot(slotted_ref[...], twice.astype(BF16))
        out_ref[...] = terms + asked_ref[...] + jnp.where(line == LINES - 1, squares, 0.0)

    def springs(
        table_ref, residual_ref, schur_ref, coupling_ref, ahead_in, behind_in, after_ref,
        near_ref, old_ref, ahead_ref, behind_ref, local_ref,
    ):
        jumps, rest = in_two(2.0 * residual_ref[...])
        local_ref[...] = dot(schur_ref[...], jumps)
        ahead_ref[half * width :] = ahead_in[...]
        behind_ref[half * width :] = behind_in[...]
        for e in range(edges):
            place = pl.ds(pl.multiple_of(table_ref[2, e] * width, width), width)

            @pl.when(table_ref[0, e] == 1)
            def _():
                ahead_ref[place, :] = local_ref[edge(e), :]

            @pl.when(table_ref[0, e] == 0)
            def _():
                behind_ref[place, :] = local_ref[edge(e), :]

        near_ref[...] = 2.0 * jnp.sum(residual_ref[...] * local_ref[...], axis=0, keepdims=True)
        old_ref[...] = joined(dot(coupling_ref[...], jnp.concatenate([jumps, rest], axis=1)), 2)

    def line_of(shape, dim):
        return (iota(shape, dim) & (LINES - 1)) * n_sub + (iota(shape, dim) >> 2)

    def owner_sums(in_ref, codes_ref, out_ref, norm_ref, kept_ref):
        given = in_ref[...]
        line = iota((lines, cases), 0) & (LINES - 1)
        asked = jnp.sum(jnp.where(line == CAPACITY, given, 0.0), axis=0, keepdims=True)
        norm_ref[...] = jnp.sum(jnp.where(line == LINES - 1, given, 0.0), axis=0, keepdims=True)
        expand = ones_where(iota((slots, lines), 0) == line_of((slots, lines), 1))
        wide = dot(jnp.broadcast_to(asked, (SIDES, slots)).astype(BF16), expand)[:1]
        marks = ones_where((iota((block, lines), 0) + 1).astype(F32) == wide)
        parts = in_three(given)
        partial = joined(dot(marks, parts), 3)
        kept_ref[...] = joined(dot(expand, parts), 3)
        sides = codes_ref[...] + jnp.where(iota((SIDES, cases), 0) == 0, asked, 0.0)
        for c in range(n_coarse):
            out_ref[c, :piece] = partial[c * piece : (c + 1) * piece]
            out_ref[c, piece:] = sides

    def coarse_sums(in_ref, rhs_ref, sides_ref):
        total = in_ref[0]
        for c in range(1, n_coarse):
            total = total + in_ref[c]
        rhs = total[:piece].astype(BF16)
        for k in range(chips):
            rhs_ref[k] = rhs
        for c in range(n_coarse):
            sides_ref[c : c + 1] = in_ref[c, piece : piece + 1]
        sides_ref[n_coarse:] = total[piece:]

    def product(mine, theirs):
        both = jnp.where(
            sub_index % 2 == 0, jnp.concatenate([mine, theirs], axis=1), jnp.concatenate([theirs, mine], axis=1)
        )
        return dot_t(coarse_inverse, both.reshape(rows, cases))

    def answer(share_ref, sides_ref, after_ref, out_ref, block_ref, sems):
        asked = jnp.transpose(sides_ref[:n_coarse])
        across = (iota((slots, block), 1) + 1).astype(F32)
        share = in_three(share_ref[...])
        moves = []
        for c in range(n_coarse):
            block_ref[c] = joined(dot(ones_where(across == asked[:, c : c + 1]), share), 3)
            moves.append(pltpu.make_async_copy(block_ref.at[c], out_ref.at[c], sems.at[c]))
            moves[c].start()
        for move in moves:
            move.wait()

    def reply(in_ref, given_ref, near_ref, before_ref, next_ref, out_ref):
        solved = in_ref[0]
        for c in range(1, n_coarse):
            solved = solved + in_ref[c]
        total = n_sub * REPLIES
        line = iota((total, slots), 0) & (REPLIES - 1)
        shift = jnp.where(line >> 1 == 1, n_sub - 1, line >> 2)
        source = ((iota((total, slots), 0) // REPLIES + shift) & (n_sub - 1)) + (line & 1) * n_sub
        expand = ones_where((source == iota((total, slots), 1)) & (line < 3 * CAPACITY))
        solved = solved.astype(BF16)
        wide = dot(expand, solved)
        far = jnp.sum(given_ref[...] * solved.astype(F32), axis=0, keepdims=True)
        high, low = in_two(near_ref[...] + far)
        line = iota((total, cases), 0) & (REPLIES - 1)
        wide = jnp.where(line == 3 * CAPACITY, high.astype(F32), wide)
        out_ref[...] = jnp.where(line == 3 * CAPACITY + 1, low.astype(F32), wide).astype(BF16)

    def join(
        table_ref, in_ref, own_ahead_ref, own_behind_ref, before_ref, next_ref, coupling_ref, old_ref, norm_ref,
        jump_ref, out_ref, behind_ref, ahead_ref,
    ):
        replies = in_ref[...]
        total = n_sub * REPLIES
        line = iota((total, cases), 0) & (REPLIES - 1)
        curvature = jnp.sum(jnp.where(line >= 3 * CAPACITY, replies.astype(F32), 0.0), axis=0, keepdims=True)
        packed = half * width
        codes_at = packed + packed // cases * prims
        line = iota((SIDES, cases), 0)
        codes = jnp.where(line == 0, own_ahead_ref[codes_at:], before_ref[codes_at:])
        codes = jnp.transpose(jnp.where(line == 2, next_ref[codes_at:], codes))
        column = jnp.concatenate([codes[:ROOM, k : k + 1] + float(k * CAPACITY) for k in range(3)], axis=0)
        chosen = ones_where(iota((3 * ROOM, total), 1).astype(F32) == column)
        values = dot(chosen, replies).astype(BF16)
        for k, side_ref, ref in ((1, before_ref, behind_ref), (2, next_ref, ahead_ref)):
            there = [side_ref[packed + n * prims : packed + (n + 1) * prims] for n in range(packed // cases)]
            there = jnp.concatenate(there, axis=1).astype(BF16)
            ref[...] = side_ref[:packed] + dot_t(there, values[k * ROOM : k * ROOM + prims])
        back = dot_t(coupling_ref[...], values[:prims])
        for e in range(edges):
            place = pl.ds(pl.multiple_of(table_ref[1, e] * width, width), width)
            facing = jnp.where(table_ref[0, e] == 1, ahead_ref[place, :], behind_ref[place, :])
            place = pl.ds(pl.multiple_of(table_ref[2, e] * width, width), width)
            own = jnp.where(table_ref[0, e] == 1, own_ahead_ref[place, :], own_behind_ref[place, :])
            jump_ref[edge(e), :] = own + back[edge(e), :] - facing
        new = joined(dot(coupling_ref[...], jnp.concatenate(in_two(2.0 * jump_ref[...]), axis=1)), 2)
        line = iota((SIDES, cases), 0)
        tail = jnp.where(line == 0, curvature, jnp.where(line == 1, norm_ref[...], 0.0))
        for c in range(n_coarse):
            out_ref[c, :prims] = old_ref[...]
            out_ref[c, prims : 2 * prims] = new
            out_ref[c, 2 * prims :] = tail

    def spread(in_ref, sides_ref, out_ref, scalars_ref):
        tail = in_ref[0, 2 * prims :]
        for c in range(1, n_coarse):
            tail = tail + in_ref[c, 2 * prims :]
        curvature, norm = tail[0:1], tail[1:2]
        alpha = norm / curvature
        line = iota((SIDES, cases), 0)
        scalars_ref[...] = jnp.where(line == 0, alpha, jnp.where(line == 1, curvature, norm))
        empty = jnp.zeros((ROOM - prims, cases), F32)
        parts = []
        for c in range(n_coarse):
            parts += [in_ref[c, :prims] - alpha * in_ref[c, prims : 2 * prims], empty]
        coupled = jnp.concatenate(parts, axis=0).astype(BF16)
        target = jnp.concatenate([sides_ref[n_coarse + k + 1 : n_coarse + k + 2, :] for k in range(n_coarse * ROOM // cases)], axis=1)
        total = n_coarse * slots
        marks = ones_where((iota((total, n_coarse * ROOM), 0) + 1).astype(F32) == target)
        out_ref[...] = dot(marks, coupled).astype(BF16)

    def owner_rows(table_ref, in_ref, sides_ref, weights_ref, rhs_ref):
        down = (iota((block, slots), 0) + 1).astype(F32)
        weights = jnp.zeros((block, cases), F32)
        for c in range(0, n_coarse, 2):
            marks = jnp.concatenate([ones_where(down == sides_ref[c + k : c + k + 1]) for k in range(2)], axis=1)
            weights = weights + dot(marks, in_ref[c * slots : (c + 2) * slots])
        weights_ref[...] = weights
        start = pl.multiple_of(table_ref[4, 0] * piece, piece)
        rhs = weights_ref[pl.ds(start, piece), :].astype(BF16)
        for k in range(chips):
            rhs_ref[k] = rhs

    def second(residual_ref, jump_ref, scalars_ref, schur_ref, remainder_ref, sums_ref):
        remainder = residual_ref[...] - scalars_ref[0:1] * jump_ref[...]
        remainder_ref[...] = remainder
        twice = 2.0 * remainder
        near = jnp.sum(twice * dot(schur_ref[...], twice.astype(BF16)), axis=0, keepdims=True)
        line = iota((SIDES, cases), 0)
        norm = jnp.sum(remainder * remainder, axis=0, keepdims=True)
        sums_ref[...] = jnp.where(line == 0, near, jnp.where(line == 1, norm, 0.0))

    field = ((order, cases), F32)
    row = ((1, cases), F32)
    gathered = ((chips, piece, cases), BF16)
    scalars_shape = ((SIDES, cases), F32)
    ints = jnp.concatenate(
        [here, neighbour_sub, neighbour_edge, primal_owner.reshape(1, prims), primal_offset], axis=1
    )
    start = load[0]
    from_before = lax.ppermute(start, "sub", to_next)
    from_next = lax.ppermute(start, "sub", to_before)
    packed = ((half * width // cases * prims + SIDES, cases), F32)
    slotted, asked, codes, table, start, ahead, behind = run(
        set_up,
        [
            ((lines, order), BF16),
            ((lines, slots), F32),
            scalars_shape,
            ((5, edges), I32),
            ((order, cases), BF16),
            packed,
            packed,
        ],
        ints, ints, coupling[0], start,
        specs=[SMEM, VMEM, VMEM, VMEM],
    )
    residual, outgoing = run(
        first, [field, ((lines, cases), F32)], table, start, from_before, from_next, slotted, asked
    )
    given = exchange(outgoing.reshape(n_sub, LINES, cases), "sub").reshape(lines, cases)
    outgoing, norm, kept = run(
        owner_sums, [((n_coarse, piece + SIDES, cases), F32), row, ((slots, cases), F32)], given, codes
    )
    incoming = exchange(outgoing, "coarse")
    rhs, sides = run(coarse_sums, [gathered, ((2 * SIDES, cases), F32)], incoming)
    mine = exchange(rhs, "sub", same_core)
    theirs = lax.ppermute(mine, "sub", other_core)
    side = ((half * width + packed[0][0], cases), F32)
    near, old, to_ahead, to_behind = run(
        springs,
        [row, ((prims, cases), F32), side, side],
        table, residual, schur[0], coupling[0], ahead, behind, mine,
        specs=[SMEM, VMEM, VMEM, VMEM, VMEM, VMEM, HBM],
        scratch=[pltpu.VMEM((order, cases), F32)],
    )
    from_before = lax.ppermute(to_ahead, "sub", to_next)
    from_next = lax.ppermute(to_behind, "sub", to_before)
    (outgoing,) = run(
        answer,
        [((n_coarse, slots, cases), F32)],
        product(mine, theirs), sides, near,
        specs=[VMEM, VMEM, HBM],
        out_specs=[HBM],
        scratch=[pltpu.VMEM((n_coarse, slots, cases), F32), pltpu.SemaphoreType.DMA((n_coarse,))],
    )
    incoming = exchange(outgoing, "coarse")
    (outgoing,) = run(
        reply,
        [((n_sub * REPLIES, cases), BF16)],
        incoming, kept, near, from_before, from_next,
        specs=[VMEM, VMEM, VMEM, HBM, HBM],
    )
    replies = exchange(outgoing.reshape(n_sub, REPLIES, cases), "sub").reshape(n_sub * REPLIES, cases)
    image, outgoing = run(
        join,
        [field, ((n_coarse, 2 * prims + SIDES, cases), F32)],
        table, replies, to_ahead, to_behind, from_before, from_next, coupling[0], old, norm,
        scratch=[pltpu.VMEM((half * width, cases), F32)] * 2,
    )
    incoming = exchange(outgoing, "coarse")
    outgoing, scalars = run(spread, [((n_coarse * slots, cases), BF16), scalars_shape], incoming, sides)
    incoming = exchange(outgoing.reshape(n_sub, n_coarse * CAPACITY, cases), "sub")
    incoming = incoming.transpose(1, 0, 2).reshape(n_coarse * slots, cases)
    weights, rhs = run(owner_rows, [((block, cases), F32), gathered], table, incoming, sides)
    mine = exchange(rhs, "sub", same_core)
    theirs = lax.ppermute(mine, "sub", other_core)
    remainder, sums = run(second, [field, scalars_shape], residual, image, scalars, schur[0])
    far = jnp.sum(weights * product(mine, theirs), axis=0)
    sums = jnp.stack([sums[0] + far, sums[1]])
    for groups in (columns, planes):
        wide = jnp.broadcast_to(sums[None], (len(groups[0]),) + sums.shape)
        sums = jnp.sum(exchange(wide, ("sub", "coarse"), groups), axis=0)
    alpha, curvature, norm = scalars[0], scalars[1], scalars[2]
    beta = sums[1] / norm
    step = sums[1] / (sums[0] - beta * beta * curvature)
    return ((alpha + step * beta) * residual + step * remainder)[None]


def solution(mesh):
    return jax.shard_map(
        body,
        mesh=mesh,
        in_specs=(
            P(("sub", "coarse"), None, None),
            P(("sub", "coarse"), None, None),
            P(("sub", "coarse"), None, None),
            P("coarse", "sub"),
            P(("sub", "coarse"), None),
            P(("sub", "coarse"), None),
            P(("sub", "coarse"), None, None),
            P(("sub", "coarse"), None),
        ),
        out_specs=P(("sub", "coarse"), None, None),
        check_vma=False,
    )
```
